32 devices in a mesh: dp: 8 (over z, y), expert: 4 (over x, core).
Axes of the slice: x: 2, y: 2, z: 4, core: 2. Of those that a mesh axis runs over, the one named last changes fastest.
Arguments:
- inputs: bfloat16 [4, 96, 197, 768], P(None, ('dp', 'expert')), may hold values from -6 to 6
- counts: int32 [4, 32], P(None, ('dp', 'expert')), may hold values from 1 to 3, 64 in all within a row
- ln1_gain: bfloat16 [768], P(('dp', 'expert')), may hold values from 0.099609375 to 1.8984375
- ln1_bias: bfloat16 [768], P(('dp', 'expert')), may hold values from -1.5 to 1.5
- w_qkv: bfloat16 [768, 2304], P(('dp', 'expert')), may hold values from -0.21875 to 0.21875
- w_out: bfloat16 [768, 768], P(('dp', 'expert')), may hold values from -0.625 to 0.625
- ln2_gain: bfloat16 [768], P(('dp', 'expert')), may hold values from 0.099609375 to 1.8984375
- ln2_bias: bfloat16 [768], P(('dp', 'expert')), may hold values from -1.5 to 1.5
- phi: bfloat16 [768, 8], P(('dp', 'expert')), may hold values from -0.125 to 0.125
- w_up: bfloat16 [8, 768, 3072], P('expert', None, 'dp'), may hold values from -1.75 to 1.75
- w_down: bfloat16 [8, 3072, 768], P('expert', 'dp'), may hold values from -0.4375 to 0.4375
- cotangent: bfloat16 [4, 96, 197, 768], P(None, ('dp', 'expert')), may hold values from -6 to 6
Outputs:
- output: bfloat16 [4, 96, 197, 768], P(None, ('dp', 'expert'))
- input_grad: bfloat16 [4, 96, 197, 768], P(None, ('dp', 'expert'))
- grad_ln1_gain: float32 [768], P(('dp', 'expert'))
- grad_ln1_bias: float32 [768], P(('dp', 'expert'))
- grad_w_qkv: float32 [768, 2304], P(('dp', 'expert'))
- grad_w_out: float32 [768, 768], P(('dp', 'expert'))
- grad_ln2_gain: float32 [768], P(('dp', 'expert'))
- grad_ln2_bias: float32 [768], P(('dp', 'expert'))
- grad_phi: float32 [768, 8], P(('dp', 'expert'))
- grad_w_up: float32 [8, 768, 3072], P('expert', None, 'dp')
- grad_w_down: float32 [8, 3072, 768], P('expert', 'dp')
The draws below stay inside these ranges and needn't reach their ends.
Inputs may be any that keep to these rules, and one draw needn't show every extreme that they name: counts[b, d] is how many of device d's first 3 image places hold live images in micro-batch b; each micro-batch holds 64 live images and some device is full.
All inputs are finite; a program needn't handle non-finite values.
Results may differ from the reference program's by a relative error of at most 0.018.
Values may be sent and summed in bfloat16 or wider, within the bound.
No kernel may reach another device: no remote copies, remote signals or barrier semaphores. Data moves between devices by JAX's collectives and lax.ppermute only.
A program may use at most 384 MiB of HBM per device.

```python
import math
import jax
import jax.numpy as jnp
import numpy as np
from jax import lax

D = 768
HEADS = 12
HEAD_DIM = 64
H = 3072
SEQ = 197
MB = 4
CAP = 3
EXPERTS = 8
IMGS = 96
DEVICES = 32


def steps_of(stream_key, shape, cuts, low, top_value):
    def one(dim, blocks):
        heights = jax.random.uniform(jax.random.fold_in(jax.random.fold_in(stream_key, 6), dim), (blocks,), jnp.float32, low / len(cuts), top_value / len(cuts))
        return jnp.repeat(jnp.exp(heights), shape[dim] // blocks).reshape((-1,) + (1,) * (len(shape) - dim - 1))

    gain = one(*cuts[0])
    for cut in cuts[1:]:
        gain = gain * one(*cut)
    return gain


def profile(number_of, total, bound, lean):
    portions = [(1 << 20) // math.isqrt(standing ** lean) + 1 for standing in range(2, number_of + 1)]
    surplus, given = total - bound - (number_of - 1), [1] * (number_of - 1)
    while surplus > 0:
        free = [i for i in range(number_of - 1) if given[i] < bound]
        mass, left = sum([portions[i] for i in free]), surplus
        for i in free:
            extra = min(bound - given[i], max(1, left * portions[i] // mass), surplus)
            given[i] = given[i] + extra
            surplus = surplus - extra
    return np.array([bound] + given)


def uneven_parts(rng, amount, total, bound, skew):
    if amount == 2:
        one = jax.random.randint(rng, (), max(1, total - bound), min(bound, total - 1) + 1)
        return jnp.stack([one, total - one])
    lengths = jnp.asarray(profile(amount, total, bound, skew), jnp.int32)
    pairs = (amount - 1) // 2
    source_of, sink = lengths[1:1 + 2 * pairs:2], lengths[2:2 + 2 * pairs:2]
    margin = jnp.minimum(source_of - 1, bound - sink)
    passed = jax.random.randint(jax.random.fold_in(rng, 1), (pairs,), 0, 1 << 20) % (margin + 1)
    lengths = lengths.at[1:1 + 2 * pairs:2].set(source_of - passed).at[2:2 + 2 * pairs:2].set(sink + passed)
    return lengths[jax.random.permutation(jax.random.fold_in(rng, 2), amount)]


def normal_values(stream_key, shape, width, bound, split=(), kind=jnp.bfloat16):
    drawn = width * jax.random.normal(stream_key, shape, jnp.float32)
    if split:
        drawn = drawn * steps_of(stream_key, shape, split, -0.22, 0.18)
    return jnp.clip(drawn, -bound, bound).astype(kind)


def setup_inputs(seed: int = 0) -> dict:
    splits = jax.random.split(jax.random.key(seed), 13)
    inputs = normal_values(splits[0], (MB, IMGS, SEQ, D), 1.0, 6.0, ((1, 32),))
    counts = jax.vmap(lambda own: uneven_parts(own, DEVICES, DEVICES * (CAP + 1) // 2, CAP, 1))(jax.random.split(splits[1], MB)).reshape((MB, DEVICES)).astype(jnp.int32)
    ln1_gain = jnp.clip(1.0 + 0.18 * jax.random.normal(splits[2], (D,), jnp.float32), 0.099609375, 1.8984375).astype(jnp.bfloat16)
    ln1_bias = normal_values(splits[3], (D,), 0.3, 1.5, ((0, 32),))
    w_qkv = normal_values(splits[4], (D, 3 * D), D ** -0.5, 0.21875, ((0, 32),))
    w_out = normal_values(splits[5], (D, D), (D // 8) ** -0.5, 0.625, ((0, 32),))
    ln2_gain = jnp.clip(1.0 + 0.18 * jax.random.normal(splits[6], (D,), jnp.float32), 0.099609375, 1.8984375).astype(jnp.bfloat16)
    ln2_bias = normal_values(splits[7], (D,), 0.3, 1.5, ((0, 32),))
    phi = normal_values(splits[8], (D, EXPERTS), (3 * D) ** -0.5, 0.125, ((0, 32),))
    w_up = normal_values(splits[9], (EXPERTS, D, H), (D // 64) ** -0.5, 1.75, ((0, 4), (2, 8)))
    w_down = normal_values(splits[10], (EXPERTS, H, D), (H // 16) ** -0.5, 0.4375, ((0, 4), (1, 8)))
    cotangent = normal_values(splits[11], (MB, IMGS, SEQ, D), 1.0, 6.0, ((1, 32),))
    return dict(inputs=inputs, counts=counts, ln1_gain=ln1_gain, ln1_bias=ln1_bias, w_qkv=w_qkv, w_out=w_out, ln2_gain=ln2_gain, ln2_bias=ln2_bias, phi=phi, w_up=w_up, w_down=w_down, cotangent=cotangent)


@jax.custom_vjp
def low(v):
    return lax.optimization_barrier(v.astype(jnp.bfloat16)).astype(jnp.float32)

@jax.custom_vjp
def low_back(v):
    return v

def low_keep(v):
    return (low(v), None)

def low_pass(kept, grad):
    return (grad,)

def back_keep(v):
    return (v, None)

def back_low(kept, grad):
    return (low(grad),)
low.defvjp(low_keep, low_pass)
low_back.defvjp(back_keep, back_low)
EXACT = lax.Precision.HIGHEST
EPSILON = 1e-06

def normalize(values, norm_gain, norm_bias):
    center = values - lax.optimization_barrier(jnp.mean(values, axis=-1, keepdims=True))
    spread = lax.optimization_barrier(jnp.mean(center * center, axis=-1, keepdims=True))
    return center * lax.rsqrt(spread + EPSILON) * norm_gain + norm_bias

def softmax_along(values, dimension):
    largest = lax.optimization_barrier(jnp.max(values, axis=dimension, keepdims=True))
    powers = jnp.exp(values - largest)
    return powers / lax.optimization_barrier(jnp.sum(powers, axis=dimension, keepdims=True))

def mixer_part(inputs, ln1_gain, ln1_bias, w_qkv, w_out, ln2_gain, ln2_bias, phi):
    images, length, features = inputs.shape
    normed = low(normalize(inputs, ln1_gain, ln1_bias))
    triple = low_back(low(jnp.einsum('gtd,de->gte', normed, w_qkv, precision=EXACT)))
    triple = triple.reshape(images, length, 3, HEADS, HEAD_DIM)
    queries = triple[:, :, 0]
    keys_all = triple[:, :, 1]
    values_all = triple[:, :, 2]
    scores = low_back(jnp.einsum('gqhc,gkhc->ghqk', queries, keys_all, precision=EXACT) * HEAD_DIM ** (-0.5))
    attention = low(softmax_along(scores, 3))
    mixed_heads = jnp.einsum('ghqk,gkhc->gqhc', attention, values_all, precision=EXACT)
    mixed_heads = low_back(low(mixed_heads.reshape(images, length, features)))
    branch = low_back(jnp.einsum('gtd,de->gte', mixed_heads, w_out, precision=EXACT))
    hidden_state = inputs + branch
    normed_two = low(normalize(hidden_state, ln2_gain, ln2_bias))
    logits = low_back(jnp.einsum('gtd,ds->gts', normed_two, phi, precision=EXACT))
    dispatch = low(softmax_along(logits, 1))
    combine = low(softmax_along(logits, 2))
    slot_in = low_back(low(jnp.einsum('gts,gtd->gsd', dispatch, normed_two, precision=EXACT)))
    return (hidden_state, combine, slot_in)

def expert_part(slot_rows, up_weight, down_weight):
    pre_act = low_back(jnp.einsum('gsd,sdf->gsf', slot_rows, up_weight, precision=EXACT))
    active = low(jax.nn.gelu(pre_act, approximate=False))
    return jnp.einsum('gsf,sfd->gsd', active, down_weight, precision=EXACT)

def combine_part(hidden_state, combine, slot_out):
    slot_out = low_back(slot_out)
    return hidden_state + jnp.einsum('gts,gsd->gtd', combine, slot_out, precision=EXACT)

def block_group(weight_set, group_in, group_live):
    ln1_gain, ln1_bias, w_qkv, w_out, ln2_gain, ln2_bias, phi, w_up, w_down = weight_set
    hidden_state, combine, slot_in = mixer_part(group_in, ln1_gain, ln1_bias, w_qkv, w_out, ln2_gain, ln2_bias, phi)
    slot_out = low(expert_part(slot_in, w_up, w_down))
    return combine_part(hidden_state, combine, slot_out) * group_live[:, None, None]

def reference(inputs, counts, ln1_gain, ln1_bias, w_qkv, w_out, ln2_gain, ln2_bias, phi, w_up, w_down, cotangent):
    per_group = 16
    groups = MB * CAP * DEVICES // per_group
    places = jnp.arange(CAP, dtype=jnp.int32)
    live_mask = (places[None, None, :] < counts[:, :, None]).astype(jnp.float32)
    live_mask = live_mask.reshape(groups, per_group)
    images_in = inputs.astype(jnp.float32).reshape(groups, per_group, SEQ, D)
    weight_set = tuple((member.astype(jnp.float32) for member in (ln1_gain, ln1_bias, w_qkv, w_out, ln2_gain, ln2_bias, phi, w_up, w_down)))
    checked = jax.checkpoint(block_group)

    def forward(weight_all, images_all):
        return lax.map(lambda packed: checked(weight_all, packed[0], packed[1]), (images_all, live_mask))
    result, pullback = jax.vjp(forward, weight_set, images_in)
    grad_weights, grad_in = pullback(cotangent.astype(jnp.float32).reshape(groups, per_group, SEQ, D))
    shape_all = (MB, CAP * DEVICES, SEQ, D)
    return (result.reshape(shape_all).astype(jnp.bfloat16), grad_in.reshape(shape_all).astype(jnp.bfloat16), grad_weights[0], grad_weights[1], grad_weights[2], grad_weights[3], grad_weights[4], grad_weights[5], grad_weights[6], grad_weights[7], grad_weights[8])
```

```python
from functools import partial

import jax
import jax.numpy as jnp
from jax import lax
from jax.sharding import PartitionSpec as P

HEADS = 12
HEAD_DIM = 64
EPSILON = 1e-06
BOTH = ("dp", "expert")


class Grid:
    def __init__(self, n, m):
        self.n, self.m = n, m
        self.size = {"z": n // 2, "y": 2, "x": m // 2, "c": 2}

    def coords(self):
        d, e = lax.axis_index("dp"), lax.axis_index("expert")
        return {"z": d // 2, "y": d % 2, "x": e // 2, "c": e % 2}

    def perm(self, axis, k):
        pairs = []
        for z in range(self.size["z"]):
            for y in range(2):
                for x in range(self.size["x"]):
                    for c in range(2):
                        p = {"z": z, "y": y, "x": x, "c": c}
                        q = dict(p)
                        q[axis] = (q[axis] + k) % self.size[axis]
                        pairs.append(tuple((r["z"] * 2 + r["y"]) * self.m + r["x"] * 2 + r["c"] for r in (p, q)))
        return pairs

    def send(self, a, axis, k):
        return lax.ppermute(a, BOTH, self.perm(axis, k))

    def by_coordinate(self, me, axis, pieces):
        s = self.size[axis]
        if s == 2:
            return jnp.stack([jnp.where(me == p, pieces[0], pieces[1]) for p in range(2)])
        if s <= 4:
            return jnp.stack([lax.select_n((me - p) % s, *pieces) for p in range(s)])
        out = jnp.zeros((s,) + pieces[0].shape, pieces[0].dtype)
        for k in range(s):
            out = lax.dynamic_update_index_in_dim(out, pieces[k], (me - k) % s, 0)
        return out

    def gather(self, a, axis, me):
        pieces = [a] + [self.send(a, axis, k) for k in range(1, self.size[axis])]
        return self.by_coordinate(me[axis], axis, pieces)

    def block(self, a, axis, me, k):
        return lax.dynamic_index_in_dim(a, (me[axis] + k) % self.size[axis], 0, keepdims=False)

    def scatter_sum(self, a, axis, me):
        own = self.block(a, axis, me, 0).astype(jnp.float32)
        for k in range(1, self.size[axis]):
            own = own + self.send(self.block(a, axis, me, k), axis, k).astype(jnp.float32)
        return own

    def exchange(self, a, axis, me):
        pieces = [self.block(a, axis, me, k) for k in range(self.size[axis])]
        pieces = pieces[:1] + [self.send(p, axis, k) for k, p in enumerate(pieces) if k]
        return self.by_coordinate(me[axis], axis, pieces)


def joined(parts, axis):
    return jnp.concatenate(parts, axis=axis) if len(parts) > 1 else parts[0]


def gather_rows(grid, a, cuts, me):
    outs, low = [], 0
    for width, order in cuts:
        b, done = a[:, low : low + width], []
        low += width
        for axis in order:
            b = grid.gather(b, axis, me)
            done.insert(0, axis)
        outs.append(jnp.transpose(b, [done.index(axis) for axis in "zyxc"] + [4, 5]))
    return joined(outs, -1).reshape(-1, a.shape[1])


def reduce_rows(grid, a, cuts, me):
    s = grid.size
    a = a.reshape(s["z"], 2, s["x"], 2, -1, a.shape[1])
    outs, low = [], 0
    for width, order in cuts:
        b, left = a[..., low : low + width], ["z", "y", "x", "c"]
        low += width
        for axis in order:
            b = jnp.moveaxis(b.astype(jnp.bfloat16), left.index(axis), 0)
            b = grid.scatter_sum(b, axis, me)
            left.remove(axis)
        outs.append(b)
    return joined(outs, -1)


def to_experts(grid, a, part, me):
    s = grid.size
    b = grid.exchange(a.reshape(s["x"], 2, *a.shape[1:]), "x", me)
    b = grid.exchange(jnp.moveaxis(b, 1, 0), "c", me)
    b = jnp.moveaxis(b, 0, 1).reshape(a.shape)
    first = grid.gather(grid.gather(b[:, :part], "z", me), "y", me)
    second = grid.gather(grid.gather(b[:, part:], "y", me), "z", me)
    r = jnp.concatenate([jnp.moveaxis(first, 0, 1), second], axis=3)
    return r.reshape(grid.n, *a.shape)


def from_experts(grid, a, part, me):
    s = grid.size
    b = a.reshape(s["z"], 2, *a.shape[1:])
    first = grid.scatter_sum(jnp.moveaxis(b[:, :, :, :part], 1, 0), "y", me).astype(jnp.bfloat16)
    first = grid.scatter_sum(first, "z", me)
    second = grid.scatter_sum(b[:, :, :, part:], "z", me).astype(jnp.bfloat16)
    second = grid.scatter_sum(second, "y", me)
    r = jnp.concatenate([first, second], axis=1).astype(jnp.bfloat16)
    r = grid.exchange(r.reshape(s["x"], 2, *r.shape[1:]), "x", me)
    r = grid.exchange(jnp.moveaxis(r, 1, 0), "c", me)
    return jnp.moveaxis(r, 0, 1).reshape(a.shape[1:])


def round_down(v):
    return lax.optimization_barrier(v.astype(jnp.bfloat16)).astype(jnp.float32)


def same_value(v):
    return v


def make_rounders():
    rounded = jax.custom_vjp(round_down)
    rounded.defvjp(lambda v: (round_down(v), None), lambda kept, grad: (grad,))
    back_rounded = jax.custom_vjp(same_value)
    back_rounded.defvjp(lambda v: (v, None), lambda kept, grad: (round_down(grad),))
    return (rounded, back_rounded)


def normalize(values, norm_gain, norm_bias):
    center = values - jnp.mean(values, axis=-1, keepdims=True)
    spread = jnp.mean(center * center, axis=-1, keepdims=True)
    return center * lax.rsqrt(spread + EPSILON) * norm_gain + norm_bias


def softmax_along(values, dimension):
    largest = jnp.max(values, axis=dimension, keepdims=True)
    powers = jnp.exp(values - largest)
    return powers / jnp.sum(powers, axis=dimension, keepdims=True)


def mixer_part(inputs, ln1_gain, ln1_bias, w_qkv, w_out, ln2_gain, ln2_bias, phi):
    rounded, back_rounded = make_rounders()
    images, length, features = inputs.shape
    normed = rounded(normalize(inputs, ln1_gain, ln1_bias))
    triple = back_rounded(rounded(jnp.einsum("gtd,de->gte", normed, w_qkv)))
    triple = triple.reshape(images, length, 3, HEADS, HEAD_DIM)
    queries = triple[:, :, 0]
    keys_all = triple[:, :, 1]
    values_all = triple[:, :, 2]
    scores = back_rounded(jnp.einsum("gqhc,gkhc->ghqk", queries, keys_all) * HEAD_DIM ** (-0.5))
    attention = rounded(softmax_along(scores, 3))
    mixed_heads = jnp.einsum("ghqk,gkhc->gqhc", attention, values_all)
    mixed_heads = back_rounded(rounded(mixed_heads.reshape(images, length, features)))
    branch = back_rounded(jnp.einsum("gtd,de->gte", mixed_heads, w_out))
    hidden_state = inputs + branch
    normed_two = rounded(normalize(hidden_state, ln2_gain, ln2_bias))
    logits = back_rounded(jnp.einsum("gtd,ds->gts", normed_two, phi))
    dispatch = rounded(softmax_along(logits, 1))
    combine = rounded(softmax_along(logits, 2))
    slot_in = back_rounded(rounded(jnp.einsum("gts,gtd->gsd", dispatch, normed_two)))
    return (hidden_state, combine, slot_in)


def combine_part(hidden_state, combine, slot_out):
    rounded, back_rounded = make_rounders()
    slot_out = back_rounded(slot_out)
    return hidden_state + jnp.einsum("gts,gsd->gtd", combine, slot_out)


def experts(rows, grads, up, down):
    f32 = jnp.float32
    pre = jnp.einsum("rsd,sdf->srf", rows, up, preferred_element_type=f32)
    active, slope = jax.vjp(partial(jax.nn.gelu, approximate=False), pre)
    active = active.astype(jnp.bfloat16)
    out = jnp.einsum("srf,sfd->rsd", active, down, preferred_element_type=f32)
    grad_active = jnp.einsum("rsd,sfd->srf", grads, down, preferred_element_type=f32)
    grad_pre = slope(grad_active)[0].astype(jnp.bfloat16)
    grad_rows = jnp.einsum("srf,sdf->rsd", grad_pre, up, preferred_element_type=f32)
    grad_up = jnp.einsum("rsd,srf->sdf", rows, grad_pre, preferred_element_type=f32)
    grad_down = jnp.einsum("srf,rsd->sfd", active, grads, preferred_element_type=f32)
    return (out, grad_rows, grad_up, grad_down)


def body(grid, inputs, counts, ln1_gain, ln1_bias, w_qkv, w_out, ln2_gain, ln2_bias, phi, w_up, w_down, cotangent):
    me = grid.coords()
    batches, capacity, length, features = inputs.shape
    images = batches * capacity
    slots = phi.shape[1]
    per = slots // grid.m
    vectors = jnp.stack([ln1_gain, ln1_bias, ln2_gain, ln2_bias], axis=1)
    small = jnp.concatenate([vectors, phi], axis=1)
    small = jnp.pad(small, ((0, 0), (0, 128 - small.shape[1])))
    packed = jnp.concatenate([w_qkv, w_out, small], axis=1)
    whole = gather_rows(grid, packed, ((1664, "zyxc"), (1536, "zxyc")), me)
    w_qkv_all, w_out_all = whole[:, : 3 * features], whole[:, 3 * features : 4 * features]
    small_all = whole[:, 4 * features :]
    dense = (
        small_all[:, 0],
        small_all[:, 1],
        w_qkv_all,
        w_out_all,
        small_all[:, 2],
        small_all[:, 3],
        small_all[:, 4 : 4 + slots],
    )
    dense = tuple(member.astype(jnp.float32) for member in dense)
    live = (jnp.arange(capacity)[None, :] < counts).astype(jnp.float32).reshape(images, 1, 1)
    image_in = inputs.reshape(images, length, features).astype(jnp.float32)
    (hidden_state, combine, slot_in), mixer_back = jax.vjp(mixer_part, image_in, *dense)
    grad_result = cotangent.reshape(images, length, features).astype(jnp.float32) * live
    grad_slot = jnp.einsum("gts,gtd->gsd", combine, grad_result)
    leaving = jnp.stack([slot_in.astype(jnp.bfloat16), grad_slot.astype(jnp.bfloat16)])
    leaving = leaving.reshape(2 * images, grid.m, per * features).transpose(1, 0, 2)
    rows_all = 2 * images
    arrived = to_experts(grid, leaving, rows_all * 2 // 3, me)
    arrived = arrived.reshape(grid.n * grid.m, 2, images, per, features)
    rows = arrived[:, 0].reshape(-1, per, features)
    grads = arrived[:, 1].reshape(-1, per, features)
    out, grad_rows, grad_up, grad_down = experts(rows, grads, w_up, w_down)
    back = jnp.stack([out.astype(jnp.bfloat16).reshape(-1, images, per * features), grad_rows.astype(jnp.bfloat16).reshape(-1, images, per * features)], axis=1)
    back = back.reshape(grid.n, grid.m, rows_all, per * features)
    home = from_experts(grid, back, rows_all * 2 // 3, me)
    home = home.transpose(1, 0, 2).reshape(2, images, slots, features).astype(jnp.float32)
    result, combine_back = jax.vjp(combine_part, hidden_state, combine, home[0])
    output = (result * live).astype(jnp.bfloat16)
    grad_hidden, grad_combine, _ = combine_back(grad_result)
    grads_all = mixer_back((grad_hidden, grad_combine, home[1]))
    vectors = jnp.stack([grads_all[1], grads_all[2], grads_all[5], grads_all[6]], axis=1)
    small = jnp.concatenate([vectors, grads_all[7]], axis=1)
    small = jnp.pad(small, ((0, 0), (0, 128 - small.shape[1])))
    packed = jnp.concatenate([grads_all[3], grads_all[4], small], axis=1)
    sums = reduce_rows(grid, packed, ((1664, "cxyz"), (1536, "cyxz")), me)
    small = sums[:, 4 * features :]
    return (
        output.reshape(inputs.shape),
        grads_all[0].astype(jnp.bfloat16).reshape(inputs.shape),
        small[:, 0],
        small[:, 1],
        sums[:, : 3 * features],
        sums[:, 3 * features : 4 * features],
        small[:, 2],
        small[:, 3],
        small[:, 4 : 4 + slots],
        grad_up,
        grad_down,
    )


def solution(mesh):
    rows = P(BOTH, None)
    row = P(BOTH)
    image = P(None, BOTH, None, None)
    up, down = P("expert", None, "dp"), P("expert", "dp", None)
    grid = Grid(mesh.shape["dp"], mesh.shape["expert"])
    return jax.shard_map(
        partial(body, grid),
        mesh=mesh,
        in_specs=(image, P(None, BOTH), row, row, rows, rows, row, row, rows, up, down, image),
        out_specs=(image, image, row, row, rows, rows, row, row, rows, up, down),
        check_vma=False,
    )
```

```python
from functools import partial

import jax
import jax.numpy as jnp
from jax import lax
from jax.experimental import pallas as pl
from jax.experimental.pallas import tpu as pltpu
from jax.sharding import PartitionSpec as P

HEADS = 12
HEAD_DIM = 64
EPSILON = 1e-06
BOTH = ("dp", "expert")
F32, BF16 = jnp.float32, jnp.bfloat16
LOW = -1e30
VMEM_LIMIT = 60 * 1024 * 1024
CHUNKS = 1


class Grid:
    def __init__(self, n, m):
        self.n, self.m = n, m
        self.size = {"z": n // 2, "y": 2, "x": m // 2, "c": 2}

    def coords(self):
        d, e = lax.axis_index("dp"), lax.axis_index("expert")
        return {"z": d // 2, "y": d % 2, "x": e // 2, "c": e % 2}

    def perm(self, axis, k):
        pairs = []
        for z in range(self.size["z"]):
            for y in range(2):
                for x in range(self.size["x"]):
                    for c in range(2):
                        p = {"z": z, "y": y, "x": x, "c": c}
                        q = dict(p)
                        q[axis] = (q[axis] + k) % self.size[axis]
                        pairs.append(tuple((r["z"] * 2 + r["y"]) * self.m + r["x"] * 2 + r["c"] for r in (p, q)))
        return pairs

    def send(self, a, axis, k):
        return lax.ppermute(a, BOTH, self.perm(axis, k))

    def by_coordinate(self, me, axis, pieces):
        s = self.size[axis]
        if s == 2:
            return jnp.stack([jnp.where(me == p, pieces[0], pieces[1]) for p in range(2)])
        if s <= 4:
            return jnp.stack([lax.select_n((me - p) % s, *pieces) for p in range(s)])
        out = jnp.zeros((s,) + pieces[0].shape, pieces[0].dtype)
        for k in range(s):
            out = lax.dynamic_update_index_in_dim(out, pieces[k], (me - k) % s, 0)
        return out

    def gather(self, a, axis, me):
        pieces = [a] + [self.send(a, axis, k) for k in range(1, self.size[axis])]
        return self.by_coordinate(me[axis], axis, pieces)

    def block(self, a, axis, me, k):
        return lax.dynamic_index_in_dim(a, (me[axis] + k) % self.size[axis], 0, keepdims=False)

    def scatter_sum(self, a, axis, me):
        own = self.block(a, axis, me, 0).astype(jnp.float32)
        for k in range(1, self.size[axis]):
            own = own + self.send(self.block(a, axis, me, k), axis, k).astype(jnp.float32)
        return own

    def exchange(self, a, axis, me):
        pieces = [self.block(a, axis, me, k) for k in range(self.size[axis])]
        pieces = pieces[:1] + [self.send(p, axis, k) for k, p in enumerate(pieces) if k]
        return self.by_coordinate(me[axis], axis, pieces)


def joined(parts, axis):
    return jnp.concatenate(parts, axis=axis) if len(parts) > 1 else parts[0]


def gather_rows(grid, a, cuts, me):
    outs, low = [], 0
    for width, order in cuts:
        b, done = a[:, low : low + width], []
        low += width
        for axis in order:
            b = grid.gather(b, axis, me)
            done.insert(0, axis)
        outs.append(jnp.transpose(b, [done.index(axis) for axis in "zyxc"] + [4, 5]))
    return joined(outs, -1).reshape(-1, a.shape[1])


def reduce_rows(grid, a, cuts, me):
    s = grid.size
    a = a.reshape(s["z"], 2, s["x"], 2, -1, a.shape[1])
    outs, low = [], 0
    for width, order in cuts:
        b, left = a[..., low : low + width], ["z", "y", "x", "c"]
        low += width
        for axis in order:
            b = jnp.moveaxis(b.astype(jnp.bfloat16), left.index(axis), 0)
            b = grid.scatter_sum(b, axis, me)
            left.remove(axis)
        outs.append(b)
    return joined(outs, -1)


def to_experts(grid, a, part, me):
    s = grid.size
    b = grid.exchange(a.reshape(s["x"], 2, *a.shape[1:]), "x", me)
    b = grid.exchange(jnp.moveaxis(b, 1, 0), "c", me)
    b = jnp.moveaxis(b, 0, 1).reshape(a.shape)
    first = grid.gather(grid.gather(b[:, :part], "z", me), "y", me)
    second = grid.gather(grid.gather(b[:, part:], "y", me), "z", me)
    r = jnp.concatenate([jnp.moveaxis(first, 0, 1), second], axis=3)
    return r.reshape(grid.n, *a.shape)


def from_experts(grid, a, part, me):
    s = grid.size
    b = a.reshape(s["z"], 2, *a.shape[1:])
    first = grid.scatter_sum(jnp.moveaxis(b[:, :, :, :part], 1, 0), "y", me).astype(jnp.bfloat16)
    first = grid.scatter_sum(first, "z", me)
    second = grid.scatter_sum(b[:, :, :, part:], "z", me).astype(jnp.bfloat16)
    second = grid.scatter_sum(second, "y", me)
    r = jnp.concatenate([first, second], axis=1).astype(jnp.bfloat16)
    r = grid.exchange(r.reshape(s["x"], 2, *r.shape[1:]), "x", me)
    r = grid.exchange(jnp.moveaxis(r, 1, 0), "c", me)
    return jnp.moveaxis(r, 0, 1).reshape(a.shape[1:])


def dot(a, b, ca=1, cb=0):
    return lax.dot_general(a, b, (((ca,), (cb,)), ((), ())), preferred_element_type=F32)


def standardized(v):
    width = v.shape[-1]
    center = v - jnp.sum(v, axis=-1, keepdims=True) * (1.0 / width)
    root = lax.rsqrt(jnp.sum(center * center, axis=-1, keepdims=True) * (1.0 / width) + EPSILON)
    return center * root, root


def head_masks():
    lane = lax.broadcasted_iota(jnp.int32, (1, 2 * HEAD_DIM), 1)
    return [(lane // HEAD_DIM == h) for h in range(2)]


def routed(logits, tokens, slots):
    row = lax.broadcasted_iota(jnp.int32, logits.shape, 0)
    lane = lax.broadcasted_iota(jnp.int32, logits.shape, 1)
    valid = (row < tokens) & (lane < slots)
    kept = jnp.where(valid, logits, LOW)
    down = jnp.where(valid, jnp.exp(kept - jnp.max(kept, axis=0, keepdims=True)), 0.0)
    down_sum = jnp.sum(down, axis=0, keepdims=True)
    over_tokens = down * (1.0 / jnp.where(down_sum > 0, down_sum, 1.0))
    across = jnp.where(valid, jnp.exp(kept - jnp.max(kept, axis=1, keepdims=True)), 0.0)
    across_sum = jnp.sum(across, axis=1, keepdims=True)
    over_slots = across * (1.0 / jnp.where(across_sum > 0, across_sum, 1.0))
    return over_tokens, over_slots


def forward_kernel(tokens, slots, live, x_ref, cot_ref, wqkv_ref, wout_ref, phi_ref, vec_ref,
                   n1_ref, triple_ref, mixed_ref, hidden_ref, logits_ref, slot_ref, grad_slot_ref, pad_ref):
    i = pl.program_id(0)
    rows, features = pad_ref.shape
    keys = triple_ref.shape[1]

    @pl.when(i == 0)
    def _():
        pad_ref[...] = jnp.zeros_like(pad_ref)

    @pl.when(live[i] == 0)
    def _():
        n1_ref[...] = jnp.zeros_like(n1_ref)
        mixed_ref[...] = jnp.zeros_like(mixed_ref)
        slot_ref[...] = jnp.zeros_like(slot_ref)
        grad_slot_ref[...] = jnp.zeros_like(grad_slot_ref)

    @pl.when(live[i] != 0)
    def _():
        pad_ref[:tokens] = x_ref[0, 0].astype(F32)
        x = pad_ref[...]
        n1, _ = standardized(x)
        n1_ref[0] = n1.astype(BF16)
        normed = (n1 * vec_ref[0:1] + vec_ref[1:2]).astype(BF16)
        for part in range(3):
            cut = slice(part * features, (part + 1) * features)
            triple_ref[0, :rows, cut] = dot(normed, wqkv_ref[:, cut]).astype(BF16)
        triple_ref[0, rows:, :] = jnp.zeros((keys - rows, 3 * features), BF16)
        bias = jnp.where(lax.broadcasted_iota(jnp.int32, (1, keys), 1) < tokens, 0.0, LOW)
        masks = head_masks()
        for pair in range(HEADS // 2):
            low = pair * 2 * HEAD_DIM
            q = triple_ref[0, :rows, low:low + 128]
            k = triple_ref[0, :, features + low:features + low + 128]
            v = triple_ref[0, :, 2 * features + low:2 * features + low + 128]
            total = None
            for mask in masks:
                scale = jnp.where(mask, HEAD_DIM ** -0.5, 0.0).astype(BF16)
                scores = dot(q * scale, k, 1, 1) + bias
                powers = jnp.exp(scores - jnp.max(scores, axis=1, keepdims=True))
                attention = (powers * (1.0 / jnp.sum(powers, axis=1, keepdims=True))).astype(BF16)
                part = dot(attention, v * jnp.where(mask, 1.0, 0.0).astype(BF16))
                total = part if total is None else total + part
            mixed_ref[0, :, low:low + 128] = total.astype(BF16)
        hidden = pad_ref[...] + dot(mixed_ref[0], wout_ref[...])
        hidden_ref[0] = hidden
        n2, _ = standardized(hidden)
        normed_two = (n2 * vec_ref[2:3] + vec_ref[3:4]).astype(BF16)
        logits = dot(normed_two, phi_ref[...])
        logits_ref[0] = logits
        dispatch, combine = routed(logits, tokens, slots)
        kept = slot_ref.shape[1]
        slot_ref[0] = dot(dispatch.astype(BF16), normed_two, 0, 0)[:kept].astype(BF16)
        pad_ref[:tokens] = cot_ref[0, 0].astype(F32)
        grad_slot_ref[0] = dot(combine.astype(BF16), pad_ref[...].astype(BF16), 0, 0)[:kept].astype(BF16)


def backward_kernel(tokens, slots, live, cot_ref, triple_ref, hidden_ref, logits_ref, slot_out_ref, grad_in_ref,
                    woutt_ref, phit_ref, vec_ref,
                    out_ref, grad_branch_ref, grad_triple_ref, small_ref, pad_ref, gm_ref):
    i = pl.program_id(0)
    rows, features = pad_ref.shape
    keys = triple_ref.shape[1]

    @pl.when(i == 0)
    def _():
        pad_ref[...] = jnp.zeros_like(pad_ref)
        gm_ref[...] = jnp.zeros_like(gm_ref)
        small_ref[...] = jnp.zeros_like(small_ref)

    @pl.when(live[i] == 0)
    def _():
        out_ref[...] = jnp.zeros_like(out_ref)
        grad_branch_ref[...] = jnp.zeros_like(grad_branch_ref)
        grad_triple_ref[...] = jnp.zeros_like(grad_triple_ref)

    @pl.when(live[i] != 0)
    def _():
        hidden = hidden_ref[0]
        n2, root = standardized(hidden)
        gain = vec_ref[2:3]
        normed_two = (n2 * gain + vec_ref[3:4]).astype(BF16)
        over_tokens, over_slots = routed(logits_ref[0], tokens, slots)
        dispatch, combine = over_tokens.astype(BF16), over_slots.astype(BF16)
        slot_out, grad_in = slot_out_ref[0], grad_in_ref[0]
        pad_ref[:tokens] = cot_ref[0, 0].astype(F32)
        cot = pad_ref[...]
        result = hidden + dot(combine, slot_out)
        out_ref[0, 0] = result[:tokens].astype(BF16)
        grad_combine = dot(cot.astype(BF16), slot_out, 1, 1)
        grad_dispatch = dot(normed_two, grad_in, 1, 1)
        grad_logits = over_tokens * (grad_dispatch - jnp.sum(grad_dispatch * over_tokens, axis=0, keepdims=True))
        grad_logits += over_slots * (grad_combine - jnp.sum(grad_combine * over_slots, axis=1, keepdims=True))
        grad_logits = grad_logits.astype(BF16)
        grad_two = dot(dispatch, grad_in) + dot(grad_logits, phit_ref[...])
        small_ref[0:1] += jnp.sum(grad_two * n2, axis=0, keepdims=True)
        small_ref[1:2] += jnp.sum(grad_two, axis=0, keepdims=True)
        kept = small_ref.shape[0] - 8
        small_ref[8:] += dot(grad_logits, normed_two, 0, 0)[:kept]
        u = grad_two * gain
        inner = u - jnp.sum(u, axis=-1, keepdims=True) * (1.0 / features)
        inner = inner - n2 * (jnp.sum(u * n2, axis=-1, keepdims=True) * (1.0 / features))
        grad_branch = (cot + root * inner).astype(BF16)
        grad_branch_ref[0] = grad_branch
        gm_ref[:rows] = dot(grad_branch, woutt_ref[...]).astype(BF16)
        valid = lax.broadcasted_iota(jnp.int32, (rows, 1), 0) < tokens
        for pair in range(HEADS // 2):
            low = pair * 2 * HEAD_DIM
            q = triple_ref[0, :, low:low + 128]
            k = triple_ref[0, :rows, features + low:features + low + 128]
            v = triple_ref[0, :rows, 2 * features + low:2 * features + low + 128]
            gm = gm_ref[:, low:low + 128]
            grad_q = grad_k = grad_v = None
            for mask in head_masks():
                one = jnp.where(mask, 1.0, 0.0).astype(BF16)
                scale = jnp.where(mask, HEAD_DIM ** -0.5, 0.0).astype(BF16)
                q_own, gm_own = q * scale, gm * one
                scores = jnp.where(valid, dot(k, q_own, 1, 1), LOW)
                powers = jnp.exp(scores - jnp.max(scores, axis=0, keepdims=True))
                attention = powers * (1.0 / jnp.sum(powers, axis=0, keepdims=True))
                grad_attention = dot(v, gm_own, 1, 1)
                mean = jnp.sum(grad_attention * attention, axis=0, keepdims=True)
                grad_scores = (attention * (grad_attention - mean)).astype(BF16)
                parts = (dot(grad_scores, k * scale, 0, 0), dot(grad_scores, q_own), dot(attention.astype(BF16), gm_own))
                if grad_q is None:
                    grad_q, grad_k, grad_v = parts
                else:
                    grad_q, grad_k, grad_v = grad_q + parts[0], grad_k + parts[1], grad_v + parts[2]
            grad_triple_ref[0, :, low:low + 128] = grad_q[:rows].astype(BF16)
            grad_triple_ref[0, :, features + low:features + low + 128] = grad_k.astype(BF16)
            grad_triple_ref[0, :, 2 * features + low:2 * features + low + 128] = grad_v.astype(BF16)


def input_kernel(tokens, live, x_ref, grad_triple_ref, grad_branch_ref, wqkvt_ref, vec_ref, out_ref, pad_ref):
    i = pl.program_id(0)
    features = pad_ref.shape[1]

    @pl.when(i == 0)
    def _():
        pad_ref[...] = jnp.zeros_like(pad_ref)

    @pl.when(live[i] == 0)
    def _():
        out_ref[...] = jnp.zeros_like(out_ref)

    @pl.when(live[i] != 0)
    def _():
        pad_ref[:tokens] = x_ref[0, 0].astype(F32)
        n1, root = standardized(pad_ref[...])
        v = dot(grad_triple_ref[0], wqkvt_ref[...]) * vec_ref[0:1]
        inner = v - jnp.sum(v, axis=-1, keepdims=True) * (1.0 / features)
        inner = inner - n1 * (jnp.sum(v * n1, axis=-1, keepdims=True) * (1.0 / features))
        grad = grad_branch_ref[0].astype(F32) + root * inner
        out_ref[0, 0] = grad[:tokens].astype(BF16)


def image_spec(tokens, features, capacity, first):
    return pl.BlockSpec((1, 1, tokens, features), lambda i, live: ((i + first) // capacity, (i + first) % capacity, 0, 0))


def own(*shape):
    return pl.BlockSpec((1,) + shape, lambda i, live: (i,) + (0,) * len(shape))


def fixed(*shape):
    return pl.BlockSpec(shape, lambda i, live: (0,) * len(shape), pipeline_mode=pl.Buffered(1))


def call(kernel, images, in_specs, out_specs, out_shape, scratch):
    return pl.pallas_call(
        kernel,
        grid_spec=pltpu.PrefetchScalarGridSpec(num_scalar_prefetch=1, grid=(images,), in_specs=in_specs, out_specs=out_specs, scratch_shapes=scratch),
        out_shape=out_shape,
        compiler_params=pltpu.CompilerParams(vmem_limit_bytes=VMEM_LIMIT, dimension_semantics=("arbitrary",)),
    )


def padded(v, step):
    return -(-v // step) * step


def forward(live, inputs, cotangent, wqkv, wout, phi, vectors, slots, first, images):
    capacity, tokens, features = inputs.shape[1:]
    rows, keys, kept = padded(tokens, 16), padded(tokens, 128), padded(slots, 16)
    image = image_spec(tokens, features, capacity, first)
    shape = jax.ShapeDtypeStruct
    return call(
        partial(forward_kernel, tokens, slots), images,
        [image, image, fixed(*wqkv.shape), fixed(*wout.shape), fixed(*phi.shape), fixed(*vectors.shape)],
        [own(rows, features), own(keys, 3 * features), own(rows, features), own(rows, features), own(rows, 128), own(kept, features), own(kept, features)],
        [shape((images, rows, features), BF16), shape((images, keys, 3 * features), BF16), shape((images, rows, features), BF16),
         shape((images, rows, features), F32), shape((images, rows, 128), F32), shape((images, kept, features), BF16), shape((images, kept, features), BF16)],
        [pltpu.VMEM((rows, features), F32)],
    )(live, inputs, cotangent, wqkv, wout, phi, vectors)


def backward(live, cotangent, triple, hidden, logits, slot_out, grad_in, woutt, phit, vectors, slots, first):
    capacity, tokens, features = cotangent.shape[1:]
    images, rows = hidden.shape[:2]
    keys, kept = triple.shape[1], padded(slots, 8)
    image = image_spec(tokens, features, capacity, first)
    shape = jax.ShapeDtypeStruct
    return call(
        partial(backward_kernel, tokens, slots), images,
        [image, own(keys, 3 * features), own(rows, features), own(rows, 128), own(128, features), own(128, features),
         fixed(*woutt.shape), fixed(*phit.shape), fixed(*vectors.shape)],
        [pl.BlockSpec((1, 1, tokens, features), lambda i, live: (i, 0, 0, 0)), own(rows, features), own(rows, 3 * features), pl.BlockSpec((8 + kept, features), lambda i, live: (0, 0))],
        [shape((images, 1, tokens, features), BF16), shape((images, rows, features), BF16), shape((images, rows, 3 * features), BF16), shape((8 + kept, features), F32)],
        [pltpu.VMEM((rows, features), F32), pltpu.VMEM((keys, features), BF16)],
    )(live, cotangent, triple, hidden, logits, slot_out, grad_in, woutt, phit, vectors)


def input_backward(live, inputs, grad_triple, grad_branch, wqkvt, vectors, first):
    capacity, tokens, features = inputs.shape[1:]
    images, rows = grad_branch.shape[:2]
    shape = jax.ShapeDtypeStruct
    return call(
        partial(input_kernel, tokens), images,
        [image_spec(tokens, features, capacity, first), own(rows, 3 * features), own(rows, features), fixed(*wqkvt.shape), fixed(*vectors.shape)],
        [pl.BlockSpec((1, 1, tokens, features), lambda i, live: (i, 0, 0, 0))],
        [shape((images, 1, tokens, features), BF16)],
        [pltpu.VMEM((rows, features), F32)],
    )(live, inputs, grad_triple, grad_branch, wqkvt, vectors)[0]


def experts(rows, grads, up, down):
    pre = jnp.einsum("srd,sdf->srf", rows, up, preferred_element_type=F32)
    active, slope = jax.vjp(partial(jax.nn.gelu, approximate=False), pre)
    active = active.astype(BF16)
    out = jnp.einsum("srf,sfd->srd", active, down, preferred_element_type=F32)
    grad_active = jnp.einsum("srd,sfd->srf", grads, down, preferred_element_type=F32)
    grad_pre = slope(grad_active)[0].astype(BF16)
    grad_rows = jnp.einsum("srf,sdf->srd", grad_pre, up, preferred_element_type=F32)
    return (out, grad_rows, active, grad_pre)


def columns(vectors, table):
    small = jnp.concatenate([jnp.stack(vectors, axis=1), table], axis=1)
    return jnp.pad(small, ((0, 0), (0, 128 - small.shape[1])))


def body(grid, inputs, counts, ln1_gain, ln1_bias, w_qkv, w_out, ln2_gain, ln2_bias, phi, w_up, w_down, cotangent):
    me = grid.coords()
    batches, capacity, tokens, features = inputs.shape
    slots = phi.shape[1]
    per = slots // grid.m
    packed = jnp.concatenate([w_qkv, w_out, columns([ln1_gain, ln1_bias, ln2_gain, ln2_bias], phi)], axis=1)
    whole = gather_rows(grid, packed, ((1664, "zyxc"), (1536, "zxyc")), me)
    wqkv, wout, small = whole[:, : 3 * features], whole[:, 3 * features : 4 * features], whole[:, 4 * features :]
    vectors = jnp.pad(small[:, :4].T.astype(F32), ((0, 4), (0, 0)))
    phi_all = jnp.pad(small[:, 4 : 4 + slots], ((0, 0), (0, 128 - slots)))
    live = (jnp.arange(capacity)[None, :] < counts).astype(jnp.int32).reshape(-1)

    chunks = []
    step = batches * capacity // CHUNKS
    for c in range(CHUNKS):
        own_live = live[c * step : (c + 1) * step]
        kept = forward(own_live, inputs, cotangent, wqkv, wout, phi_all, vectors, slots, c * step, step)
        leaving = jnp.stack([kept[5][:, :slots], kept[6][:, :slots]]).reshape(2, step, grid.m, per, features)
        leaving = leaving.transpose(2, 3, 0, 1, 4).reshape(grid.m, per * 2 * step, features)
        chunks.append([own_live, kept, leaving])
    part = padded(per * 2 * step * 2 // 3, 8)
    for c in range(CHUNKS):
        arrived = to_experts(grid, chunks[c][2], part, me)
        arrived = arrived.reshape(grid.n * grid.m, per, 2, step, features)
        rows, grads = (arrived[:, :, k].transpose(1, 0, 2, 3).reshape(per, -1, features) for k in range(2))
        out, grad_rows, active, grad_pre = experts(rows, grads, w_up, w_down)
        back = jnp.stack([a.astype(BF16).reshape(per, grid.n, grid.m, step, features) for a in (out, grad_rows)])
        back = back.transpose(2, 3, 1, 0, 4, 5).reshape(grid.n, grid.m, per * 2 * step, features)
        home = from_experts(grid, back, part, me).reshape(grid.m, per, 2, step, features)
        home = home.transpose(2, 3, 0, 1, 4).reshape(2, step, slots, features)
        chunks[c] += [(rows, grads, active, grad_pre), jnp.pad(home, ((0, 0), (0, 0), (0, 128 - slots), (0, 0)))]
    outs, grads_out, small, made = [], [], 0.0, []
    for c, (own_live, kept, _, _, home) in enumerate(chunks):
        out, grad_branch, grad_triple, sums = backward(
            own_live, cotangent, kept[1], kept[3], kept[4], home[0], home[1], wout.T, phi_all.T, vectors, slots, c * step
        )
        outs.append(out)
        small = small + sums
        made.append((kept[0], kept[2], grad_branch, grad_triple))
    rows, grads, active, grad_pre = (joined([c[3][k] for c in chunks], 1) for k in range(4))
    grad_up = jnp.einsum("srd,srf->sdf", rows, grad_pre, preferred_element_type=F32)
    grad_down = jnp.einsum("srf,srd->sfd", active, grads, preferred_element_type=F32)
    n1, mixed, grad_branch, grad_triple = (joined([m[k] for m in made], 0).reshape(-1, made[0][k].shape[-1]) for k in range(4))
    product = dot(n1, grad_triple, 0, 0)
    total = jnp.sum(grad_triple.astype(F32), axis=0, keepdims=True)
    grad_wqkv = vectors[0][:, None] * product + vectors[1][:, None] * total
    grad_ln1_gain = jnp.sum(wqkv.astype(F32) * product, axis=1)
    grad_ln1_bias = jnp.sum(wqkv.astype(F32) * total, axis=1)
    grad_wout = dot(mixed, grad_branch, 0, 0)
    small = columns([grad_ln1_gain, grad_ln1_bias, small[0], small[1]], small[8 : 8 + slots].T)
    packed = jnp.concatenate([grad_wqkv.astype(BF16), grad_wout.astype(BF16), small.astype(BF16)], axis=1)
    sums = reduce_rows(grid, packed, ((1664, "cxyz"), (1536, "cyxz")), me)
    small = sums[:, 4 * features :]
    for c, (own_live, _, _, _, _) in enumerate(chunks):
        grads_out.append(input_backward(own_live, inputs, made[c][3], made[c][2], wqkv.T, vectors, c * step))
    return (
        joined(outs, 0).reshape(inputs.shape),
        joined(grads_out, 0).reshape(inputs.shape),
        small[:, 0],
        small[:, 1],
        sums[:, : 3 * features],
        sums[:, 3 * features : 4 * features],
        small[:, 2],
        small[:, 3],
        small[:, 4 : 4 + slots],
        grad_up,
        grad_down,
    )


def solution(mesh):
    rows = P(BOTH, None)
    row = P(BOTH)
    image = P(None, BOTH, None, None)
    up, down = P("expert", None, "dp"), P("expert", "dp", None)
    grid = Grid(mesh.shape["dp"], mesh.shape["expert"])
    return jax.shard_map(
        partial(body, grid),
        mesh=mesh,
        in_specs=(image, P(None, BOTH), row, row, rows, rows, row, row, rows, up, down, image),
        out_specs=(image, image, row, row, rows, rows, row, row, rows, up, down),
        check_vma=False,
    )
```

```python
from functools import partial

import jax
import jax.numpy as jnp
from jax import lax
from jax.experimental import pallas as pl
from jax.experimental.pallas import tpu as pltpu
from jax.sharding import PartitionSpec as P

HEAD_DIM = 64
EPSILON = 1e-06
BOTH = ("dp", "expert")
F32, BF16 = jnp.float32, jnp.bfloat16
LOW = -1e30
LIMIT = 60
PIECES = 4
SMALL = 60
GATHER_CUT = 1664


class Grid:
    def __init__(self, n, m):
        self.n, self.m = n, m
        self.size = {"z": n // 2, "y": 2, "x": m // 2, "c": 2, "e": m}

    def coords(self):
        d, e = lax.axis_index("dp"), lax.axis_index("expert")
        return {"z": d // 2, "y": d % 2, "x": e // 2, "c": e % 2, "e": e}

    def perm(self, axis, k):
        pairs = []
        for source in range(self.n * self.m):
            d, e = divmod(source, self.m)
            p = {"z": d // 2, "y": d % 2, "x": e // 2, "c": e % 2, "e": e}
            q = (p[axis] + k) % self.size[axis]
            if axis == "e":
                target = d * self.m + q
            else:
                p[axis] = q
                target = (p["z"] * 2 + p["y"]) * self.m + p["x"] * 2 + p["c"]
            pairs.append((source, target))
        return pairs

    def send(self, a, axis, k):
        return lax.ppermute(a, BOTH, self.perm(axis, k))

    def by_coordinate(self, me, axis, pieces, at=0):
        s = self.size[axis]
        if s == 2:
            return jnp.stack([jnp.where(me == p, pieces[0], pieces[1]) for p in range(2)], axis=at)
        if s <= 4:
            return jnp.stack([lax.select_n((me - p) % s, *pieces) for p in range(s)], axis=at)
        shape = pieces[0].shape
        out = jnp.zeros(shape[:at] + (s,) + shape[at:], pieces[0].dtype)
        for k in range(s):
            out = lax.dynamic_update_index_in_dim(out, pieces[k], (me - k) % s, at)
        return out

    def block(self, a, axis, me, k, at=0):
        return lax.dynamic_index_in_dim(a, (me[axis] + k) % self.size[axis], at, keepdims=False)


def joined(parts, axis):
    return jnp.concatenate(parts, axis=axis) if len(parts) > 1 else parts[0]


def send_on(grid, items):
    return [[grid.send(a, axis, k) for k in range(1, grid.size[axis])] for a, axis in items]


def gather_steps(grid, me, parts, orders):
    done = [[] for _ in parts]
    for step in range(len(orders[0])):
        axes = [order[step] for order in orders]
        received = yield send_on(grid, list(zip(parts, axes)))
        for i, axis in enumerate(axes):
            at = sum(a in done[i] for a in "zyxc"[: "zyxc".index(axis)])
            done[i].append(axis)
            parts[i] = grid.by_coordinate(me[axis], axis, [parts[i]] + received[i], at)
    return parts


def reduce_steps(grid, me, parts, orders):
    left = ["zyxc"[: len(order)] for order in orders]
    for step in range(len(orders[0])):
        axes = [order[step] for order in orders]
        at = [left[i].index(axis) for i, axis in enumerate(axes)]
        left = [left[i].replace(axis, "") for i, axis in enumerate(axes)]
        blocks = [
            [grid.block(p, axis, me, k, a) for k in range(grid.size[axis])] for p, axis, a in zip(parts, axes, at)
        ]
        received = yield [[grid.send(b, axis, k) for k, b in enumerate(bs) if k] for bs, axis in zip(blocks, axes)]
        parts = [sum([b.astype(F32) for b in r], bs[0].astype(F32)) for bs, r in zip(blocks, received)]
        if step < len(orders[0]) - 1:
            parts = [p.astype(BF16) for p in parts]
    return parts


def swap_step(grid, blocks, axis, sign):
    received = yield [[grid.send(b, axis, sign * k) for k, b in enumerate(blocks) if k]]
    return list(blocks[:1]) + received[0]


def out_steps(grid, rows):
    r = rows.shape[0] // grid.m
    pieces = yield from swap_step(grid, [rows[k * r : (k + 1) * r] for k in range(grid.m)], "e", 1)
    own = jnp.concatenate(pieces, axis=0)
    return (yield from swap_step(grid, [own] * grid.size["z"], "z", 1))


def home_steps(grid, pieces):
    pieces = yield from swap_step(grid, pieces, "z", -1)
    own = sum([p.astype(F32) for p in pieces]).astype(BF16)
    r = own.shape[0] // grid.m
    pieces = yield from swap_step(grid, [own[k * r : (k + 1) * r] for k in range(grid.m)], "e", -1)
    return jnp.concatenate(pieces, axis=0)


def neighbour_steps(grid, arrays):
    received = yield [[grid.send(a, "y", 1) for a in arrays]]
    return received[0]


class Flow:
    def __init__(self, steps):
        self.steps, self.value, self.done = steps, None, False
        self.advance(None)

    def advance(self, received):
        try:
            self.waiting = self.steps.send(received)
        except StopIteration as end:
            self.value, self.done, self.waiting = end.value, True, None


def beside(flows, token, work=None):
    flows = [flow for flow in flows if flow is not None and not flow.done]
    made = work(token) if work else ()
    received, made, token = lax.optimization_barrier(([flow.waiting for flow in flows], made, token))
    for flow, arrays in zip(flows, received):
        flow.advance(arrays)
    return made, token


def dot(a, b, ca=1, cb=0):
    return lax.dot_general(a, b, (((ca,), (cb,)), ((), ())), preferred_element_type=F32)


def padded(v, step):
    return -(-v // step) * step


def standardized(v):
    width = v.shape[-1]
    center = v - jnp.sum(v, axis=-1, keepdims=True) * (1.0 / width)
    root = lax.rsqrt(jnp.sum(center * center, axis=-1, keepdims=True) * (1.0 / width) + EPSILON)
    return center * root, root


def head_masks():
    lane = lax.broadcasted_iota(jnp.int32, (1, 2 * HEAD_DIM), 1)
    return [(lane // HEAD_DIM == h) for h in range(2)]


def routed(logits, tokens, slots):
    row = lax.broadcasted_iota(jnp.int32, logits.shape, 0)
    lane = lax.broadcasted_iota(jnp.int32, logits.shape, 1)
    valid = (row < tokens) & (lane < slots)
    kept = jnp.where(valid, logits, LOW)
    down = jnp.where(valid, jnp.exp(kept - jnp.max(kept, axis=0, keepdims=True)), 0.0)
    down_sum = jnp.sum(down, axis=0, keepdims=True)
    over_tokens = down * (1.0 / jnp.where(down_sum > 0, down_sum, 1.0))
    across = jnp.where(valid, jnp.exp(kept - jnp.max(kept, axis=1, keepdims=True)), 0.0)
    across_sum = jnp.sum(across, axis=1, keepdims=True)
    over_slots = across * (1.0 / jnp.where(across_sum > 0, across_sum, 1.0))
    return over_tokens, over_slots


def longer(v, count):
    return jnp.concatenate([v, jnp.zeros((count - v.shape[0], v.shape[1]), v.dtype)], axis=0)


def forward_kernel(
    tokens, slots, place, live, x_ref, cot_ref, one_ref, two_ref, vec_ref,
    n1_ref, triple_ref, mixed_ref, hidden_ref, logits_ref, slot_ref, pad_ref,
):
    i = pl.program_id(0)
    rows, features = pad_ref.shape
    keys = padded(rows, 128)

    @pl.when(i == 0)
    def _():
        pad_ref[...] = jnp.zeros_like(pad_ref)

    @pl.when(live[i] == 0)
    def _():
        n1_ref[...] = jnp.zeros_like(n1_ref)
        mixed_ref[...] = jnp.zeros_like(mixed_ref)
        for s in range(slots):
            slot_ref[pl.ds(place(live, s, i), 1)] = jnp.zeros((1, slot_ref.shape[1]), F32)

    @pl.when(live[i] != 0)
    def _():
        pad_ref[:tokens] = x_ref[0, 0].astype(F32)
        n1, _ = standardized(pad_ref[...])
        n1_ref[0] = n1.astype(BF16)
        normed = (n1 * vec_ref[0:1] + vec_ref[1:2]).astype(BF16)
        for part in range(3):
            cut = slice(part * features, (part + 1) * features)
            weights = one_ref[:, cut] if part < 2 else two_ref[:, :features]
            triple_ref[0, :, cut] = dot(normed, weights).astype(BF16)
        bias = jnp.where(lax.broadcasted_iota(jnp.int32, (1, keys), 1) < tokens, 0.0, LOW)
        masks = head_masks()
        for low in range(0, features, 128):
            q = triple_ref[0, :, low : low + 128]
            k = longer(triple_ref[0, :, features + low : features + low + 128], keys)
            v = longer(triple_ref[0, :, 2 * features + low : 2 * features + low + 128], keys)
            outs = []
            for mask in masks:
                scores = dot(q * jnp.where(mask, HEAD_DIM**-0.5, 0.0).astype(BF16), k, 1, 1) + bias
                powers = jnp.exp(scores - jnp.max(scores, axis=1, keepdims=True))
                outs.append(dot(powers.astype(BF16), v) * (1.0 / jnp.sum(powers, axis=1, keepdims=True)))
            mixed_ref[0, :, low : low + 128] = jnp.where(masks[0], outs[0], outs[1]).astype(BF16)
        hidden = pad_ref[...] + dot(mixed_ref[0], two_ref[:, features : 2 * features])
        hidden_ref[0] = hidden
        n2, _ = standardized(hidden)
        normed_two = (n2 * vec_ref[2:3] + vec_ref[3:4]).astype(BF16)
        logits = dot(normed_two, two_ref[:, 2 * features :])
        logits_ref[0] = logits
        dispatch, combine = routed(logits, tokens, slots)
        slot_in = dot(dispatch.astype(BF16), normed_two, 0, 0)
        pad_ref[:tokens] = cot_ref[0, 0].astype(F32)
        grad_slot = dot(combine.astype(BF16), pad_ref[...].astype(BF16), 0, 0)
        for s in range(slots):
            slot_ref[pl.ds(place(live, s, i), 1), :features] = slot_in[s : s + 1]
            slot_ref[pl.ds(place(live, s, i), 1), features:] = grad_slot[s : s + 1]


def expert_kernel(pieces, images, *refs):
    rows_in, (up, up_other, down, down_other) = refs[:pieces], refs[pieces : pieces + 4]
    rows_out, (active_ref, slope_ref) = refs[pieces + 4 : 2 * pieces + 4], refs[2 * pieces + 4 :]
    per, features = up.shape[:2]
    both = jnp.concatenate([r[...] for r in rows_in], axis=0)
    rows, grads = both[:, :features], both[:, features:]
    index = lax.broadcasted_iota(jnp.int32, (rows.shape[0], 1), 0)
    total = total_back = 0.0
    for part, (up_ref, down_ref) in enumerate(((up, down), (up_other, down_other))):
        for j in range(per):
            mine = (index // images) % per == j
            pre = dot(rows, up_ref[j])
            phi = 0.5 * (1.0 + lax.erf(pre * (0.5**0.5)))
            density = jnp.exp(pre * pre * -0.5) * (0.5 / jnp.pi) ** 0.5
            active = jnp.where(mine, pre * phi, 0.0).astype(BF16)
            grad = dot(grads, down_ref[j], 1, 1)
            grad = jnp.where(mine, grad * (phi + pre * density), 0.0).astype(BF16)
            active_ref[part, j] = active
            slope_ref[part, j] = grad
            total = total + dot(active, down_ref[j])
            total_back = total_back + dot(grad, up_ref[j], 1, 1)
    size = rows_in[0].shape[0]
    for k, ref in enumerate(rows_out):
        ref[:, :features] = total[k * size : (k + 1) * size].astype(BF16)
        ref[:, features:] = total_back[k * size : (k + 1) * size].astype(BF16)


def expert_grad_kernel(pieces, *refs):
    rows_in, (active_ref, slope_ref) = refs[:pieces], refs[pieces : pieces + 2]
    outs = refs[pieces + 2 :]
    features = outs[0].shape[1]
    both = jnp.concatenate([r[...] for r in rows_in], axis=0)
    rows, grads = both[:, :features].T, both[:, features:]
    for part in range(2):
        up_ref, down_ref = outs[2 * part : 2 * part + 2]
        for j in range(up_ref.shape[0]):
            up_ref[j] = dot(rows, slope_ref[part, j]).astype(up_ref.dtype)
            down_ref[j] = dot(active_ref[part, j], grads, 0, 0).astype(down_ref.dtype)


def backward_kernel(
    tokens, slots, place, live, cot_ref, triple_ref, hidden_ref, logits_ref, home_ref, two_ref, phit_ref, vec_ref,
    out_ref, branch_ref, grad_ref, total_ref, small_ref, pad_ref, gm_ref,
):
    i = pl.program_id(0)
    rows, features = pad_ref.shape
    keys = gm_ref.shape[0]

    @pl.when(i == 0)
    def _():
        pad_ref[...] = jnp.zeros_like(pad_ref)
        gm_ref[...] = jnp.zeros_like(gm_ref)
        total_ref[...] = jnp.zeros_like(total_ref)
        small_ref[...] = jnp.zeros_like(small_ref)

    @pl.when(live[i] == 0)
    def _():
        out_ref[...] = jnp.zeros_like(out_ref)
        branch_ref[...] = jnp.zeros_like(branch_ref)
        grad_ref[...] = jnp.zeros_like(grad_ref)

    @pl.when(live[i] != 0)
    def _():
        hidden = hidden_ref[0]
        n2, root = standardized(hidden)
        gain = vec_ref[2:3]
        normed_two = (n2 * gain + vec_ref[3:4]).astype(BF16)
        over_tokens, over_slots = routed(logits_ref[0], tokens, slots)
        over_tokens, over_slots = over_tokens[:, :slots], over_slots[:, :slots]
        dispatch, combine = over_tokens.astype(BF16), over_slots.astype(BF16)
        home = jnp.concatenate([home_ref[pl.ds(place(live, s, i), 1)] for s in range(slots)], axis=0).astype(BF16)
        slot_out, grad_in = home[:, :features], home[:, features:]
        pad_ref[:tokens] = cot_ref[0, 0].astype(F32)
        cot = pad_ref[...]
        result = hidden + dot(combine, slot_out)
        out_ref[0] = result[:tokens].astype(BF16)
        grad_combine = dot(cot.astype(BF16), slot_out, 1, 1)
        grad_dispatch = dot(normed_two, grad_in, 1, 1)
        grad_logits = over_tokens * (grad_dispatch - jnp.sum(grad_dispatch * over_tokens, axis=0, keepdims=True))
        grad_logits += over_slots * (grad_combine - jnp.sum(grad_combine * over_slots, axis=1, keepdims=True))
        grad_logits = grad_logits.astype(BF16)
        grad_two = dot(dispatch, grad_in) + dot(grad_logits, phit_ref[:slots])
        small_ref[:slots] += dot(grad_logits, normed_two, 0, 0)
        small_ref[slots : slots + 1] += jnp.sum(grad_two * n2, axis=0, keepdims=True)
        small_ref[slots + 1 : slots + 2] += jnp.sum(grad_two, axis=0, keepdims=True)
        u = grad_two * gain
        inner = u - jnp.sum(u, axis=-1, keepdims=True) * (1.0 / features)
        inner = inner - n2 * (jnp.sum(u * n2, axis=-1, keepdims=True) * (1.0 / features))
        branch = (cot + root * inner).astype(BF16)
        branch_ref[0] = branch
        gm_ref[:rows] = dot(branch, two_ref[:, features : 2 * features], 1, 1).astype(BF16)
        valid = lax.broadcasted_iota(jnp.int32, (rows, 1), 0) < tokens
        for low in range(0, features, 128):
            q = longer(triple_ref[0, :, low : low + 128], keys)
            k = triple_ref[0, :, features + low : features + low + 128]
            v = triple_ref[0, :, 2 * features + low : 2 * features + low + 128]
            gm = gm_ref[:, low : low + 128]
            sums = None
            for mask in head_masks():
                one = jnp.where(mask, 1.0, 0.0).astype(BF16)
                scale = jnp.where(mask, HEAD_DIM**-0.5, 0.0).astype(BF16)
                gm_own = gm * one
                q_own = q * scale
                scores = jnp.where(valid, dot(k, q_own, 1, 1), LOW)
                powers = jnp.exp(scores - jnp.max(scores, axis=0, keepdims=True))
                inverse = 1.0 / jnp.sum(powers, axis=0, keepdims=True)
                grad_attention = dot(v, gm_own, 1, 1)
                mean = jnp.sum(grad_attention * powers, axis=0, keepdims=True) * inverse
                attention = powers * inverse
                grad_scores = (attention * (grad_attention - mean)).astype(BF16)
                parts = (dot(grad_scores, k * scale, 0, 0)[:rows], dot(grad_scores, q_own), dot(attention.astype(BF16), gm_own))
                sums = parts if sums is None else tuple(a + b for a, b in zip(sums, parts))
            for part in range(3):
                cut = slice(part * features + low, part * features + low + 128)
                grad_ref[0, :, cut] = sums[part].astype(BF16)
                total_ref[0:1, cut] += jnp.sum(sums[part], axis=0, keepdims=True)


def input_kernel(tokens, live, x_ref, triple_ref, branch_ref, one_ref, two_ref, vec_ref, *refs):
    i, (out_ref, pad_ref) = pl.program_id(0), refs[-2:]
    features = pad_ref.shape[1]

    @pl.when(i == 0)
    def _():
        pad_ref[...] = jnp.zeros_like(pad_ref)

    @pl.when(live[i] == 0)
    def _():
        out_ref[...] = jnp.zeros_like(out_ref)

    @pl.when(live[i] != 0)
    def _():
        pad_ref[:tokens] = x_ref[0, 0].astype(F32)
        n1, root = standardized(pad_ref[...])
        v = dot(triple_ref[0, :, : 2 * features], one_ref[...], 1, 1) + dot(triple_ref[0, :, 2 * features :], two_ref[:, :features], 1, 1)
        v = v * vec_ref[0:1]
        inner = v - jnp.sum(v, axis=-1, keepdims=True) * (1.0 / features)
        inner = inner - n1 * (jnp.sum(v * n1, axis=-1, keepdims=True) * (1.0 / features))
        grad = branch_ref[0].astype(F32) + root * inner
        out_ref[0] = grad[:tokens].astype(BF16)


def weight_grad_kernel(slots, left_ref, left_out_ref, right_ref, right_out_ref, one_ref, two_ref, total_ref, small_ref, columns_ref, out_ref, norm_ref):
    i, (features, tile) = pl.program_id(0), out_ref.shape
    third = features // tile

    @pl.when(i == 0)
    def _():
        norm_ref[...] = jnp.zeros_like(norm_ref)

    def tokens(ref):
        return ref[...].reshape(-1, tile)

    def wide_part(w_ref):
        product = dot(left_ref[...], tokens(right_ref))
        total = total_ref[0:1]
        out_ref[...] = (product * columns_ref[:, 0:1] + columns_ref[:, 1:2] * total).astype(BF16)
        for low in range(0, tile, 128):
            cut = slice(low, low + 128)
            weights = w_ref[:, cut].astype(F32)
            norm_ref[:, :128] += weights * product[:, cut]
            norm_ref[:, 128:] += weights * total[:, cut]

    @pl.when(i < 2 * third)
    def _():
        wide_part(one_ref)

    @pl.when((i >= 2 * third) & (i < 3 * third))
    def _():
        wide_part(two_ref)

    @pl.when((i >= 3 * third) & (i < 4 * third))
    def _():
        out_ref[...] = dot(left_out_ref[...], tokens(right_out_ref)).astype(BF16)

    @pl.when(i == 4 * third)
    def _():
        out_ref[:, :128] = small_ref[...].astype(BF16)
        lane = lax.broadcasted_iota(jnp.int32, (features, tile - 128), 1)
        gain = jnp.sum(norm_ref[:, :128], axis=1, keepdims=True)
        bias = jnp.sum(norm_ref[:, 128:], axis=1, keepdims=True)
        out_ref[:, 128:] = jnp.where(lane == 0, gain, jnp.where(lane == 1, bias, 0.0)).astype(BF16)


def own(*shape, low=0):
    return pl.BlockSpec((1,) + shape, lambda i, live: (i + low,) + (0,) * len(shape))


def fixed(*shape):
    return pl.BlockSpec(shape, lambda i, *live: (0,) * len(shape), pipeline_mode=pl.Buffered(1))


def shaped(*shape, dtype=BF16):
    return jax.ShapeDtypeStruct(shape, dtype)


def params(mib, axes=1):
    return pltpu.CompilerParams(vmem_limit_bytes=mib * 1024 * 1024, dimension_semantics=("arbitrary",) * axes)


def by_image(kernel, images, in_specs, out_specs, out_shape, scratch, flops, mib):
    return pl.pallas_call(
        kernel,
        grid_spec=pltpu.PrefetchScalarGridSpec(
            num_scalar_prefetch=1, grid=(images,), in_specs=in_specs, out_specs=out_specs, scratch_shapes=scratch
        ),
        out_shape=out_shape,
        compiler_params=params(mib),
        cost_estimate=pl.CostEstimate(flops=flops, bytes_accessed=flops // 1000, transcendentals=0),
    )


class Mixer:
    def __init__(self, grid, inputs, cotangent, slots, live, expert):
        self.inputs, self.cotangent, self.slots = inputs, cotangent, slots
        self.live = jnp.concatenate([live, expert[None]])
        self.owners, self.per = grid.m, slots // grid.m
        self.batches, self.capacity, self.tokens, self.features = inputs.shape
        self.images = self.batches * self.capacity
        self.rows, self.keys = padded(self.tokens, 16), padded(self.tokens, 128)
        self.pad = pltpu.VMEM((self.rows, self.features), F32)
        self.flops = self.rows * self.features * self.features * 8

    def place(self, live, s, i):
        owner = lax.rem(s // self.per + self.owners - live[self.images], self.owners)
        return (owner * self.per + s % self.per) * self.images + i

    def image(self, low):
        return pl.BlockSpec((1, 1, self.tokens, self.features), lambda i, live: ((i + low) // self.capacity, (i + low) % self.capacity, 0, 0))

    def made(self, low=0):
        return pl.BlockSpec((1, self.tokens, self.features), lambda i, live: (i + low, 0, 0))

    def forward(self, one, two, vec):
        n, r, f = self.images, self.rows, self.features
        return by_image(
            partial(forward_kernel, self.tokens, self.slots, self.place), n,
            [self.image(0), self.image(0), fixed(*one.shape), fixed(*two.shape), fixed(*vec.shape)],
            [own(r, f), own(r, 3 * f), own(r, f), own(r, f), own(r, 128), fixed(self.slots * n, 2 * f)],
            [shaped(n, r, f), shaped(n, r, 3 * f), shaped(n, r, f), shaped(n, r, f, dtype=F32), shaped(n, r, 128, dtype=F32), shaped(self.slots * n, 2 * f, dtype=F32)],
            [self.pad], 3 * n * self.flops, LIMIT,
        )(self.live, self.inputs, self.cotangent, one, two, vec)

    def backward(self, triple, hidden, logits, home, two, phit, vec):
        n, r, f = self.images, self.rows, self.features
        small = padded(self.slots + 2, 8)
        return by_image(
            partial(backward_kernel, self.tokens, self.slots, self.place), n,
            [self.image(0), own(r, 3 * f), own(r, f), own(r, 128), fixed(self.slots * n, 2 * f), fixed(*two.shape), fixed(*phit.shape), fixed(*vec.shape)],
            [self.made(), own(r, f), own(r, 3 * f), fixed(8, 3 * f), fixed(small, f)],
            [shaped(n, self.tokens, f), shaped(n, r, f), shaped(n, r, 3 * f), shaped(8, 3 * f, dtype=F32), shaped(small, f, dtype=F32)],
            [self.pad, pltpu.VMEM((self.keys, f), BF16)], 3 * n * self.flops, LIMIT,
        )(self.live, self.cotangent, triple, hidden, logits, home, two, phit, vec)

    def input_back(self, token, low, high, triple, branch, one, two, vec, into):
        r, f = self.rows, self.features
        return pl.pallas_call(
            partial(input_kernel, self.tokens),
            grid_spec=pltpu.PrefetchScalarGridSpec(
                num_scalar_prefetch=1,
                grid=(high - low,),
                in_specs=[self.image(low), own(r, 3 * f, low=low), own(r, f, low=low), fixed(*one.shape), fixed(*two.shape), fixed(*vec.shape)]
                + [pl.BlockSpec(memory_space=pl.ANY)] * (into is not None),
                out_specs=self.made(low),
                scratch_shapes=[self.pad],
            ),
            out_shape=shaped(self.images, self.tokens, f),
            input_output_aliases={} if into is None else {7: 0},
            compiler_params=params(LIMIT),
        )(token[low:high], self.inputs, triple, branch, one, two, vec, *([] if into is None else [into]))

    def turned(self, array):
        return array.reshape(-1, array.shape[-1]).T

    def weight_grads(self, left, left_out, right, right_out, one, two, total, small, columns, tile=256):
        f, third = self.features, self.features // tile
        def at(array, first, count):
            lead = array.shape[:-1]
            return pl.BlockSpec(lead + (tile,), lambda i: (0,) * len(lead) + (jnp.clip(i - first, 0, count - 1),))
        return pl.pallas_call(
            partial(weight_grad_kernel, self.slots),
            grid=(4 * third + 1,),
            in_specs=[fixed(*left.shape), fixed(*left_out.shape), at(right, 0, 3 * third), at(right_out, 3 * third, third),
                      at(one, 0, 2 * third), at(two, 2 * third, third), at(total, 0, 3 * third), fixed(*small.shape), fixed(*columns.shape)],
            out_specs=pl.BlockSpec((f, tile), lambda i: (0, i)),
            out_shape=shaped(f, 4 * f + tile),
            scratch_shapes=[pltpu.VMEM((f, 256), F32)],
            compiler_params=params(LIMIT),
        )(left, left_out, right, right_out, one, two, total, small, columns)


def expert_forward(pieces, weights, images):
    per, _, hidden = weights[0].shape
    size, count = pieces[0].shape[0], len(pieces)
    kept = shaped(2, per, size * count, hidden)
    made = pl.pallas_call(
        partial(expert_kernel, count, images),
        out_shape=[shaped(*p.shape) for p in pieces] + [kept, kept],
        compiler_params=params(LIMIT, 0),
    )(*pieces, *weights)
    return made[:count], made[count:]


def expert_grads(pieces, kept, up, down):
    return pl.pallas_call(
        partial(expert_grad_kernel, len(pieces)),
        out_shape=[shaped(*up.shape, dtype=F32), shaped(*down.shape, dtype=F32), shaped(*up.shape), shaped(*down.shape)],
        compiler_params=params(LIMIT, 0),
    )(*pieces, *kept)


def wide(a, width=128):
    return jnp.pad(a, ((0, 0), (0, width - a.shape[1])))


def body(grid, inputs, counts, ln1_gain, ln1_bias, w_qkv, w_out, ln2_gain, ln2_bias, phi, w_up, w_down, cotangent):
    me = grid.coords()
    batches, capacity, tokens, features = inputs.shape
    images = batches * capacity
    slots = phi.shape[1]
    per = slots // grid.m
    token = (jnp.arange(capacity)[None, :] < counts).astype(jnp.int32).reshape(-1)
    mixer = Mixer(grid, inputs, cotangent, slots, token, me["e"])
    vectors = jnp.stack([ln1_gain, ln1_bias, ln2_gain, ln2_bias], axis=1)
    ends = jnp.concatenate([w_qkv[:, 2 * features :], w_out, wide(jnp.concatenate([phi, vectors], axis=1))], axis=1)
    flow = Flow(gather_steps(grid, me, [w_qkv[:, : 2 * features], ends], ("zxyc", "zyxc")))
    for _ in range(3):
        _, token = beside([flow], token)
    other = Flow(neighbour_steps(grid, lax.optimization_barrier(([w_up, w_down], token))[0]))
    _, token = beside([flow], token)
    one, two = (a.reshape(-1, a.shape[-1]) for a in flow.value)
    columns = two[:, 2 * features : 2 * features + padded(slots + 4, 16)].astype(F32)
    turned = columns.T
    vec = jnp.pad(turned[slots : slots + 4], ((0, 4), (0, 0)))

    made, token = beside([other], token, lambda token: mixer.forward(one, two, vec))
    n1, triple, mixed, hidden, logits, slot = made
    flow = Flow(out_steps(grid, slot.astype(BF16)))
    _, token = beside([flow], token)
    lefts, token = beside([flow], token, lambda token: (mixer.turned(n1), mixer.turned(mixed)))
    pieces = flow.value
    back, kept = expert_forward(pieces, [w_up, other.value[0], w_down, other.value[1]], images)
    flow = Flow(home_steps(grid, back))
    made, token = beside([flow], token, lambda token: expert_grads(pieces, kept, w_up, w_down))
    grad_up, grad_down, *others = made
    _, token = beside([flow], token)
    other = Flow(neighbour_steps(grid, others))
    made, token = beside(
        [other], token, lambda token: mixer.backward(triple, hidden, logits, flow.value.astype(F32), two, turned.astype(BF16), vec)
    )
    outs, branch, grad_triple, total, small = made
    packed = mixer.weight_grads(
        *lefts, grad_triple, branch, one, two, total, wide(small.T), columns[:, slots : slots + 2]
    )
    grad_up, grad_down = grad_up + other.value[0].astype(F32), grad_down + other.value[1].astype(F32)
    cut = padded(packed.shape[1] // 2, 128)
    packed = packed.reshape(grid.size["z"], 2, grid.size["x"], 2, -1, packed.shape[1])
    flow = Flow(reduce_steps(grid, me, [packed[..., :cut], packed[..., cut:]], ("cxyz", "cyxz")))
    grad_in, step = None, images // PIECES
    for low in range(0, images, step):
        grad_in, token = beside(
            [flow], token, lambda token: mixer.input_back(token, low, low + step, grad_triple, branch, one, two, vec, grad_in)
        )
    while not flow.done:
        _, token = beside([flow], token)
    sums = jnp.concatenate(flow.value, axis=-1)
    small = sums[:, 4 * features :]
    return (
        outs.reshape(inputs.shape),
        grad_in.reshape(inputs.shape),
        small[:, 128],
        small[:, 129],
        sums[:, : 3 * features],
        sums[:, 3 * features : 4 * features],
        small[:, slots],
        small[:, slots + 1],
        small[:, :slots],
        grad_up,
        grad_down,
    )


def solution(mesh):
    rows = P(BOTH, None)
    row = P(BOTH)
    image = P(None, BOTH, None, None)
    up, down = P("expert", None, "dp"), P("expert", "dp", None)
    grid = Grid(mesh.shape["dp"], mesh.shape["expert"])
    return jax.shard_map(
        partial(body, grid),
        mesh=mesh,
        in_specs=(image, P(None, BOTH), row, row, rows, rows, row, row, rows, up, down, image),
        out_specs=(image, image, row, row, rows, rows, row, row, rows, up, down),
        check_vma=False,
    )
```

```python
from functools import partial

import jax
import jax.numpy as jnp
from jax import lax
from jax.experimental import pallas as pl
from jax.experimental.pallas import tpu as pltpu
from jax.sharding import PartitionSpec as P

HEAD_DIM = 64
EPSILON = 1e-06
BOTH = ("dp", "expert")
F32, BF16 = jnp.float32, jnp.bfloat16
LOW = -1e30
LIMIT = 52
SHARES = (2, 6, 4)
SMALL = 52
GATHER_CUT = 1664


class Grid:
    def __init__(self, n, m):
        self.n, self.m = n, m
        self.size = {"z": n // 2, "y": 2, "x": m // 2, "c": 2, "e": m}

    def coords(self):
        d, e = lax.axis_index("dp"), lax.axis_index("expert")
        return {"z": d // 2, "y": d % 2, "x": e // 2, "c": e % 2, "e": e}

    def perm(self, axis, k):
        pairs = []
        for source in range(self.n * self.m):
            d, e = divmod(source, self.m)
            p = {"z": d // 2, "y": d % 2, "x": e // 2, "c": e % 2, "e": e}
            q = (p[axis] + k) % self.size[axis]
            if axis == "e":
                target = d * self.m + q
            else:
                p[axis] = q
                target = (p["z"] * 2 + p["y"]) * self.m + p["x"] * 2 + p["c"]
            pairs.append((source, target))
        return pairs

    def send(self, a, axis, k):
        return lax.ppermute(a, BOTH, self.perm(axis, k))

    def by_coordinate(self, me, axis, pieces, at=0):
        s = self.size[axis]
        if s == 2:
            return jnp.stack([jnp.where(me == p, pieces[0], pieces[1]) for p in range(2)], axis=at)
        if s <= 4:
            return jnp.stack([lax.select_n((me - p) % s, *pieces) for p in range(s)], axis=at)
        shape = pieces[0].shape
        out = jnp.zeros(shape[:at] + (s,) + shape[at:], pieces[0].dtype)
        for k in range(s):
            out = lax.dynamic_update_index_in_dim(out, pieces[k], (me - k) % s, at)
        return out

    def block(self, a, axis, me, k, at=0):
        return lax.dynamic_index_in_dim(a, (me[axis] + k) % self.size[axis], at, keepdims=False)


def joined(parts, axis):
    return jnp.concatenate(parts, axis=axis) if len(parts) > 1 else parts[0]


def send_on(grid, items):
    return [[grid.send(a, axis, k) for k in range(1, grid.size[axis])] for a, axis in items]


def gather_steps(grid, me, a, cut):
    got = yield send_on(grid, [(a, "z")])
    a = grid.by_coordinate(me["z"], "z", [a] + got[0])
    parts = [a[..., :cut], a[..., cut:]]
    for axes, at in (("yx", (1, 1)), ("xy", (2, 1)), ("cc", (3, 3))):
        got = yield send_on(grid, list(zip(parts, axes)))
        parts = [grid.by_coordinate(me[x], x, [p] + r, i) for p, r, x, i in zip(parts, got, axes, at)]
    return [p.reshape(-1, p.shape[-1]) for p in parts]


def reduce_steps(grid, me, a, cut):
    s = grid.size
    a = a.reshape(s["z"], 2, s["x"], 2, -1, a.shape[1])
    got = yield [[grid.send(grid.block(a, "c", me, 1, 3), "c", 1)]]
    a = (grid.block(a, "c", me, 0, 3).astype(F32) + got[0][0].astype(F32)).astype(BF16)
    parts = [a[..., :cut], a[..., cut:]]
    for axes, at in (("xy", (2, 1)), ("yx", (1, 1))):
        blocks = [[grid.block(p, x, me, k, i) for k in range(s[x])] for p, x, i in zip(parts, axes, at)]
        got = yield [[grid.send(b, x, k) for k, b in enumerate(bs) if k] for bs, x in zip(blocks, axes)]
        parts = [sum([b.astype(F32) for b in r], bs[0].astype(F32)).astype(BF16) for bs, r in zip(blocks, got)]
    a = jnp.concatenate(parts, axis=-1)
    blocks = [grid.block(a, "z", me, k) for k in range(s["z"])]
    got = yield [[grid.send(b, "z", k) for k, b in enumerate(blocks) if k]]
    return sum([b.astype(F32) for b in got[0]], blocks[0].astype(F32))


def swap_step(grid, blocks, axis, sign):
    received = yield [[grid.send(b, axis, sign * k) for k, b in enumerate(blocks) if k]]
    return list(blocks[:1]) + received[0]


def out_steps(grid, rows):
    r = rows.shape[0] // grid.m
    pieces = yield from swap_step(grid, [rows[k * r : (k + 1) * r] for k in range(grid.m)], "e", 1)
    own = jnp.concatenate(pieces, axis=0)
    return (yield from swap_step(grid, [own] * grid.size["z"], "z", 1))


def home_steps(grid, pieces):
    pieces = yield from swap_step(grid, pieces, "z", -1)
    own = sum([p.astype(F32) for p in pieces]).astype(BF16)
    r = own.shape[0] // grid.m
    pieces = yield from swap_step(grid, [own[k * r : (k + 1) * r] for k in range(grid.m)], "e", -1)
    return jnp.concatenate(pieces, axis=0)


def neighbour_steps(grid, arrays):
    received = yield [[grid.send(a, "y", 1) for a in arrays]]
    return received[0]


class Flow:
    def __init__(self, steps):
        self.steps, self.value, self.done = steps, None, False
        self.advance(None)

    def advance(self, received):
        try:
            self.waiting = self.steps.send(received)
        except StopIteration as end:
            self.value, self.done, self.waiting = end.value, True, None


def beside(flows, token, work=None):
    flows = [flow for flow in flows if flow is not None and not flow.done]
    made = work(token) if work else ()
    received, made, token = lax.optimization_barrier(([flow.waiting for flow in flows], made, token))
    for flow, arrays in zip(flows, received):
        flow.advance(arrays)
    return made, token


def dot(a, b, ca=1, cb=0):
    return lax.dot_general(a, b, (((ca,), (cb,)), ((), ())), preferred_element_type=F32)


def padded(v, step):
    return -(-v // step) * step


def standardized(v):
    width = v.shape[-1]
    center = v - jnp.sum(v, axis=-1, keepdims=True) * (1.0 / width)
    root = lax.rsqrt(jnp.sum(center * center, axis=-1, keepdims=True) * (1.0 / width) + EPSILON)
    return center * root, root


def lanes_of(head, width):
    return lax.broadcasted_iota(jnp.int32, (1, width), 1) // HEAD_DIM == head


def by_head(v, scale):
    width = v.shape[1]
    return jnp.concatenate([v * jnp.where(lanes_of(h, width), scale, 0.0).astype(BF16) for h in range(width // HEAD_DIM)], axis=0)


def own_columns(v):
    half = v.shape[0] // 2
    return jnp.where(lanes_of(0, v.shape[1]), v[:half], v[half:])


def routed(logits, tokens, slots):
    row = lax.broadcasted_iota(jnp.int32, logits.shape, 0)
    lane = lax.broadcasted_iota(jnp.int32, logits.shape, 1)
    valid = (row < tokens) & (lane < slots)
    kept = jnp.where(valid, logits, LOW)
    down = jnp.where(valid, jnp.exp(kept - jnp.max(kept, axis=0, keepdims=True)), 0.0)
    down_sum = jnp.sum(down, axis=0, keepdims=True)
    over_tokens = down * (1.0 / jnp.where(down_sum > 0, down_sum, 1.0))
    across = jnp.where(valid, jnp.exp(kept - jnp.max(kept, axis=1, keepdims=True)), 0.0)
    across_sum = jnp.sum(across, axis=1, keepdims=True)
    over_slots = across * (1.0 / jnp.where(across_sum > 0, across_sum, 1.0))
    return over_tokens, over_slots


def longer(v, count):
    return jnp.concatenate([v, jnp.zeros((count - v.shape[0], v.shape[1]), v.dtype)], axis=0)


def pad_kernel(tokens, cot_ref, out_ref):
    rows = out_ref.shape[1]
    for k in range(cot_ref.shape[1]):
        out_ref[k] = jnp.zeros((rows, out_ref.shape[2]), BF16)
        out_ref[k, :tokens] = cot_ref[0, k]


def standardize_kernel(tokens, x_ref, n1_ref, root_ref, pad_ref):
    @pl.when(pl.program_id(0) == 0)
    def _():
        pad_ref[...] = jnp.zeros_like(pad_ref)

    for k in range(x_ref.shape[1]):
        pad_ref[k, :tokens] = x_ref[0, k].astype(F32)
        n1, root = standardized(pad_ref[k])
        n1_ref[k] = n1.astype(BF16)
        root_ref[k] = jnp.broadcast_to(root, root_ref.shape[1:])


def forward_kernel(
    tokens, slots, place, live, x_ref, n1_ref, cot_ref, one_ref, two_ref, vec_ref,
    triple_ref, mixed_ref, hidden_ref, logits_ref, slot_ref, pad_ref,
):
    i = pl.program_id(0)
    rows, features = pad_ref.shape
    keys = padded(rows, 128)

    @pl.when(i == 0)
    def _():
        pad_ref[...] = jnp.zeros_like(pad_ref)

    @pl.when(live[i] == 0)
    def _():
        mixed_ref[...] = jnp.zeros_like(mixed_ref)
        for s in range(slots):
            slot_ref[pl.ds(place(live, s, i), 1)] = jnp.zeros((1, slot_ref.shape[1]), F32)

    @pl.when(live[i] != 0)
    def _():
        pad_ref[:tokens] = x_ref[0, 0].astype(F32)
        normed = (n1_ref[0].astype(F32) * vec_ref[0:1] + vec_ref[1:2]).astype(BF16)
        for part in range(3):
            cut = slice(part * features, (part + 1) * features)
            weights = one_ref[:, cut] if part < 2 else two_ref[:, :features]
            triple_ref[0, :, cut] = dot(normed, weights).astype(BF16)
        bias = jnp.where(lax.broadcasted_iota(jnp.int32, (1, keys), 1) < tokens, 0.0, LOW)
        for low in range(0, features, 128):
            q = triple_ref[0, :, low : low + 128]
            k = longer(triple_ref[0, :, features + low : features + low + 128], keys)
            v = longer(triple_ref[0, :, 2 * features + low : 2 * features + low + 128], keys)
            scores = dot(by_head(q, HEAD_DIM**-0.5), k, 1, 1) + bias
            powers = jnp.exp(scores - jnp.max(scores, axis=1, keepdims=True))
            total = dot(powers.astype(BF16), v) * (1.0 / jnp.sum(powers, axis=1, keepdims=True))
            mixed_ref[0, :, low : low + 128] = own_columns(total).astype(BF16)
        hidden = pad_ref[...] + dot(mixed_ref[0], two_ref[:, features : 2 * features])
        hidden_ref[0] = hidden
        n2, _ = standardized(hidden)
        normed_two = (n2 * vec_ref[2:3] + vec_ref[3:4]).astype(BF16)
        logits = dot(normed_two, two_ref[:, 2 * features :])
        logits_ref[0] = logits
        dispatch, combine = routed(logits, tokens, slots)
        slot_in = dot(dispatch.astype(BF16), normed_two, 0, 0)
        grad_slot = dot(combine.astype(BF16), cot_ref[0], 0, 0)
        for s in range(slots):
            slot_ref[pl.ds(place(live, s, i), 1), :features] = slot_in[s : s + 1]
            slot_ref[pl.ds(place(live, s, i), 1), features:] = grad_slot[s : s + 1]


def expert_kernel(pieces, images, *refs):
    rows_in, (up, up_other, down, down_other) = refs[:pieces], refs[pieces : pieces + 4]
    rows_out, (active_ref, slope_ref) = refs[pieces + 4 : 2 * pieces + 4], refs[2 * pieces + 4 :]
    per, features = up.shape[:2]
    both = jnp.concatenate([r[...] for r in rows_in], axis=0)
    rows, grads = both[:, :features], both[:, features:]
    index = lax.broadcasted_iota(jnp.int32, (rows.shape[0], 1), 0)
    total = total_back = 0.0
    for part, (up_ref, down_ref) in enumerate(((up, down), (up_other, down_other))):
        for j in range(per):
            mine = (index // images) % per == j
            pre = dot(rows, up_ref[j])
            phi = 0.5 * (1.0 + lax.erf(pre * (0.5**0.5)))
            density = jnp.exp(pre * pre * -0.5) * (0.5 / jnp.pi) ** 0.5
            active = jnp.where(mine, pre * phi, 0.0).astype(BF16)
            grad = dot(grads, down_ref[j], 1, 1)
            grad = jnp.where(mine, grad * (phi + pre * density), 0.0).astype(BF16)
            active_ref[part, j] = active
            slope_ref[part, j] = grad
            total = total + dot(active, down_ref[j])
            total_back = total_back + dot(grad, up_ref[j], 1, 1)
    size = rows_in[0].shape[0]
    for k, ref in enumerate(rows_out):
        ref[:, :features] = total[k * size : (k + 1) * size].astype(BF16)
        ref[:, features:] = total_back[k * size : (k + 1) * size].astype(BF16)


def expert_grad_kernel(pieces, *refs):
    rows_in, (active_ref, slope_ref) = refs[:pieces], refs[pieces : pieces + 2]
    outs = refs[pieces + 2 :]
    features = outs[0].shape[1]
    both = jnp.concatenate([r[...] for r in rows_in], axis=0)
    rows, grads = both[:, :features].T, both[:, features:]
    for part in range(2):
        up_ref, down_ref = outs[2 * part : 2 * part + 2]
        for j in range(up_ref.shape[0]):
            up_ref[j] = dot(rows, slope_ref[part, j]).astype(up_ref.dtype)
            down_ref[j] = dot(active_ref[part, j], grads, 0, 0).astype(down_ref.dtype)


def backward_kernel(
    tokens, slots, place, live, cot_ref, triple_ref, hidden_ref, logits_ref, home_ref, two_ref, phit_ref, vec_ref,
    out_ref, branch_ref, grad_ref, total_ref, small_ref, gm_ref,
):
    i = pl.program_id(0)
    rows, features = hidden_ref.shape[1:]
    keys = gm_ref.shape[0]

    @pl.when(i == 0)
    def _():
        gm_ref[...] = jnp.zeros_like(gm_ref)
        total_ref[...] = jnp.zeros_like(total_ref)
        small_ref[...] = jnp.zeros_like(small_ref)

    @pl.when(live[i] == 0)
    def _():
        out_ref[...] = jnp.zeros_like(out_ref)
        branch_ref[...] = jnp.zeros_like(branch_ref)
        grad_ref[...] = jnp.zeros_like(grad_ref)

    @pl.when(live[i] != 0)
    def _():
        hidden = hidden_ref[0]
        n2, root = standardized(hidden)
        gain = vec_ref[2:3]
        normed_two = (n2 * gain + vec_ref[3:4]).astype(BF16)
        over_tokens, over_slots = routed(logits_ref[0], tokens, slots)
        over_tokens, over_slots = over_tokens[:, :slots], over_slots[:, :slots]
        dispatch, combine = over_tokens.astype(BF16), over_slots.astype(BF16)
        home = jnp.concatenate([home_ref[pl.ds(place(live, s, i), 1)] for s in range(slots)], axis=0).astype(BF16)
        slot_out, grad_in = home[:, :features], home[:, features:]
        cot = cot_ref[0].astype(F32)
        result = hidden + dot(combine, slot_out)
        out_ref[0] = result[:tokens].astype(BF16)
        grad_combine = dot(cot_ref[0], slot_out, 1, 1)
        grad_dispatch = dot(normed_two, grad_in, 1, 1)
        grad_logits = over_tokens * (grad_dispatch - jnp.sum(grad_dispatch * over_tokens, axis=0, keepdims=True))
        grad_logits += over_slots * (grad_combine - jnp.sum(grad_combine * over_slots, axis=1, keepdims=True))
        grad_logits = grad_logits.astype(BF16)
        grad_two = dot(dispatch, grad_in) + dot(grad_logits, phit_ref[:slots])
        small_ref[:slots] += dot(grad_logits, normed_two, 0, 0)
        small_ref[slots : slots + 1] += jnp.sum(grad_two * n2, axis=0, keepdims=True)
        small_ref[slots + 1 : slots + 2] += jnp.sum(grad_two, axis=0, keepdims=True)
        u = grad_two * gain
        inner = u - jnp.sum(u, axis=-1, keepdims=True) * (1.0 / features)
        inner = inner - n2 * (jnp.sum(u * n2, axis=-1, keepdims=True) * (1.0 / features))
        branch = (cot + root * inner).astype(BF16)
        branch_ref[0] = branch
        gm_ref[:rows] = dot(branch, two_ref[:, features : 2 * features], 1, 1).astype(BF16)
        valid = lax.broadcasted_iota(jnp.int32, (rows, 1), 0) < tokens
        for low in range(0, features, 256):
            q = longer(triple_ref[0, :, low : low + 256], keys)
            k = triple_ref[0, :, features + low : features + low + 256]
            v = triple_ref[0, :, 2 * features + low : 2 * features + low + 256]
            gm = gm_ref[:, low : low + 256]
            scores_all = dot(by_head(k, HEAD_DIM**-0.5), q, 1, 1)
            grad_all = dot(by_head(v, 1.0), gm, 1, 1)
            for pair in range(2):
                attention, grad_scores = [], []
                for head in (2 * pair, 2 * pair + 1):
                    cut = slice(head * rows, (head + 1) * rows)
                    scores = jnp.where(valid, scores_all[cut], LOW)
                    powers = jnp.exp(scores - jnp.max(scores, axis=0, keepdims=True))
                    inverse = 1.0 / jnp.sum(powers, axis=0, keepdims=True)
                    mean = jnp.sum(grad_all[cut] * powers, axis=0, keepdims=True) * inverse
                    powers = powers * inverse
                    attention.append(powers.astype(BF16))
                    grad_scores.append((powers * (grad_all[cut] - mean)).astype(BF16))
                own = slice(pair * 128, (pair + 1) * 128)
                grads = (
                    own_columns(dot(jnp.concatenate([g.T for g in grad_scores], axis=0), k[:, own]))[:rows] * HEAD_DIM**-0.5,
                    own_columns(dot(jnp.concatenate(grad_scores, axis=0), q[:, own])) * HEAD_DIM**-0.5,
                    own_columns(dot(jnp.concatenate(attention, axis=0), gm[:, own])),
                )
                for part, grad in enumerate(grads):
                    cut = slice(part * features + low + pair * 128, part * features + low + (pair + 1) * 128)
                    grad_ref[0, :, cut] = grad.astype(BF16)
                    total_ref[0:1, cut] += jnp.sum(grad, axis=0, keepdims=True)


def input_kernel(tokens, triple_ref, n1_ref, root_ref, branch_ref, one_ref, two_ref, vec_ref, *refs):
    out_ref = refs[-1]
    count, rows, features = branch_ref.shape
    flat = lambda a: a.reshape(count * rows, a.shape[-1])
    triple, n1, root = flat(triple_ref[...]), flat(n1_ref[...]).astype(F32), flat(root_ref[...])[:, :1]
    v = dot(triple[:, : 2 * features], one_ref[...], 1, 1) + dot(triple[:, 2 * features :], two_ref[...], 1, 1)
    v = v * vec_ref[0:1]
    inner = v - jnp.sum(v, axis=-1, keepdims=True) * (1.0 / features)
    inner = inner - n1 * (jnp.sum(v * n1, axis=-1, keepdims=True) * (1.0 / features))
    grad = flat(branch_ref[...]).astype(F32) + root * inner
    for k in range(count):
        out_ref[k] = grad[k * rows : k * rows + tokens].astype(BF16)


def weight_grad_kernel(slots, left_ref, left_out_ref, right_ref, right_out_ref, one_ref, two_ref, total_ref, small_ref, columns_ref, out_ref, norm_ref):
    i, (features, tile) = pl.program_id(0), out_ref.shape
    third = features // tile

    @pl.when(i == 0)
    def _():
        norm_ref[...] = jnp.zeros_like(norm_ref)

    def tokens(ref):
        return ref[...].reshape(-1, tile)

    def wide_part(w_ref):
        product = dot(left_ref[...], tokens(right_ref))
        total = total_ref[0:1]
        out_ref[...] = (product * columns_ref[:, 0:1] + columns_ref[:, 1:2] * total).astype(BF16)
        for low in range(0, tile, 128):
            cut = slice(low, low + 128)
            weights = w_ref[:, cut].astype(F32)
            norm_ref[:, :128] += weights * product[:, cut]
            norm_ref[:, 128:] += weights * total[:, cut]

    @pl.when(i < 2 * third)
    def _():
        wide_part(one_ref)

    @pl.when((i >= 2 * third) & (i < 3 * third))
    def _():
        wide_part(two_ref)

    @pl.when((i >= 3 * third) & (i < 4 * third))
    def _():
        out_ref[...] = dot(left_out_ref[...], tokens(right_out_ref)).astype(BF16)

    @pl.when(i == 4 * third)
    def _():
        lane = lax.broadcasted_iota(jnp.int32, (features, 128), 1)
        gain = jnp.sum(norm_ref[:, :128], axis=1, keepdims=True)
        bias = jnp.sum(norm_ref[:, 128:], axis=1, keepdims=True)
        narrow = jnp.where(lane == slots + 2, gain, jnp.where(lane == slots + 3, bias, small_ref[...]))
        out_ref[:, :128] = narrow.astype(BF16)


def own(*shape, low=0):
    return pl.BlockSpec((1,) + shape, lambda i, live: (i + low,) + (0,) * len(shape))


def fixed(*shape):
    return pl.BlockSpec(shape, lambda i, *live: (0,) * len(shape), pipeline_mode=pl.Buffered(1))


def shaped(*shape, dtype=BF16):
    return jax.ShapeDtypeStruct(shape, dtype)


def params(mib, axes=1):
    return pltpu.CompilerParams(vmem_limit_bytes=mib * 1024 * 1024, dimension_semantics=("arbitrary",) * axes)


def by_image(kernel, images, in_specs, out_specs, out_shape, scratch, flops, mib):
    return pl.pallas_call(
        kernel,
        grid_spec=pltpu.PrefetchScalarGridSpec(
            num_scalar_prefetch=1, grid=(images,), in_specs=in_specs, out_specs=out_specs, scratch_shapes=scratch
        ),
        out_shape=out_shape,
        compiler_params=params(mib),
        cost_estimate=pl.CostEstimate(flops=flops, bytes_accessed=flops // 1000, transcendentals=0),
    )


class Mixer:
    def __init__(self, grid, inputs, slots, live, expert):
        self.inputs, self.slots = inputs, slots
        self.live = jnp.concatenate([live, expert[None]])
        self.owners, self.per = grid.m, slots // grid.m
        self.batches, self.capacity, self.tokens, self.features = inputs.shape
        self.images = self.batches * self.capacity
        self.rows, self.keys = padded(self.tokens, 16), padded(self.tokens, 128)
        self.pad = pltpu.VMEM((self.rows, self.features), F32)
        self.flops = self.rows * self.features * self.features * 8

    def place(self, live, s, i):
        owner = lax.rem(s // self.per + self.owners - live[self.images], self.owners)
        return (owner * self.per + s % self.per) * self.images + i

    def image(self, low):
        return pl.BlockSpec((1, 1, self.tokens, self.features), lambda i, live: ((i + low) // self.capacity, (i + low) % self.capacity, 0, 0))

    def made(self, low=0):
        return pl.BlockSpec((1, self.tokens, self.features), lambda i, live: (i + low, 0, 0))

    def padded_cotangent(self, cotangent):
        n, c, r, f = self.images, self.capacity, self.rows, self.features
        return pl.pallas_call(
            partial(pad_kernel, self.tokens),
            grid=(self.batches,),
            in_specs=[pl.BlockSpec((1, c, self.tokens, f), lambda i: (i, 0, 0, 0))],
            out_specs=pl.BlockSpec((c, r, f), lambda i: (i, 0, 0)),
            out_shape=shaped(n, r, f),
            compiler_params=params(LIMIT),
        )(cotangent)

    def standardize(self):
        n, c, r, f = self.images, self.capacity, self.rows, self.features
        group = lambda *shape: pl.BlockSpec((c,) + shape, lambda i: (i,) + (0,) * len(shape))
        return pl.pallas_call(
            partial(standardize_kernel, self.tokens),
            grid=(self.batches,),
            in_specs=[pl.BlockSpec((1, c, self.tokens, f), lambda i: (i, 0, 0, 0))],
            out_specs=[group(r, f), group(r, 128)],
            out_shape=[shaped(n, r, f), shaped(n, r, 128, dtype=F32)],
            scratch_shapes=[pltpu.VMEM((c, r, f), F32)],
            compiler_params=params(LIMIT),
        )(self.inputs)

    def forward(self, n1, cot, one, two, vec):
        n, r, f = self.images, self.rows, self.features
        return by_image(
            partial(forward_kernel, self.tokens, self.slots, self.place), n,
            [self.image(0), own(r, f), own(r, f), fixed(*one.shape), fixed(*two.shape), fixed(*vec.shape)],
            [own(r, 3 * f), own(r, f), own(r, f), own(r, 128), fixed(self.slots * n, 2 * f)],
            [shaped(n, r, 3 * f), shaped(n, r, f), shaped(n, r, f, dtype=F32), shaped(n, r, 128, dtype=F32), shaped(self.slots * n, 2 * f, dtype=F32)],
            [self.pad], 3 * n * self.flops, LIMIT,
        )(self.live, self.inputs, n1, cot, one, two, vec)

    def backward(self, cot, triple, hidden, logits, home, two, phit, vec):
        n, r, f = self.images, self.rows, self.features
        small = padded(self.slots + 2, 8)
        return by_image(
            partial(backward_kernel, self.tokens, self.slots, self.place), n,
            [own(r, f), own(r, 3 * f), own(r, f), own(r, 128), fixed(self.slots * n, 2 * f), fixed(*two.shape), fixed(*phit.shape), fixed(*vec.shape)],
            [self.made(), own(r, f), own(r, 3 * f), fixed(8, 3 * f), fixed(small, f)],
            [shaped(n, self.tokens, f), shaped(n, r, f), shaped(n, r, 3 * f), shaped(8, 3 * f, dtype=F32), shaped(small, f, dtype=F32)],
            [pltpu.VMEM((self.keys, f), BF16)], 3 * n * self.flops, LIMIT,
        )(self.live, cot, triple, hidden, logits, home, two, phit, vec)

    def input_back(self, low, high, triple, n1, root, branch, one, two, vec, into, step):
        r, f = self.rows, self.features
        some = lambda *shape: pl.BlockSpec((step,) + shape, lambda i: (i + low // step,) + (0,) * len(shape))
        return pl.pallas_call(
            partial(input_kernel, self.tokens),
            grid=((high - low) // step,),
            in_specs=[some(r, 3 * f), some(r, f), some(r, 128), some(r, f), fixed(*one.shape), fixed(f, f), fixed(*vec.shape)]
            + [pl.BlockSpec(memory_space=pl.ANY)] * (into is not None),
            out_specs=some(self.tokens, f),
            out_shape=shaped(self.images, self.tokens, f),
            input_output_aliases={} if into is None else {7: 0},
            compiler_params=params(LIMIT),
        )(triple, n1, root, branch, one, two, vec, *([] if into is None else [into]))

    def turned(self, array):
        return array.reshape(-1, array.shape[-1]).T

    def weight_grads(self, left, left_out, right, right_out, one, two, total, small, columns, tile=256):
        f, third = self.features, self.features // tile
        def at(array, first, count):
            lead = array.shape[:-1]
            return pl.BlockSpec(lead + (tile,), lambda i: (0,) * len(lead) + (jnp.clip(i - first, 0, count - 1),))
        return pl.pallas_call(
            partial(weight_grad_kernel, self.slots),
            grid=(4 * third + 1,),
            in_specs=[fixed(*left.shape), fixed(*left_out.shape), at(right, 0, 3 * third), at(right_out, 3 * third, third),
                      at(one, 0, 2 * third), at(two, 2 * third, third), at(total, 0, 3 * third), fixed(*small.shape), fixed(*columns.shape)],
            out_specs=pl.BlockSpec((f, tile), lambda i: (0, i)),
            out_shape=shaped(f, 4 * f + 128),
            scratch_shapes=[pltpu.VMEM((f, 256), F32)],
            compiler_params=params(LIMIT),
        )(left, left_out, right, right_out, one, two, total, small, columns)


def expert_forward(pieces, weights, images):
    per, _, hidden = weights[0].shape
    size, count = pieces[0].shape[0], len(pieces)
    kept = shaped(2, per, size * count, hidden)
    made = pl.pallas_call(
        partial(expert_kernel, count, images),
        out_shape=[shaped(*p.shape) for p in pieces] + [kept, kept],
        compiler_params=params(SMALL, 0),
    )(*pieces, *weights)
    return made[:count], made[count:]


def expert_grads(pieces, kept, up, down):
    return pl.pallas_call(
        partial(expert_grad_kernel, len(pieces)),
        out_shape=[shaped(*up.shape, dtype=F32), shaped(*down.shape, dtype=F32), shaped(*up.shape), shaped(*down.shape)],
        compiler_params=params(SMALL, 0),
    )(*pieces, *kept)


def wide(a, width=128):
    return jnp.pad(a, ((0, 0), (0, width - a.shape[1])))


def body(grid, inputs, counts, ln1_gain, ln1_bias, w_qkv, w_out, ln2_gain, ln2_bias, phi, w_up, w_down, cotangent):
    me = grid.coords()
    batches, capacity, tokens, features = inputs.shape
    images = batches * capacity
    slots = phi.shape[1]
    per = slots // grid.m
    token = (jnp.arange(capacity)[None, :] < counts).astype(jnp.int32).reshape(-1)
    mixer = Mixer(grid, inputs, slots, token, me["e"])
    vectors = jnp.stack([ln1_gain, ln1_bias, ln2_gain, ln2_bias], axis=1)
    packed = jnp.concatenate([w_qkv, w_out, wide(jnp.concatenate([phi, vectors], axis=1))], axis=1)
    flow = Flow(gather_steps(grid, me, packed, 2 * features))
    cot, token = beside([flow], token, lambda token: mixer.padded_cotangent(cotangent))
    _, token = beside([flow], token)
    (n1, root), token = beside([flow], token, lambda token: mixer.standardize())
    other = Flow(neighbour_steps(grid, lax.optimization_barrier(([w_up, w_down], token))[0]))
    _, token = beside([flow], token)
    one, two = flow.value
    columns = two[:, 2 * features : 2 * features + padded(slots + 4, 16)].astype(F32)
    turned = columns.T
    vec = jnp.pad(turned[slots : slots + 4], ((0, 4), (0, 0)))

    made, token = beside([other], token, lambda token: mixer.forward(n1, cot, one, two, vec))
    triple, mixed, hidden, logits, slot = made
    flow = Flow(out_steps(grid, slot.astype(BF16)))
    _, token = beside([flow], token)
    lefts, token = beside([flow], token, lambda token: (mixer.turned(n1), mixer.turned(mixed)))
    pieces = flow.value
    back, kept = expert_forward(pieces, [w_up, other.value[0], w_down, other.value[1]], images)
    flow = Flow(home_steps(grid, back))
    made, token = beside([flow], token, lambda token: expert_grads(pieces, kept, w_up, w_down))
    grad_up, grad_down, *others = made
    _, token = beside([flow], token)
    other = Flow(neighbour_steps(grid, others))
    made, token = beside(
        [other], token, lambda token: mixer.backward(cot, triple, hidden, logits, flow.value.astype(F32), two, turned.astype(BF16), vec)
    )
    outs, branch, grad_triple, total, small = made
    packed = mixer.weight_grads(
        *lefts, grad_triple, branch, one, two, total, wide(small.T), columns[:, slots : slots + 2]
    )
    grad_up, grad_down = grad_up + other.value[0].astype(F32), grad_down + other.value[1].astype(F32)
    flow = Flow(reduce_steps(grid, me, packed, padded(packed.shape[1] // 2, 128)))
    grad_in, low = None, 0
    for count in SHARES:
        grad_in, token = beside(
            [flow],
            token,
            lambda token: mixer.input_back(
                low * images // 12, (low + count) * images // 12, grad_triple, n1, root, branch, one, two, vec, grad_in, max(images // 6, 1)
            ),
        )
        low += count
    while not flow.done:
        _, token = beside([flow], token)
    sums = flow.value
    small = sums[:, 4 * features :]
    return (
        outs.reshape(inputs.shape),
        grad_in.reshape(inputs.shape),
        small[:, slots + 2],
        small[:, slots + 3],
        sums[:, : 3 * features],
        sums[:, 3 * features : 4 * features],
        small[:, slots],
        small[:, slots + 1],
        small[:, :slots],
        grad_up,
        grad_down,
    )


def solution(mesh):
    rows = P(BOTH, None)
    row = P(BOTH)
    image = P(None, BOTH, None, None)
    up, down = P("expert", None, "dp"), P("expert", "dp", None)
    grid = Grid(mesh.shape["dp"], mesh.shape["expert"])
    return jax.shard_map(
        partial(body, grid),
        mesh=mesh,
        in_specs=(image, P(None, BOTH), row, row, rows, rows, row, row, rows, up, down, image),
        out_specs=(image, image, row, row, rows, rows, row, row, rows, up, down),
        check_vma=False,
    )
```

```python
from functools import partial

import jax
import jax.numpy as jnp
from jax import lax
from jax.experimental import pallas as pl
from jax.experimental.pallas import tpu as pltpu
from jax.sharding import PartitionSpec as P

HEAD_DIM = 64
EPSILON = 1e-06
BOTH = ("dp", "expert")
F32, BF16 = jnp.float32, jnp.bfloat16
LOW = -1e30
LIMIT = 52
SHARES = (2, 6, 4)
SMALL = 52
GATHER_CUT = 1664


class Grid:
    def __init__(self, n, m):
        self.n, self.m = n, m
        self.size = {"z": n // 2, "y": 2, "x": m // 2, "c": 2, "e": m}

    def coords(self):
        d, e = lax.axis_index("dp"), lax.axis_index("expert")
        return {"z": d // 2, "y": d % 2, "x": e // 2, "c": e % 2, "e": e}

    def perm(self, axis, k):
        pairs = []
        for source in range(self.n * self.m):
            d, e = divmod(source, self.m)
            p = {"z": d // 2, "y": d % 2, "x": e // 2, "c": e % 2, "e": e}
            q = (p[axis] + k) % self.size[axis]
            if axis == "e":
                target = d * self.m + q
            else:
                p[axis] = q
                target = (p["z"] * 2 + p["y"]) * self.m + p["x"] * 2 + p["c"]
            pairs.append((source, target))
        return pairs

    def send(self, a, axis, k):
        return lax.ppermute(a, BOTH, self.perm(axis, k))

    def by_coordinate(self, me, axis, pieces, at=0):
        s = self.size[axis]
        if s == 2:
            return jnp.stack([jnp.where(me == p, pieces[0], pieces[1]) for p in range(2)], axis=at)
        if s <= 4:
            return jnp.stack([lax.select_n((me - p) % s, *pieces) for p in range(s)], axis=at)
        shape = pieces[0].shape
        out = jnp.zeros(shape[:at] + (s,) + shape[at:], pieces[0].dtype)
        for k in range(s):
            out = lax.dynamic_update_index_in_dim(out, pieces[k], (me - k) % s, at)
        return out

    def block(self, a, axis, me, k, at=0):
        return lax.dynamic_index_in_dim(a, (me[axis] + k) % self.size[axis], at, keepdims=False)


def joined(parts, axis):
    return jnp.concatenate(parts, axis=axis) if len(parts) > 1 else parts[0]


def send_on(grid, items):
    return [[grid.send(a, axis, k) for k in range(1, grid.size[axis])] for a, axis in items]


def gather_steps(grid, me, a, cut):
    got = yield send_on(grid, [(a, "z")])
    a = grid.by_coordinate(me["z"], "z", [a] + got[0])
    parts = [a[..., :cut], a[..., cut:]]
    for axes, at in (("yx", (1, 1)), ("xy", (2, 1)), ("cc", (3, 3))):
        got = yield send_on(grid, list(zip(parts, axes)))
        parts = [grid.by_coordinate(me[x], x, [p] + r, i) for p, r, x, i in zip(parts, got, axes, at)]
    return [p.reshape(-1, p.shape[-1]) for p in parts]


def reduce_steps(grid, me, a, cut):
    s = grid.size
    if len(a) == 1:
        a = a[0].reshape(s["z"], 2, s["x"], 2, -1, a[0].shape[1])
        own, other = (grid.block(a, "c", me, k, 3) for k in range(2))
    else:
        own, other = (p.reshape(s["z"], 2, s["x"], -1, p.shape[1]) for p in a)
    got = yield [[grid.send(other, "c", 1)]]
    a = (own.astype(F32) + got[0][0].astype(F32)).astype(BF16)
    parts = [a[..., :cut], a[..., cut:]]
    for axes, at in (("xy", (2, 1)), ("yx", (1, 1))):
        blocks = [[grid.block(p, x, me, k, i) for k in range(s[x])] for p, x, i in zip(parts, axes, at)]
        got = yield [[grid.send(b, x, k) for k, b in enumerate(bs) if k] for bs, x in zip(blocks, axes)]
        parts = [sum([b.astype(F32) for b in r], bs[0].astype(F32)).astype(BF16) for bs, r in zip(blocks, got)]
    a = jnp.concatenate(parts, axis=-1)
    blocks = [grid.block(a, "z", me, k) for k in range(s["z"])]
    got = yield [[grid.send(b, "z", k) for k, b in enumerate(blocks) if k]]
    return sum([b.astype(F32) for b in got[0]], blocks[0].astype(F32))


def swap_step(grid, blocks, axis, sign):
    received = yield [[grid.send(b, axis, sign * k) for k, b in enumerate(blocks) if k]]
    return list(blocks[:1]) + received[0]


def out_steps(grid, rows):
    r = rows.shape[0] // grid.m
    pieces = yield from swap_step(grid, [rows[k * r : (k + 1) * r] for k in range(grid.m)], "e", 1)
    own = jnp.concatenate(pieces, axis=0)
    return (yield from swap_step(grid, [own] * grid.size["z"], "z", 1))


def home_steps(grid, pieces):
    pieces = yield from swap_step(grid, pieces, "z", -1)
    own = sum([p.astype(F32) for p in pieces]).astype(BF16)
    r = own.shape[0] // grid.m
    pieces = yield from swap_step(grid, [own[k * r : (k + 1) * r] for k in range(grid.m)], "e", -1)
    return jnp.concatenate(pieces, axis=0)


def neighbour_steps(grid, arrays):
    received = yield [[grid.send(a, "y", 1) for a in arrays]]
    return received[0]


class Flow:
    def __init__(self, steps):
        self.steps, self.value, self.done = steps, None, False
        self.advance(None)

    def advance(self, received):
        try:
            self.waiting = self.steps.send(received)
        except StopIteration as end:
            self.value, self.done, self.waiting = end.value, True, None


def beside(flows, token, work=None):
    flows = [flow for flow in flows if flow is not None and not flow.done]
    made = work(token) if work else ()
    received, made, token = lax.optimization_barrier(([flow.waiting for flow in flows], made, token))
    for flow, arrays in zip(flows, received):
        flow.advance(arrays)
    return made, token


def dot(a, b, ca=1, cb=0):
    return lax.dot_general(a, b, (((ca,), (cb,)), ((), ())), preferred_element_type=F32)


def padded(v, step):
    return -(-v // step) * step


def standardized(v):
    width = v.shape[-1]
    center = v - jnp.sum(v, axis=-1, keepdims=True) * (1.0 / width)
    root = lax.rsqrt(jnp.sum(center * center, axis=-1, keepdims=True) * (1.0 / width) + EPSILON)
    return center * root, root


def lanes_of(head, width):
    return lax.broadcasted_iota(jnp.int32, (1, width), 1) // HEAD_DIM == head


def by_head(v, scale):
    width = v.shape[1]
    return jnp.concatenate([v * jnp.where(lanes_of(h, width), scale, 0.0).astype(BF16) for h in range(width // HEAD_DIM)], axis=0)


def own_columns(v):
    half = v.shape[0] // 2
    return jnp.where(lanes_of(0, v.shape[1]), v[:half], v[half:])


def routed(logits, tokens, slots):
    row = lax.broadcasted_iota(jnp.int32, logits.shape, 0)
    lane = lax.broadcasted_iota(jnp.int32, logits.shape, 1)
    valid = (row < tokens) & (lane < slots)
    kept = jnp.where(valid, logits, LOW)
    down = jnp.where(valid, jnp.exp(kept - jnp.max(kept, axis=0, keepdims=True)), 0.0)
    down_sum = jnp.sum(down, axis=0, keepdims=True)
    over_tokens = down * (1.0 / jnp.where(down_sum > 0, down_sum, 1.0))
    across = jnp.where(valid, jnp.exp(kept - jnp.max(kept, axis=1, keepdims=True)), 0.0)
    across_sum = jnp.sum(across, axis=1, keepdims=True)
    over_slots = across * (1.0 / jnp.where(across_sum > 0, across_sum, 1.0))
    return over_tokens, over_slots


def longer(v, count):
    return jnp.concatenate([v, jnp.zeros((count - v.shape[0], v.shape[1]), v.dtype)], axis=0)


def pad_kernel(tokens, cot_ref, out_ref):
    rows = out_ref.shape[1]
    for k in range(cot_ref.shape[1]):
        out_ref[k] = jnp.zeros((rows, out_ref.shape[2]), BF16)
        out_ref[k, :tokens] = cot_ref[0, k]


def standardize_kernel(tokens, x_ref, n1_ref, root_ref, pad_ref):
    @pl.when(pl.program_id(0) == 0)
    def _():
        pad_ref[...] = jnp.zeros_like(pad_ref)

    for k in range(x_ref.shape[1]):
        pad_ref[k, :tokens] = x_ref[0, k].astype(F32)
        n1, root = standardized(pad_ref[k])
        n1_ref[k] = n1.astype(BF16)
        root_ref[k] = jnp.broadcast_to(root, root_ref.shape[1:])


def forward_kernel(
    tokens, slots, place, live, x_ref, n1_ref, cot_ref, one_ref, two_ref, vec_ref,
    triple_ref, mixed_ref, hidden_ref, logits_ref, slot_ref, pad_ref,
):
    i = pl.program_id(0)
    rows, features = pad_ref.shape
    keys = padded(rows, 128)

    @pl.when(i == 0)
    def _():
        pad_ref[...] = jnp.zeros_like(pad_ref)

    @pl.when(live[i] == 0)
    def _():
        mixed_ref[...] = jnp.zeros_like(mixed_ref)
        for s in range(slots):
            slot_ref[pl.ds(place(live, s, i), 1)] = jnp.zeros((1, slot_ref.shape[1]), F32)

    @pl.when(live[i] != 0)
    def _():
        pad_ref[:tokens] = x_ref[0, 0].astype(F32)
        normed = (n1_ref[0].astype(F32) * vec_ref[0:1] + vec_ref[1:2]).astype(BF16)
        for part in range(3):
            cut = slice(part * features, (part + 1) * features)
            weights = one_ref[:, cut] if part < 2 else two_ref[:, :features]
            triple_ref[0, :, cut] = dot(normed, weights).astype(BF16)
        bias = jnp.where(lax.broadcasted_iota(jnp.int32, (1, keys), 1) < tokens, 0.0, LOW)
        for low in range(0, features, 128):
            q = triple_ref[0, :, low : low + 128]
            k = longer(triple_ref[0, :, features + low : features + low + 128], keys)
            v = longer(triple_ref[0, :, 2 * features + low : 2 * features + low + 128], keys)
            scores = dot(by_head(q, HEAD_DIM**-0.5), k, 1, 1) + bias
            powers = jnp.exp(scores - jnp.max(scores, axis=1, keepdims=True))
            total = dot(powers.astype(BF16), v) * (1.0 / jnp.sum(powers, axis=1, keepdims=True))
            mixed_ref[0, :, low : low + 128] = own_columns(total).astype(BF16)
        hidden = pad_ref[...] + dot(mixed_ref[0], two_ref[:, features : 2 * features])
        hidden_ref[0] = hidden
        n2, _ = standardized(hidden)
        normed_two = (n2 * vec_ref[2:3] + vec_ref[3:4]).astype(BF16)
        logits = dot(normed_two, two_ref[:, 2 * features :])
        logits_ref[0] = logits
        dispatch, combine = routed(logits, tokens, slots)
        slot_in = dot(dispatch.astype(BF16), normed_two, 0, 0)
        grad_slot = dot(combine.astype(BF16), cot_ref[0], 0, 0)
        for s in range(slots):
            slot_ref[pl.ds(place(live, s, i), 1), :features] = slot_in[s : s + 1]
            slot_ref[pl.ds(place(live, s, i), 1), features:] = grad_slot[s : s + 1]


def expert_kernel(pieces, images, *refs):
    rows_in, (up, up_other, down, down_other) = refs[:pieces], refs[pieces : pieces + 4]
    rows_out, (active_ref, slope_ref) = refs[pieces + 4 : 2 * pieces + 4], refs[2 * pieces + 4 :]
    per, features = up.shape[:2]
    both = jnp.concatenate([r[...] for r in rows_in], axis=0)
    rows, grads = both[:, :features], both[:, features:]
    index = lax.broadcasted_iota(jnp.int32, (rows.shape[0], 1), 0)
    total = total_back = 0.0
    for part, (up_ref, down_ref) in enumerate(((up, down), (up_other, down_other))):
        for j in range(per):
            mine = (index // images) % per == j
            pre = dot(rows, up_ref[j])
            phi = 0.5 * (1.0 + lax.erf(pre * (0.5**0.5)))
            density = jnp.exp(pre * pre * -0.5) * (0.5 / jnp.pi) ** 0.5
            active = jnp.where(mine, pre * phi, 0.0).astype(BF16)
            grad = dot(grads, down_ref[j], 1, 1)
            grad = jnp.where(mine, grad * (phi + pre * density), 0.0).astype(BF16)
            active_ref[part, j] = active
            slope_ref[part, j] = grad
            total = total + dot(active, down_ref[j])
            total_back = total_back + dot(grad, up_ref[j], 1, 1)
    size = rows_in[0].shape[0]
    for k, ref in enumerate(rows_out):
        ref[:, :features] = total[k * size : (k + 1) * size].astype(BF16)
        ref[:, features:] = total_back[k * size : (k + 1) * size].astype(BF16)


def expert_grad_kernel(pieces, *refs):
    rows_in, (active_ref, slope_ref) = refs[:pieces], refs[pieces : pieces + 2]
    outs = refs[pieces + 2 :]
    features = outs[0].shape[1]
    both = jnp.concatenate([r[...] for r in rows_in], axis=0)
    rows, grads = both[:, :features].T, both[:, features:]
    for part in range(2):
        up_ref, down_ref = outs[2 * part : 2 * part + 2]
        for j in range(up_ref.shape[0]):
            up_ref[j] = dot(rows, slope_ref[part, j]).astype(up_ref.dtype)
            down_ref[j] = dot(active_ref[part, j], grads, 0, 0).astype(down_ref.dtype)


def backward_kernel(
    tokens, slots, place, live, cot_ref, triple_ref, hidden_ref, logits_ref, home_ref, two_ref, phit_ref, vec_ref,
    out_ref, branch_ref, grad_ref, total_ref, small_ref, gm_ref,
):
    i = pl.program_id(0)
    rows, features = hidden_ref.shape[1:]
    keys = gm_ref.shape[0]

    @pl.when(i == 0)
    def _():
        gm_ref[...] = jnp.zeros_like(gm_ref)
        total_ref[...] = jnp.zeros_like(total_ref)
        small_ref[...] = jnp.zeros_like(small_ref)

    @pl.when(live[i] == 0)
    def _():
        out_ref[...] = jnp.zeros_like(out_ref)
        branch_ref[...] = jnp.zeros_like(branch_ref)
        grad_ref[...] = jnp.zeros_like(grad_ref)

    @pl.when(live[i] != 0)
    def _():
        hidden = hidden_ref[0]
        n2, root = standardized(hidden)
        gain = vec_ref[2:3]
        normed_two = (n2 * gain + vec_ref[3:4]).astype(BF16)
        over_tokens, over_slots = routed(logits_ref[0], tokens, slots)
        over_tokens, over_slots = over_tokens[:, :slots], over_slots[:, :slots]
        dispatch, combine = over_tokens.astype(BF16), over_slots.astype(BF16)
        home = jnp.concatenate([home_ref[pl.ds(place(live, s, i), 1)] for s in range(slots)], axis=0).astype(BF16)
        slot_out, grad_in = home[:, :features], home[:, features:]
        cot = cot_ref[0].astype(F32)
        result = hidden + dot(combine, slot_out)
        out_ref[0] = result[:tokens].astype(BF16)
        grad_combine = dot(cot_ref[0], slot_out, 1, 1)
        grad_dispatch = dot(normed_two, grad_in, 1, 1)
        grad_logits = over_tokens * (grad_dispatch - jnp.sum(grad_dispatch * over_tokens, axis=0, keepdims=True))
        grad_logits += over_slots * (grad_combine - jnp.sum(grad_combine * over_slots, axis=1, keepdims=True))
        grad_logits = grad_logits.astype(BF16)
        grad_two = dot(dispatch, grad_in) + dot(grad_logits, phit_ref[:slots])
        small_ref[:slots] += dot(grad_logits, normed_two, 0, 0)
        small_ref[slots : slots + 1] += jnp.sum(grad_two * n2, axis=0, keepdims=True)
        small_ref[slots + 1 : slots + 2] += jnp.sum(grad_two, axis=0, keepdims=True)
        u = grad_two * gain
        inner = u - jnp.sum(u, axis=-1, keepdims=True) * (1.0 / features)
        inner = inner - n2 * (jnp.sum(u * n2, axis=-1, keepdims=True) * (1.0 / features))
        branch = (cot + root * inner).astype(BF16)
        branch_ref[0] = branch
        gm_ref[:rows] = dot(branch, two_ref[:, features : 2 * features], 1, 1).astype(BF16)
        valid = lax.broadcasted_iota(jnp.int32, (rows, 1), 0) < tokens
        for low in range(0, features, 256):
            q = longer(triple_ref[0, :, low : low + 256], keys)
            k = triple_ref[0, :, features + low : features + low + 256]
            v = triple_ref[0, :, 2 * features + low : 2 * features + low + 256]
            gm = gm_ref[:, low : low + 256]
            scores_all = dot(by_head(k, HEAD_DIM**-0.5), q, 1, 1)
            grad_all = dot(by_head(v, 1.0), gm, 1, 1)
            for pair in range(2):
                attention, grad_scores = [], []
                for head in (2 * pair, 2 * pair + 1):
                    cut = slice(head * rows, (head + 1) * rows)
                    scores = jnp.where(valid, scores_all[cut], LOW)
                    powers = jnp.exp(scores - jnp.max(scores, axis=0, keepdims=True))
                    inverse = 1.0 / jnp.sum(powers, axis=0, keepdims=True)
                    mean = jnp.sum(grad_all[cut] * powers, axis=0, keepdims=True) * inverse
                    powers = powers * inverse
                    attention.append(powers.astype(BF16))
                    grad_scores.append((powers * (grad_all[cut] - mean)).astype(BF16))
                own = slice(pair * 128, (pair + 1) * 128)
                grads = (
                    own_columns(dot(jnp.concatenate([g.T for g in grad_scores], axis=0), k[:, own]))[:rows] * HEAD_DIM**-0.5,
                    own_columns(dot(jnp.concatenate(grad_scores, axis=0), q[:, own])) * HEAD_DIM**-0.5,
                    own_columns(dot(jnp.concatenate(attention, axis=0), gm[:, own])),
                )
                for part, grad in enumerate(grads):
                    cut = slice(part * features + low + pair * 128, part * features + low + (pair + 1) * 128)
                    grad_ref[0, :, cut] = grad.astype(BF16)
                    total_ref[0:1, cut] += jnp.sum(grad, axis=0, keepdims=True)


def input_kernel(tokens, triple_ref, n1_ref, root_ref, branch_ref, one_ref, two_ref, vec_ref, *refs):
    out_ref = refs[-1]
    count, rows, features = branch_ref.shape
    flat = lambda a: a.reshape(count * rows, a.shape[-1])
    triple, n1, root = flat(triple_ref[...]), flat(n1_ref[...]).astype(F32), flat(root_ref[...])[:, :1]
    v = dot(triple[:, : 2 * features], one_ref[...], 1, 1) + dot(triple[:, 2 * features :], two_ref[...], 1, 1)
    v = v * vec_ref[0:1]
    inner = v - jnp.sum(v, axis=-1, keepdims=True) * (1.0 / features)
    inner = inner - n1 * (jnp.sum(v * n1, axis=-1, keepdims=True) * (1.0 / features))
    grad = flat(branch_ref[...]).astype(F32) + root * inner
    for k in range(count):
        out_ref[k] = grad[k * rows : k * rows + tokens].astype(BF16)


def weight_grad_kernel(slots, devices, core, left_ref, left_out_hbm, right_ref, right_out_ref, one_ref, two_ref, total_ref, small_ref, columns_ref, *refs):
    *outs, norm_ref, left_out_ref, arrived = refs
    i, features, tile = pl.program_id(0), left_ref.shape[0], outs[0].shape[1]
    third = features // tile

    def store(value):
        if len(outs) == 1:
            outs[0][...] = value.astype(BF16)
            return
        value = value.reshape(devices // 2, 2, -1, tile)
        for k, ref in enumerate(outs):
            half = jnp.where(core[0] == k, value[:, 0], value[:, 1])
            ref[...] = half.reshape(-1, tile).astype(BF16)

    later = pltpu.make_async_copy(left_out_hbm, left_out_ref, arrived)

    @pl.when(i == 0)
    def _():
        later.start()
        norm_ref[...] = jnp.zeros_like(norm_ref)

    @pl.when(i == 3 * third)
    def _():
        later.wait()

    def tokens(ref):
        return ref[...].reshape(-1, tile)

    def wide_part(w_ref):
        product = dot(left_ref[...], tokens(right_ref))
        total = total_ref[0:1]
        store(product * columns_ref[:, 0:1] + columns_ref[:, 1:2] * total)
        for low in range(0, tile, 128):
            cut = slice(low, low + 128)
            weights = w_ref[:, cut].astype(F32)
            norm_ref[:, :128] += weights * product[:, cut]
            norm_ref[:, 128:] += weights * total[:, cut]

    @pl.when(i < 2 * third)
    def _():
        wide_part(one_ref)

    @pl.when((i >= 2 * third) & (i < 3 * third))
    def _():
        wide_part(two_ref)

    @pl.when((i >= 3 * third) & (i < 4 * third))
    def _():
        store(dot(left_out_ref[...], tokens(right_out_ref)))

    @pl.when(i == 4 * third)
    def _():
        lane = lax.broadcasted_iota(jnp.int32, (features, 128), 1)
        gain = jnp.sum(norm_ref[:, :128], axis=1, keepdims=True)
        bias = jnp.sum(norm_ref[:, 128:], axis=1, keepdims=True)
        narrow = jnp.where(lane == slots + 2, gain, jnp.where(lane == slots + 3, bias, small_ref[...]))
        store(jnp.concatenate([narrow] * (tile // 128), axis=1))


def own(*shape, low=0):
    return pl.BlockSpec((1,) + shape, lambda i, live: (i + low,) + (0,) * len(shape))


def fixed(*shape):
    return pl.BlockSpec(shape, lambda i, *live: (0,) * len(shape), pipeline_mode=pl.Buffered(1))


def shaped(*shape, dtype=BF16):
    return jax.ShapeDtypeStruct(shape, dtype)


def params(mib, axes=1):
    return pltpu.CompilerParams(vmem_limit_bytes=mib * 1024 * 1024, dimension_semantics=("arbitrary",) * axes)


def by_image(kernel, images, in_specs, out_specs, out_shape, scratch, flops, mib):
    return pl.pallas_call(
        kernel,
        grid_spec=pltpu.PrefetchScalarGridSpec(
            num_scalar_prefetch=1, grid=(images,), in_specs=in_specs, out_specs=out_specs, scratch_shapes=scratch
        ),
        out_shape=out_shape,
        compiler_params=params(mib),
        cost_estimate=pl.CostEstimate(flops=flops, bytes_accessed=flops // 1000, transcendentals=0),
    )


class Mixer:
    def __init__(self, grid, inputs, slots, live, expert):
        self.inputs, self.slots = inputs, slots
        self.live = jnp.concatenate([live, expert[None]])
        self.owners, self.per = grid.m, slots // grid.m
        self.batches, self.capacity, self.tokens, self.features = inputs.shape
        self.images = self.batches * self.capacity
        self.rows, self.keys = padded(self.tokens, 16), padded(self.tokens, 128)
        self.pad = pltpu.VMEM((self.rows, self.features), F32)
        self.flops = self.rows * self.features * self.features * 8

    def place(self, live, s, i):
        owner = lax.rem(s // self.per + self.owners - live[self.images], self.owners)
        return (owner * self.per + s % self.per) * self.images + i

    def image(self, low):
        return pl.BlockSpec((1, 1, self.tokens, self.features), lambda i, live: ((i + low) // self.capacity, (i + low) % self.capacity, 0, 0))

    def made(self, low=0):
        return pl.BlockSpec((1, self.tokens, self.features), lambda i, live: (i + low, 0, 0))

    def padded_cotangent(self, cotangent):
        n, c, r, f = self.images, self.capacity, self.rows, self.features
        return pl.pallas_call(
            partial(pad_kernel, self.tokens),
            grid=(self.batches,),
            in_specs=[pl.BlockSpec((1, c, self.tokens, f), lambda i: (i, 0, 0, 0))],
            out_specs=pl.BlockSpec((c, r, f), lambda i: (i, 0, 0)),
            out_shape=shaped(n, r, f),
            compiler_params=params(LIMIT),
        )(cotangent)

    def standardize(self):
        n, c, r, f = self.images, self.capacity, self.rows, self.features
        group = lambda *shape: pl.BlockSpec((c,) + shape, lambda i: (i,) + (0,) * len(shape))
        return pl.pallas_call(
            partial(standardize_kernel, self.tokens),
            grid=(self.batches,),
            in_specs=[pl.BlockSpec((1, c, self.tokens, f), lambda i: (i, 0, 0, 0))],
            out_specs=[group(r, f), group(r, 128)],
            out_shape=[shaped(n, r, f), shaped(n, r, 128, dtype=F32)],
            scratch_shapes=[pltpu.VMEM((c, r, f), F32)],
            compiler_params=params(LIMIT),
        )(self.inputs)

    def forward(self, n1, cot, one, two, vec):
        n, r, f = self.images, self.rows, self.features
        return by_image(
            partial(forward_kernel, self.tokens, self.slots, self.place), n,
            [self.image(0), own(r, f), own(r, f), fixed(*one.shape), fixed(*two.shape), fixed(*vec.shape)],
            [own(r, 3 * f), own(r, f), own(r, f), own(r, 128), fixed(self.slots * n, 2 * f)],
            [shaped(n, r, 3 * f), shaped(n, r, f), shaped(n, r, f, dtype=F32), shaped(n, r, 128, dtype=F32), shaped(self.slots * n, 2 * f, dtype=F32)],
            [self.pad], 3 * n * self.flops, LIMIT,
        )(self.live, self.inputs, n1, cot, one, two, vec)

    def backward(self, cot, triple, hidden, logits, home, two, phit, vec):
        n, r, f = self.images, self.rows, self.features
        small = padded(self.slots + 2, 8)
        return by_image(
            partial(backward_kernel, self.tokens, self.slots, self.place), n,
            [own(r, f), own(r, 3 * f), own(r, f), own(r, 128), fixed(self.slots * n, 2 * f), fixed(*two.shape), fixed(*phit.shape), fixed(*vec.shape)],
            [self.made(), own(r, f), own(r, 3 * f), fixed(8, 3 * f), fixed(small, f)],
            [shaped(n, self.tokens, f), shaped(n, r, f), shaped(n, r, 3 * f), shaped(8, 3 * f, dtype=F32), shaped(small, f, dtype=F32)],
            [pltpu.VMEM((self.keys, f), BF16)], 3 * n * self.flops, LIMIT,
        )(self.live, cot, triple, hidden, logits, home, two, phit, vec)

    def input_back(self, low, high, triple, n1, root, branch, one, two, vec, into, step):
        r, f = self.rows, self.features
        some = lambda *shape: pl.BlockSpec((step,) + shape, lambda i: (i + low // step,) + (0,) * len(shape))
        return pl.pallas_call(
            partial(input_kernel, self.tokens),
            grid=((high - low) // step,),
            in_specs=[some(r, 3 * f), some(r, f), some(r, 128), some(r, f), fixed(*one.shape), fixed(f, f), fixed(*vec.shape)]
            + [pl.BlockSpec(memory_space=pl.ANY)] * (into is not None),
            out_specs=some(self.tokens, f),
            out_shape=shaped(self.images, self.tokens, f),
            input_output_aliases={} if into is None else {7: 0},
            compiler_params=params(LIMIT),
        )(triple, n1, root, branch, one, two, vec, *([] if into is None else [into]))

    def turned(self, array):
        return array.reshape(-1, array.shape[-1]).T

    def weight_grads(self, core, devices, left, left_out, right, right_out, one, two, total, small, columns, tile=256):
        f, third = self.features, self.features // tile
        apart = f // devices % 8 == 0
        rows = [f // 2, f // 2] if apart else [f]

        def at(array, first, count):
            lead = array.shape[:-1]
            return pl.BlockSpec(lead + (tile,), lambda i, core: (0,) * len(lead) + (jnp.clip(i - first, 0, count - 1),))

        return pl.pallas_call(
            partial(weight_grad_kernel, self.slots, devices),
            grid_spec=pltpu.PrefetchScalarGridSpec(
                num_scalar_prefetch=1,
                grid=(4 * third + 1,),
                in_specs=[fixed(*left.shape), pl.BlockSpec(memory_space=pl.ANY), at(right, 0, 3 * third), at(right_out, 3 * third, third),
                          at(one, 0, 2 * third), at(two, 2 * third, third), at(total, 0, 3 * third), fixed(*small.shape), fixed(*columns.shape)],
                out_specs=[pl.BlockSpec((r, tile), lambda i, core: (0, i)) for r in rows],
                scratch_shapes=[pltpu.VMEM((f, 256), F32), pltpu.VMEM(left_out.shape, BF16), pltpu.SemaphoreType.DMA],
            ),
            out_shape=[shaped(r, 4 * f + 128) for r in rows],
            compiler_params=params(LIMIT),
        )(core[None], left, left_out, right, right_out, one, two, total, small, columns)


def expert_forward(pieces, weights, images):
    per, _, hidden = weights[0].shape
    size, count = pieces[0].shape[0], len(pieces)
    kept = shaped(2, per, size * count, hidden)
    made = pl.pallas_call(
        partial(expert_kernel, count, images),
        out_shape=[shaped(*p.shape) for p in pieces] + [kept, kept],
        compiler_params=params(SMALL, 0),
    )(*pieces, *weights)
    return made[:count], made[count:]


def expert_grads(pieces, kept, up, down):
    return pl.pallas_call(
        partial(expert_grad_kernel, len(pieces)),
        out_shape=[shaped(*up.shape, dtype=F32), shaped(*down.shape, dtype=F32), shaped(*up.shape), shaped(*down.shape)],
        compiler_params=params(SMALL, 0),
    )(*pieces, *kept)


def wide(a, width=128):
    return jnp.pad(a, ((0, 0), (0, width - a.shape[1])))


def body(grid, inputs, counts, ln1_gain, ln1_bias, w_qkv, w_out, ln2_gain, ln2_bias, phi, w_up, w_down, cotangent):
    me = grid.coords()
    batches, capacity, tokens, features = inputs.shape
    images = batches * capacity
    slots = phi.shape[1]
    per = slots // grid.m
    token = (jnp.arange(capacity)[None, :] < counts).astype(jnp.int32).reshape(-1)
    mixer = Mixer(grid, inputs, slots, token, me["e"])
    vectors = jnp.stack([ln1_gain, ln1_bias, ln2_gain, ln2_bias])
    vectors = dot(vectors, jnp.eye(4, dtype=BF16), 0, 0).astype(BF16)
    packed = jnp.concatenate([w_qkv, w_out, wide(jnp.concatenate([phi, vectors], axis=1))], axis=1)
    flow = Flow(gather_steps(grid, me, packed, 2 * features))
    cot, token = beside([flow], token, lambda token: mixer.padded_cotangent(cotangent))
    _, token = beside([flow], token)
    (n1, root), token = beside([flow], token, lambda token: mixer.standardize())
    other = Flow(neighbour_steps(grid, lax.optimization_barrier(([w_up, w_down], token))[0]))
    _, token = beside([flow], token)
    one, two = flow.value
    columns = two[:, 2 * features : 2 * features + padded(slots + 4, 16)].astype(F32)
    turned = columns.T
    vec = jnp.pad(turned[slots : slots + 4], ((0, 4), (0, 0)))

    made, token = beside([], token, lambda token: mixer.forward(n1, cot, one, two, vec))
    triple, mixed, hidden, logits, slot = made
    flow = Flow(out_steps(grid, slot.astype(BF16)))
    _, token = beside([flow, other], token)
    lefts, token = beside([flow], token, lambda token: (mixer.turned(n1), mixer.turned(mixed)))
    pieces = flow.value
    back, kept = expert_forward(pieces, [w_up, other.value[0], w_down, other.value[1]], images)
    flow = Flow(home_steps(grid, back))
    made, token = beside([flow], token, lambda token: expert_grads(pieces, kept, w_up, w_down))
    grad_up, grad_down, *others = made
    _, token = beside([flow], token)
    other = Flow(neighbour_steps(grid, others))
    made, token = beside(
        [other], token, lambda token: mixer.backward(cot, triple, hidden, logits, flow.value.astype(F32), two, turned.astype(BF16), vec)
    )
    outs, branch, grad_triple, total, small = made
    packed = mixer.weight_grads(
        me["c"], grid.n * grid.m, *lefts, grad_triple, branch, one, two, total, wide(small.T), columns[:, slots : slots + 2]
    )
    flow = Flow(reduce_steps(grid, me, packed, padded(packed[0].shape[1] // 2, 128)))
    grad_in, low, flows = None, 0, [flow]
    for count in SHARES:
        grad_in, token = beside(
            flows,
            token,
            lambda token: mixer.input_back(
                low * images // 12, (low + count) * images // 12, grad_triple, n1, root, branch, one, two, vec, grad_in, max(images // 6, 1)
            ),
        )
        low += count
    while not flow.done:
        _, token = beside([flow], token)
    sums = flow.value
    grad_up, grad_down = grad_up + other.value[0].astype(F32), grad_down + other.value[1].astype(F32)
    small = sums[:, 4 * features :]
    return (
        outs.reshape(inputs.shape),
        grad_in.reshape(inputs.shape),
        small[:, slots + 2],
        small[:, slots + 3],
        sums[:, : 3 * features],
        sums[:, 3 * features : 4 * features],
        small[:, slots],
        small[:, slots + 1],
        small[:, :slots],
        grad_up,
        grad_down,
    )


def solution(mesh):
    rows = P(BOTH, None)
    row = P(BOTH)
    image = P(None, BOTH, None, None)
    up, down = P("expert", None, "dp"), P("expert", "dp", None)
    grid = Grid(mesh.shape["dp"], mesh.shape["expert"])
    return jax.shard_map(
        partial(body, grid),
        mesh=mesh,
        in_specs=(image, P(None, BOTH), row, row, rows, rows, row, row, rows, up, down, image),
        out_specs=(image, image, row, row, rows, rows, row, row, rows, up, down),
        check_vma=False,
    )
```

```python
from functools import partial

import jax
import jax.numpy as jnp
from jax import lax
from jax.experimental import pallas as pl
from jax.experimental.pallas import tpu as pltpu
from jax.sharding import PartitionSpec as P

HEAD_DIM = 64
EPSILON = 1e-06
BOTH = ("dp", "expert")
F32, BF16 = jnp.float32, jnp.bfloat16
LOW = -1e30
LIMIT = 52
SHARES = (2, 8, 2)
SMALL = 52
GATHER_CUT = 1664


class Grid:
    def __init__(self, n, m):
        self.n, self.m = n, m
        self.size = {"z": n // 2, "y": 2, "x": m // 2, "c": 2, "e": m}

    def coords(self):
        d, e = lax.axis_index("dp"), lax.axis_index("expert")
        return {"z": d // 2, "y": d % 2, "x": e // 2, "c": e % 2, "e": e}

    def perm(self, axis, k):
        pairs = []
        for source in range(self.n * self.m):
            d, e = divmod(source, self.m)
            p = {"z": d // 2, "y": d % 2, "x": e // 2, "c": e % 2, "e": e}
            q = (p[axis] + k) % self.size[axis]
            if axis == "e":
                target = d * self.m + q
            else:
                p[axis] = q
                target = (p["z"] * 2 + p["y"]) * self.m + p["x"] * 2 + p["c"]
            pairs.append((source, target))
        return pairs

    def send(self, a, axis, k):
        return lax.ppermute(a, BOTH, self.perm(axis, k))

    def by_coordinate(self, me, axis, pieces, at=0):
        s = self.size[axis]
        if s == 2:
            return jnp.stack([jnp.where(me == p, pieces[0], pieces[1]) for p in range(2)], axis=at)
        if s <= 4:
            return jnp.stack([lax.select_n((me - p) % s, *pieces) for p in range(s)], axis=at)
        shape = pieces[0].shape
        out = jnp.zeros(shape[:at] + (s,) + shape[at:], pieces[0].dtype)
        for k in range(s):
            out = lax.dynamic_update_index_in_dim(out, pieces[k], (me - k) % s, at)
        return out

    def block(self, a, axis, me, k, at=0):
        return lax.dynamic_index_in_dim(a, (me[axis] + k) % self.size[axis], at, keepdims=False)


def joined(parts, axis):
    return jnp.concatenate(parts, axis=axis) if len(parts) > 1 else parts[0]


def send_on(grid, items):
    return [[grid.send(a, axis, k) for k in range(1, grid.size[axis])] for a, axis in items]


def gather_steps(grid, me, a, cut):
    got = yield send_on(grid, [(a, "z")])
    a = grid.by_coordinate(me["z"], "z", [a] + got[0])
    parts = [a[..., :cut], a[..., cut:]]
    for axes, at in (("yx", (1, 1)), ("xy", (2, 1)), ("cc", (3, 3))):
        got = yield send_on(grid, list(zip(parts, axes)))
        parts = [grid.by_coordinate(me[x], x, [p] + r, i) for p, r, x, i in zip(parts, got, axes, at)]
    return [p.reshape(-1, p.shape[-1]) for p in parts]


def reduce_steps(grid, me, a, cut):
    s = grid.size
    if len(a) == 1:
        a = a[0].reshape(s["z"], 2, s["x"], 2, -1, a[0].shape[1])
        own, other = (grid.block(a, "c", me, k, 3) for k in range(2))
    else:
        own, other = (p.reshape(s["z"], 2, s["x"], -1, p.shape[1]) for p in a)
    got = yield [[grid.send(other, "c", 1)]]
    a = (own.astype(F32) + got[0][0].astype(F32)).astype(BF16)
    parts = [a[..., :cut], a[..., cut:]]
    for axes, at in (("xy", (2, 1)), ("yx", (1, 1))):
        blocks = [[grid.block(p, x, me, k, i) for k in range(s[x])] for p, x, i in zip(parts, axes, at)]
        got = yield [[grid.send(b, x, k) for k, b in enumerate(bs) if k] for bs, x in zip(blocks, axes)]
        parts = [sum([b.astype(F32) for b in r], bs[0].astype(F32)).astype(BF16) for bs, r in zip(blocks, got)]
    a = jnp.concatenate(parts, axis=-1)
    blocks = [grid.block(a, "z", me, k) for k in range(s["z"])]
    got = yield [[grid.send(b, "z", k) for k, b in enumerate(blocks) if k]]
    return sum([b.astype(F32) for b in got[0]], blocks[0].astype(F32))


def swap_step(grid, blocks, axis, sign):
    received = yield [[grid.send(b, axis, sign * k) for k, b in enumerate(blocks) if k]]
    return list(blocks[:1]) + received[0]


def out_steps(grid, rows):
    r = rows.shape[0] // grid.m
    pieces = yield from swap_step(grid, [rows[k * r : (k + 1) * r] for k in range(grid.m)], "e", 1)
    own = jnp.concatenate(pieces, axis=0)
    return (yield from swap_step(grid, [own] * grid.size["z"], "z", 1))


def home_steps(grid, pieces):
    pieces = yield from swap_step(grid, pieces, "z", -1)
    own = sum([p.astype(F32) for p in pieces]).astype(BF16)
    r = own.shape[0] // grid.m
    pieces = yield from swap_step(grid, [own[k * r : (k + 1) * r] for k in range(grid.m)], "e", -1)
    return jnp.concatenate(pieces, axis=0)


def neighbour_steps(grid, arrays):
    received = yield [[grid.send(a, "y", 1) for a in arrays]]
    return received[0]


class Flow:
    def __init__(self, steps):
        self.steps, self.value, self.done = steps, None, False
        self.advance(None)

    def advance(self, received):
        try:
            self.waiting = self.steps.send(received)
        except StopIteration as end:
            self.value, self.done, self.waiting = end.value, True, None


def beside(flows, token, work=None):
    flows = [flow for flow in flows if flow is not None and not flow.done]
    made = work(token) if work else ()
    received, made, token = lax.optimization_barrier(([flow.waiting for flow in flows], made, token))
    for flow, arrays in zip(flows, received):
        flow.advance(arrays)
    return made, token


def dot(a, b, ca=1, cb=0):
    return lax.dot_general(a, b, (((ca,), (cb,)), ((), ())), preferred_element_type=F32)


def padded(v, step):
    return -(-v // step) * step


def standardized(v):
    width = v.shape[-1]
    mean = jnp.sum(v, axis=-1, keepdims=True) * (1.0 / width)
    center = v - mean
    root = lax.rsqrt(jnp.sum(center * center, axis=-1, keepdims=True) * (1.0 / width) + EPSILON)
    return center * root, mean, root


def lanes_of(head, width):
    return lax.broadcasted_iota(jnp.int32, (1, width), 1) // HEAD_DIM == head


def by_head(v, scale):
    width = v.shape[1]
    return jnp.concatenate([v * jnp.where(lanes_of(h, width), scale, 0.0).astype(BF16) for h in range(width // HEAD_DIM)], axis=0)


def own_columns(v):
    half = v.shape[0] // 2
    return jnp.where(lanes_of(0, v.shape[1]), v[:half], v[half:])


def routed(logits, tokens, slots):
    row = lax.broadcasted_iota(jnp.int32, logits.shape, 0)
    lane = lax.broadcasted_iota(jnp.int32, logits.shape, 1)
    valid = (row < tokens) & (lane < slots)
    kept = jnp.where(valid, logits, LOW)
    down = jnp.where(valid, jnp.exp(kept - jnp.max(kept, axis=0, keepdims=True)), 0.0)
    down_sum = jnp.sum(down, axis=0, keepdims=True)
    over_tokens = down * (1.0 / jnp.where(down_sum > 0, down_sum, 1.0))
    across = jnp.where(valid, jnp.exp(kept - jnp.max(kept, axis=1, keepdims=True)), 0.0)
    across_sum = jnp.sum(across, axis=1, keepdims=True)
    over_slots = across * (1.0 / jnp.where(across_sum > 0, across_sum, 1.0))
    return over_tokens, over_slots


def longer(v, count):
    return jnp.concatenate([v, jnp.zeros((count - v.shape[0], v.shape[1]), v.dtype)], axis=0)


def pad_kernel(tokens, cot_ref, out_ref):
    rows = out_ref.shape[1]
    for k in range(cot_ref.shape[1]):
        out_ref[k] = jnp.zeros((rows, out_ref.shape[2]), BF16)
        out_ref[k, :tokens] = cot_ref[0, k]


def standardize_kernel(tokens, x_ref, n1_ref, root_ref, pad_ref):
    @pl.when(pl.program_id(0) == 0)
    def _():
        pad_ref[...] = jnp.zeros_like(pad_ref)

    for k in range(x_ref.shape[1]):
        pad_ref[k, :tokens] = x_ref[0, k].astype(F32)
        n1, _, root = standardized(pad_ref[k])
        n1_ref[k] = n1.astype(BF16)
        root_ref[k] = jnp.broadcast_to(root, root_ref.shape[1:])


def forward_kernel(
    tokens, slots, place, live, x_ref, n1_ref, cot_ref, one_ref, two_ref, vec_ref,
    triple_ref, mixed_ref, hidden_ref, kept_ref, slot_ref, pad_ref,
):
    i = pl.program_id(0)
    rows, features = pad_ref.shape
    keys = padded(rows, 128)

    @pl.when(i == 0)
    def _():
        pad_ref[...] = jnp.zeros_like(pad_ref)

    @pl.when(live[i] == 0)
    def _():
        mixed_ref[...] = jnp.zeros_like(mixed_ref)
        for s in range(slots):
            slot_ref[pl.ds(place(live, s, i), 1)] = jnp.zeros((1, slot_ref.shape[1]), F32)

    @pl.when(live[i] != 0)
    def _():
        pad_ref[:tokens] = x_ref[0, 0].astype(F32)
        normed = (n1_ref[0].astype(F32) * vec_ref[0:1] + vec_ref[1:2]).astype(BF16)
        for part in range(3):
            cut = slice(part * features, (part + 1) * features)
            weights = one_ref[:, cut] if part < 2 else two_ref[:, :features]
            triple_ref[0, :, cut] = dot(normed, weights).astype(BF16)
        bias = jnp.where(lax.broadcasted_iota(jnp.int32, (1, keys), 1) < tokens, 0.0, LOW)
        for low in range(0, features, 128):
            q = triple_ref[0, :, low : low + 128]
            k = longer(triple_ref[0, :, features + low : features + low + 128], keys)
            v = longer(triple_ref[0, :, 2 * features + low : 2 * features + low + 128], keys)
            scores = dot(by_head(q, HEAD_DIM**-0.5), k, 1, 1) + bias
            powers = jnp.exp(scores - jnp.max(scores, axis=1, keepdims=True))
            total = dot(powers.astype(BF16), v) * (1.0 / jnp.sum(powers, axis=1, keepdims=True))
            mixed_ref[0, :, low : low + 128] = own_columns(total).astype(BF16)
        hidden = pad_ref[...] + dot(mixed_ref[0], two_ref[:, features : 2 * features])
        hidden_ref[0] = hidden
        n2, mean, root = standardized(hidden)
        normed_two = (n2 * vec_ref[2:3] + vec_ref[3:4]).astype(BF16)
        logits = dot(normed_two, two_ref[:, 2 * features :])
        dispatch, combine = routed(logits, tokens, slots)
        for part, value in enumerate((dispatch, combine, mean, root)):
            kept_ref[0, :, part * 128 : (part + 1) * 128] = jnp.broadcast_to(value, (rows, 128))
        slot_in = dot(dispatch.astype(BF16), normed_two, 0, 0)
        grad_slot = dot(combine.astype(BF16), cot_ref[0], 0, 0)
        for s in range(slots):
            slot_ref[pl.ds(place(live, s, i), 1), :features] = slot_in[s : s + 1]
            slot_ref[pl.ds(place(live, s, i), 1), features:] = grad_slot[s : s + 1]


def expert_kernel(pieces, images, *refs):
    rows_in, (up, up_other, down, down_other) = refs[:pieces], refs[pieces : pieces + 4]
    rows_out, (active_ref, slope_ref) = refs[pieces + 4 : 2 * pieces + 4], refs[2 * pieces + 4 :]
    per, features = up.shape[:2]
    both = jnp.concatenate([r[...] for r in rows_in], axis=0)
    rows, grads = both[:, :features], both[:, features:]
    index = lax.broadcasted_iota(jnp.int32, (rows.shape[0], 1), 0)
    total = total_back = 0.0
    for part, (up_ref, down_ref) in enumerate(((up, down), (up_other, down_other))):
        for j in range(per):
            mine = (index // images) % per == j
            pre = dot(rows, up_ref[j])
            phi = 0.5 * (1.0 + lax.erf(pre * (0.5**0.5)))
            density = jnp.exp(pre * pre * -0.5) * (0.5 / jnp.pi) ** 0.5
            active = jnp.where(mine, pre * phi, 0.0).astype(BF16)
            grad = dot(grads, down_ref[j], 1, 1)
            grad = jnp.where(mine, grad * (phi + pre * density), 0.0).astype(BF16)
            active_ref[part, j] = active
            slope_ref[part, j] = grad
            total = total + dot(active, down_ref[j])
            total_back = total_back + dot(grad, up_ref[j], 1, 1)
    size = rows_in[0].shape[0]
    for k, ref in enumerate(rows_out):
        ref[:, :features] = total[k * size : (k + 1) * size].astype(BF16)
        ref[:, features:] = total_back[k * size : (k + 1) * size].astype(BF16)


def expert_grad_kernel(pieces, *refs):
    rows_in, (active_ref, slope_ref) = refs[:pieces], refs[pieces : pieces + 2]
    outs = refs[pieces + 2 :]
    features = outs[0].shape[1]
    both = jnp.concatenate([r[...] for r in rows_in], axis=0)
    rows, grads = both[:, :features].T, both[:, features:]
    for part in range(2):
        up_ref, down_ref = outs[2 * part : 2 * part + 2]
        for j in range(up_ref.shape[0]):
            up_ref[j] = dot(rows, slope_ref[part, j]).astype(up_ref.dtype)
            down_ref[j] = dot(active_ref[part, j], grads, 0, 0).astype(down_ref.dtype)


def backward_kernel(
    tokens, slots, place, live, cot_ref, triple_ref, hidden_ref, kept_ref, home_ref, two_ref, phit_ref, vec_ref,
    out_ref, branch_ref, grad_ref, total_ref, small_ref, gm_ref,
):
    i = pl.program_id(0)
    rows, features = hidden_ref.shape[1:]
    keys = gm_ref.shape[0]

    @pl.when(i == 0)
    def _():
        gm_ref[...] = jnp.zeros_like(gm_ref)
        total_ref[...] = jnp.zeros_like(total_ref)
        small_ref[...] = jnp.zeros_like(small_ref)

    @pl.when(live[i] == 0)
    def _():
        out_ref[...] = jnp.zeros_like(out_ref)
        branch_ref[...] = jnp.zeros_like(branch_ref)
        grad_ref[...] = jnp.zeros_like(grad_ref)

    @pl.when(live[i] != 0)
    def _():
        hidden = hidden_ref[0]
        over_tokens, over_slots = kept_ref[0, :, :slots], kept_ref[0, :, 128 : 128 + slots]
        mean, root = (jnp.concatenate([kept_ref[0, :, low : low + 128]] * (features // 128), axis=1) for low in (256, 384))
        n2 = (hidden - mean) * root
        gain = vec_ref[2:3]
        normed_two = (n2 * gain + vec_ref[3:4]).astype(BF16)
        dispatch, combine = over_tokens.astype(BF16), over_slots.astype(BF16)
        home = jnp.concatenate([home_ref[pl.ds(place(live, s, i), 1)] for s in range(slots)], axis=0).astype(BF16)
        slot_out, grad_in = home[:, :features], home[:, features:]
        cot = cot_ref[0].astype(F32)
        result = hidden + dot(combine, slot_out)
        out_ref[0] = result[:tokens].astype(BF16)
        grad_combine = dot(cot_ref[0], slot_out, 1, 1)
        grad_dispatch = dot(normed_two, grad_in, 1, 1)
        grad_logits = over_tokens * (grad_dispatch - jnp.sum(grad_dispatch * over_tokens, axis=0, keepdims=True))
        grad_logits += over_slots * (grad_combine - jnp.sum(grad_combine * over_slots, axis=1, keepdims=True))
        grad_logits = grad_logits.astype(BF16)
        grad_two = dot(dispatch, grad_in) + dot(grad_logits, phit_ref[:slots])
        small_ref[:slots] += dot(grad_logits, normed_two, 0, 0)
        small_ref[slots : slots + 1] += jnp.sum(grad_two * n2, axis=0, keepdims=True)
        small_ref[slots + 1 : slots + 2] += jnp.sum(grad_two, axis=0, keepdims=True)
        u = grad_two * gain
        inner = u - jnp.sum(u, axis=-1, keepdims=True) * (1.0 / features)
        inner = inner - n2 * (jnp.sum(u * n2, axis=-1, keepdims=True) * (1.0 / features))
        branch = (cot + root * inner).astype(BF16)
        branch_ref[0] = branch
        gm_ref[:rows] = dot(branch, two_ref[:, features : 2 * features], 1, 1).astype(BF16)
        valid = lax.broadcasted_iota(jnp.int32, (rows, 1), 0) < tokens
        for low in range(0, features, 256):
            q = longer(triple_ref[0, :, low : low + 256], keys)
            k = triple_ref[0, :, features + low : features + low + 256]
            v = triple_ref[0, :, 2 * features + low : 2 * features + low + 256]
            gm = gm_ref[:, low : low + 256]
            scores_all = dot(by_head(k, HEAD_DIM**-0.5), q, 1, 1)
            grad_all = dot(by_head(v, 1.0), gm, 1, 1)
            for pair in range(2):
                attention, grad_scores = [], []
                for head in (2 * pair, 2 * pair + 1):
                    cut = slice(head * rows, (head + 1) * rows)
                    scores = jnp.where(valid, scores_all[cut], LOW)
                    powers = jnp.exp(scores - jnp.max(scores, axis=0, keepdims=True))
                    inverse = 1.0 / jnp.sum(powers, axis=0, keepdims=True)
                    mean = jnp.sum(grad_all[cut] * powers, axis=0, keepdims=True) * inverse
                    powers = powers * inverse
                    attention.append(powers.astype(BF16))
                    grad_scores.append((powers * (grad_all[cut] - mean)).astype(BF16))
                own = slice(pair * 128, (pair + 1) * 128)
                grads = (
                    own_columns(dot(jnp.concatenate([g.T for g in grad_scores], axis=0), k[:, own]))[:rows] * HEAD_DIM**-0.5,
                    own_columns(dot(jnp.concatenate(grad_scores, axis=0), q[:, own])) * HEAD_DIM**-0.5,
                    own_columns(dot(jnp.concatenate(attention, axis=0), gm[:, own])),
                )
                for part, grad in enumerate(grads):
                    cut = slice(part * features + low + pair * 128, part * features + low + (pair + 1) * 128)
                    grad_ref[0, :, cut] = grad.astype(BF16)
                    total_ref[0:1, cut] += jnp.sum(grad, axis=0, keepdims=True)


def input_kernel(tokens, triple_ref, n1_ref, root_ref, branch_ref, one_ref, two_ref, vec_ref, *refs):
    out_ref = refs[-1]
    count, rows, features = branch_ref.shape
    flat = lambda a: a.reshape(count * rows, a.shape[-1])
    triple, n1, root = flat(triple_ref[...]), flat(n1_ref[...]).astype(F32), flat(root_ref[...])[:, :1]
    v = dot(triple[:, : 2 * features], one_ref[...], 1, 1) + dot(triple[:, 2 * features :], two_ref[...], 1, 1)
    v = v * vec_ref[0:1]
    inner = v - jnp.sum(v, axis=-1, keepdims=True) * (1.0 / features)
    inner = inner - n1 * (jnp.sum(v * n1, axis=-1, keepdims=True) * (1.0 / features))
    grad = flat(branch_ref[...]).astype(F32) + root * inner
    for k in range(count):
        out_ref[k] = grad[k * rows : k * rows + tokens].astype(BF16)


def weight_grad_kernel(slots, devices, core, left_ref, left_out_hbm, right_ref, right_out_ref, one_ref, two_ref, total_ref, small_ref, columns_ref, *refs):
    *outs, norm_ref, left_out_ref, arrived = refs
    i, features, tile = pl.program_id(0), left_ref.shape[0], outs[0].shape[1]
    third = features // tile

    def store(value):
        if len(outs) == 1:
            outs[0][...] = value.astype(BF16)
            return
        value = value.reshape(devices // 2, 2, -1, tile)
        for k, ref in enumerate(outs):
            half = jnp.where(core[0] == k, value[:, 0], value[:, 1])
            ref[...] = half.reshape(-1, tile).astype(BF16)

    later = pltpu.make_async_copy(left_out_hbm, left_out_ref, arrived)

    @pl.when(i == 0)
    def _():
        later.start()
        norm_ref[...] = jnp.zeros_like(norm_ref)

    @pl.when(i == 3 * third)
    def _():
        later.wait()

    def tokens(ref):
        return ref[...].reshape(-1, tile)

    def wide_part(w_ref):
        product = dot(left_ref[...], tokens(right_ref))
        total = total_ref[0:1]
        store(product * columns_ref[:, 0:1] + columns_ref[:, 1:2] * total)
        for low in range(0, tile, 128):
            cut = slice(low, low + 128)
            weights = w_ref[:, cut].astype(F32)
            norm_ref[:, :128] += weights * product[:, cut]
            norm_ref[:, 128:] += weights * total[:, cut]

    @pl.when(i < 2 * third)
    def _():
        wide_part(one_ref)

    @pl.when((i >= 2 * third) & (i < 3 * third))
    def _():
        wide_part(two_ref)

    @pl.when((i >= 3 * third) & (i < 4 * third))
    def _():
        store(dot(left_out_ref[...], tokens(right_out_ref)))

    @pl.when(i == 4 * third)
    def _():
        lane = lax.broadcasted_iota(jnp.int32, (features, 128), 1)
        gain = jnp.sum(norm_ref[:, :128], axis=1, keepdims=True)
        bias = jnp.sum(norm_ref[:, 128:], axis=1, keepdims=True)
        narrow = jnp.where(lane == slots + 2, gain, jnp.where(lane == slots + 3, bias, small_ref[...]))
        store(jnp.concatenate([narrow] * (tile // 128), axis=1))


def own(*shape, low=0):
    return pl.BlockSpec((1,) + shape, lambda i, live: (i + low,) + (0,) * len(shape))


def fixed(*shape):
    return pl.BlockSpec(shape, lambda i, *live: (0,) * len(shape), pipeline_mode=pl.Buffered(1))


def shaped(*shape, dtype=BF16):
    return jax.ShapeDtypeStruct(shape, dtype)


def params(mib, axes=1):
    return pltpu.CompilerParams(vmem_limit_bytes=mib * 1024 * 1024, dimension_semantics=("arbitrary",) * axes)


def by_image(kernel, images, in_specs, out_specs, out_shape, scratch, flops, mib):
    return pl.pallas_call(
        kernel,
        grid_spec=pltpu.PrefetchScalarGridSpec(
            num_scalar_prefetch=1, grid=(images,), in_specs=in_specs, out_specs=out_specs, scratch_shapes=scratch
        ),
        out_shape=out_shape,
        compiler_params=params(mib),
        cost_estimate=pl.CostEstimate(flops=flops, bytes_accessed=flops // 1000, transcendentals=0),
    )


class Mixer:
    def __init__(self, grid, inputs, slots, live, expert):
        self.inputs, self.slots = inputs, slots
        self.live = jnp.concatenate([live, expert[None]])
        self.owners, self.per = grid.m, slots // grid.m
        self.batches, self.capacity, self.tokens, self.features = inputs.shape
        self.images = self.batches * self.capacity
        self.rows, self.keys = padded(self.tokens, 16), padded(self.tokens, 128)
        self.pad = pltpu.VMEM((self.rows, self.features), F32)
        self.flops = self.rows * self.features * self.features * 8

    def place(self, live, s, i):
        owner = lax.rem(s // self.per + self.owners - live[self.images], self.owners)
        return (owner * self.per + s % self.per) * self.images + i

    def image(self, low):
        return pl.BlockSpec((1, 1, self.tokens, self.features), lambda i, live: ((i + low) // self.capacity, (i + low) % self.capacity, 0, 0))

    def made(self, low=0):
        return pl.BlockSpec((1, self.tokens, self.features), lambda i, live: (i + low, 0, 0))

    def padded_cotangent(self, cotangent):
        n, c, r, f = self.images, self.capacity, self.rows, self.features
        return pl.pallas_call(
            partial(pad_kernel, self.tokens),
            grid=(self.batches,),
            in_specs=[pl.BlockSpec((1, c, self.tokens, f), lambda i: (i, 0, 0, 0))],
            out_specs=pl.BlockSpec((c, r, f), lambda i: (i, 0, 0)),
            out_shape=shaped(n, r, f),
            compiler_params=params(LIMIT),
        )(cotangent)

    def standardize(self):
        n, c, r, f = self.images, self.capacity, self.rows, self.features
        group = lambda *shape: pl.BlockSpec((c,) + shape, lambda i: (i,) + (0,) * len(shape))
        return pl.pallas_call(
            partial(standardize_kernel, self.tokens),
            grid=(self.batches,),
            in_specs=[pl.BlockSpec((1, c, self.tokens, f), lambda i: (i, 0, 0, 0))],
            out_specs=[group(r, f), group(r, 128)],
            out_shape=[shaped(n, r, f), shaped(n, r, 128, dtype=F32)],
            scratch_shapes=[pltpu.VMEM((c, r, f), F32)],
            compiler_params=params(LIMIT),
        )(self.inputs)

    def forward(self, n1, cot, one, two, vec):
        n, r, f = self.images, self.rows, self.features
        return by_image(
            partial(forward_kernel, self.tokens, self.slots, self.place), n,
            [self.image(0), own(r, f), own(r, f), fixed(*one.shape), fixed(*two.shape), fixed(*vec.shape)],
            [own(r, 3 * f), own(r, f), own(r, f), own(r, 512), fixed(self.slots * n, 2 * f)],
            [shaped(n, r, 3 * f), shaped(n, r, f), shaped(n, r, f, dtype=F32), shaped(n, r, 512, dtype=F32), shaped(self.slots * n, 2 * f, dtype=F32)],
            [self.pad], 3 * n * self.flops, LIMIT,
        )(self.live, self.inputs, n1, cot, one, two, vec)

    def backward(self, cot, triple, hidden, logits, home, two, phit, vec):
        n, r, f = self.images, self.rows, self.features
        small = padded(self.slots + 2, 8)
        return by_image(
            partial(backward_kernel, self.tokens, self.slots, self.place), n,
            [own(r, f), own(r, 3 * f), own(r, f), own(r, 512), fixed(self.slots * n, 2 * f), fixed(*two.shape), fixed(*phit.shape), fixed(*vec.shape)],
            [self.made(), own(r, f), own(r, 3 * f), fixed(8, 3 * f), fixed(small, f)],
            [shaped(n, self.tokens, f), shaped(n, r, f), shaped(n, r, 3 * f), shaped(8, 3 * f, dtype=F32), shaped(small, f, dtype=F32)],
            [pltpu.VMEM((self.keys, f), BF16)], 3 * n * self.flops, LIMIT,
        )(self.live, cot, triple, hidden, logits, home, two, phit, vec)

    def input_back(self, low, high, triple, n1, root, branch, one, two, vec, into, step):
        r, f = self.rows, self.features
        some = lambda *shape: pl.BlockSpec((step,) + shape, lambda i: (i + low // step,) + (0,) * len(shape))
        return pl.pallas_call(
            partial(input_kernel, self.tokens),
            grid=((high - low) // step,),
            in_specs=[some(r, 3 * f), some(r, f), some(r, 128), some(r, f), fixed(*one.shape), fixed(f, f), fixed(*vec.shape)]
            + [pl.BlockSpec(memory_space=pl.ANY)] * (into is not None),
            out_specs=some(self.tokens, f),
            out_shape=shaped(self.images, self.tokens, f),
            input_output_aliases={} if into is None else {7: 0},
            compiler_params=params(LIMIT),
        )(triple, n1, root, branch, one, two, vec, *([] if into is None else [into]))

    def turned(self, array):
        return array.reshape(-1, array.shape[-1]).T

    def weight_grads(self, core, devices, left, left_out, right, right_out, one, two, total, small, columns, tile=256):
        f, third = self.features, self.features // tile
        apart = f // devices % 8 == 0
        rows = [f // 2, f // 2] if apart else [f]

        def at(array, first, count):
            lead = array.shape[:-1]
            return pl.BlockSpec(lead + (tile,), lambda i, core: (0,) * len(lead) + (jnp.clip(i - first, 0, count - 1),))

        return pl.pallas_call(
            partial(weight_grad_kernel, self.slots, devices),
            grid_spec=pltpu.PrefetchScalarGridSpec(
                num_scalar_prefetch=1,
                grid=(4 * third + 1,),
                in_specs=[fixed(*left.shape), pl.BlockSpec(memory_space=pl.ANY), at(right, 0, 3 * third), at(right_out, 3 * third, third),
                          at(one, 0, 2 * third), at(two, 2 * third, third), at(total, 0, 3 * third), fixed(*small.shape), fixed(*columns.shape)],
                out_specs=[pl.BlockSpec((r, tile), lambda i, core: (0, i)) for r in rows],
                scratch_shapes=[pltpu.VMEM((f, 256), F32), pltpu.VMEM(left_out.shape, BF16), pltpu.SemaphoreType.DMA],
            ),
            out_shape=[shaped(r, 4 * f + 128) for r in rows],
            compiler_params=params(LIMIT),
        )(core[None], left, left_out, right, right_out, one, two, total, small, columns)


def expert_forward(pieces, weights, images):
    per, _, hidden = weights[0].shape
    size, count = pieces[0].shape[0], len(pieces)
    kept = shaped(2, per, size * count, hidden)
    made = pl.pallas_call(
        partial(expert_kernel, count, images),
        out_shape=[shaped(*p.shape) for p in pieces] + [kept, kept],
        compiler_params=params(SMALL, 0),
    )(*pieces, *weights)
    return made[:count], made[count:]


def expert_grads(pieces, kept, up, down):
    return pl.pallas_call(
        partial(expert_grad_kernel, len(pieces)),
        out_shape=[shaped(*up.shape, dtype=F32), shaped(*down.shape, dtype=F32), shaped(*up.shape), shaped(*down.shape)],
        compiler_params=params(SMALL, 0),
    )(*pieces, *kept)


def wide(a, width=128):
    return jnp.pad(a, ((0, 0), (0, width - a.shape[1])))


def body(grid, inputs, counts, ln1_gain, ln1_bias, w_qkv, w_out, ln2_gain, ln2_bias, phi, w_up, w_down, cotangent):
    me = grid.coords()
    batches, capacity, tokens, features = inputs.shape
    images = batches * capacity
    slots = phi.shape[1]
    per = slots // grid.m
    token = (jnp.arange(capacity)[None, :] < counts).astype(jnp.int32).reshape(-1)
    mixer = Mixer(grid, inputs, slots, token, me["e"])
    vectors = jnp.stack([ln1_gain, ln1_bias, ln2_gain, ln2_bias])
    vectors = dot(vectors, jnp.eye(4, dtype=BF16), 0, 0).astype(BF16)
    packed = jnp.concatenate([w_qkv, w_out, wide(jnp.concatenate([phi, vectors], axis=1))], axis=1)
    flow = Flow(gather_steps(grid, me, packed, 2 * features))
    cot, token = beside([flow], token, lambda token: mixer.padded_cotangent(cotangent))
    _, token = beside([flow], token)
    (n1, root), token = beside([flow], token, lambda token: mixer.standardize())
    other = Flow(neighbour_steps(grid, lax.optimization_barrier(([w_up, w_down], token))[0]))
    _, token = beside([flow], token)
    one, two = flow.value
    columns = two[:, 2 * features : 2 * features + padded(slots + 4, 16)].astype(F32)
    turned = columns.T
    vec = jnp.pad(turned[slots : slots + 4], ((0, 4), (0, 0)))

    made, token = beside([], token, lambda token: mixer.forward(n1, cot, one, two, vec))
    triple, mixed, hidden, logits, slot = made
    flow = Flow(out_steps(grid, slot.astype(BF16)))
    _, token = beside([flow, other], token)
    lefts, token = beside([flow], token, lambda token: (mixer.turned(n1), mixer.turned(mixed)))
    pieces = flow.value
    back, kept = expert_forward(pieces, [w_up, other.value[0], w_down, other.value[1]], images)
    flow = Flow(home_steps(grid, back))
    made, token = beside([flow], token, lambda token: expert_grads(pieces, kept, w_up, w_down))
    grad_up, grad_down, *others = made
    _, token = beside([flow], token)
    split = (per + 1) // 2
    other = Flow(neighbour_steps(grid, [others[0], others[1][:split]]))
    made, token = beside(
        [other], token, lambda token: mixer.backward(cot, triple, hidden, logits, flow.value.astype(F32), two, turned.astype(BF16), vec)
    )
    outs, branch, grad_triple, total, small = made
    rest = Flow(neighbour_steps(grid, lax.optimization_barrier((others[1][split:], token))[:1]))
    packed, token = beside([rest], token, lambda token: mixer.weight_grads(
        me["c"], grid.n * grid.m, *lefts, grad_triple, branch, one, two, total, wide(small.T), columns[:, slots : slots + 2]
    ))
    flow = Flow(reduce_steps(grid, me, packed, padded(packed[0].shape[1] // 2, 128)))
    grad_in, low, flows = None, 0, [flow]
    for count in SHARES:
        (grad_in, outs), token = beside(
            flows,
            token,
            lambda token: (mixer.input_back(
                low * images // 12, (low + count) * images // 12, grad_triple, n1, root, branch, one, two, vec, grad_in, max(images // 6, 1)
            ), outs),
        )
        low += count
    while not flow.done:
        _, token = beside([flow], token)
    sums = flow.value
    grad_up = grad_up + other.value[0].astype(F32)
    grad_down = grad_down + jnp.concatenate([other.value[1], rest.value[0]], axis=0).astype(F32)
    small = sums[:, 4 * features :]
    return (
        outs.reshape(inputs.shape),
        grad_in.reshape(inputs.shape),
        small[:, slots + 2],
        small[:, slots + 3],
        sums[:, : 3 * features],
        sums[:, 3 * features : 4 * features],
        small[:, slots],
        small[:, slots + 1],
        small[:, :slots],
        grad_up,
        grad_down,
    )


def solution(mesh):
    rows = P(BOTH, None)
    row = P(BOTH)
    image = P(None, BOTH, None, None)
    up, down = P("expert", None, "dp"), P("expert", "dp", None)
    grid = Grid(mesh.shape["dp"], mesh.shape["expert"])
    return jax.shard_map(
        partial(body, grid),
        mesh=mesh,
        in_specs=(image, P(None, BOTH), row, row, rows, rows, row, row, rows, up, down, image),
        out_specs=(image, image, row, row, rows, rows, row, row, rows, up, down),
        check_vma=False,
    )
```

```python
from functools import partial

import jax
import jax.numpy as jnp
from jax import lax
from jax.experimental import pallas as pl
from jax.experimental.pallas import tpu as pltpu
from jax.sharding import PartitionSpec as P

HEAD_DIM = 64
EPSILON = 1e-06
BOTH = ("dp", "expert")
F32, BF16 = jnp.float32, jnp.bfloat16
LOW = -1e30
LIMIT = 51
SHARES = (2, 8, 2)
SMALL = 51
GATHER_CUT = 1664


class Grid:
    def __init__(self, n, m):
        self.n, self.m = n, m
        self.size = {"z": n // 2, "y": 2, "x": m // 2, "c": 2, "e": m}

    def coords(self):
        d, e = lax.axis_index("dp"), lax.axis_index("expert")
        return {"z": d // 2, "y": d % 2, "x": e // 2, "c": e % 2, "e": e}

    def perm(self, axis, k):
        pairs = []
        for source in range(self.n * self.m):
            d, e = divmod(source, self.m)
            p = {"z": d // 2, "y": d % 2, "x": e // 2, "c": e % 2, "e": e}
            q = (p[axis] + k) % self.size[axis]
            if axis == "e":
                target = d * self.m + q
            else:
                p[axis] = q
                target = (p["z"] * 2 + p["y"]) * self.m + p["x"] * 2 + p["c"]
            pairs.append((source, target))
        return pairs

    def send(self, a, axis, k):
        return lax.ppermute(a, BOTH, self.perm(axis, k))

    def by_coordinate(self, me, axis, pieces, at=0):
        s = self.size[axis]
        if s == 2:
            return jnp.stack([jnp.where(me == p, pieces[0], pieces[1]) for p in range(2)], axis=at)
        if s <= 4:
            return jnp.stack([lax.select_n((me - p) % s, *pieces) for p in range(s)], axis=at)
        shape = pieces[0].shape
        out = jnp.zeros(shape[:at] + (s,) + shape[at:], pieces[0].dtype)
        for k in range(s):
            out = lax.dynamic_update_index_in_dim(out, pieces[k], (me - k) % s, at)
        return out

    def block(self, a, axis, me, k, at=0):
        return lax.dynamic_index_in_dim(a, (me[axis] + k) % self.size[axis], at, keepdims=False)


def joined(parts, axis):
    return jnp.concatenate(parts, axis=axis) if len(parts) > 1 else parts[0]


def send_on(grid, items):
    return [[grid.send(a, axis, k) for k in range(1, grid.size[axis])] for a, axis in items]


def gather_steps(grid, me, a, cut):
    got = yield send_on(grid, [(a, "z")])
    a = grid.by_coordinate(me["z"], "z", [a] + got[0])
    parts = [a[..., :cut], a[..., cut:]]
    for axes, at in (("yx", (1, 1)), ("xy", (2, 1)), ("cc", (3, 3))):
        got = yield send_on(grid, list(zip(parts, axes)))
        parts = [grid.by_coordinate(me[x], x, [p] + r, i) for p, r, x, i in zip(parts, got, axes, at)]
    return [p.reshape(-1, p.shape[-1]) for p in parts]


def reduce_steps(grid, me, a, cut):
    s = grid.size
    if len(a) == 1:
        a = a[0].reshape(s["z"], 2, s["x"], 2, -1, a[0].shape[1])
        own, other = (grid.block(a, "c", me, k, 3) for k in range(2))
    else:
        own, other = (p.reshape(s["z"], 2, s["x"], -1, p.shape[1]) for p in a)
    got = yield [[grid.send(other, "c", 1)]]
    a = (own.astype(F32) + got[0][0].astype(F32)).astype(BF16)
    parts = [a[..., :cut], a[..., cut:]]
    for axes, at in (("xy", (2, 1)), ("yx", (1, 1))):
        blocks = [[grid.block(p, x, me, k, i) for k in range(s[x])] for p, x, i in zip(parts, axes, at)]
        got = yield [[grid.send(b, x, k) for k, b in enumerate(bs) if k] for bs, x in zip(blocks, axes)]
        parts = [sum([b.astype(F32) for b in r], bs[0].astype(F32)).astype(BF16) for bs, r in zip(blocks, got)]
    a = jnp.concatenate(parts, axis=-1)
    blocks = [grid.block(a, "z", me, k) for k in range(s["z"])]
    got = yield [[grid.send(b, "z", k) for k, b in enumerate(blocks) if k]]
    return sum([b.astype(F32) for b in got[0]], blocks[0].astype(F32))


def swap_step(grid, blocks, axis, sign):
    received = yield [[grid.send(b, axis, sign * k) for k, b in enumerate(blocks) if k]]
    return list(blocks[:1]) + received[0]


def out_steps(grid, rows):
    r = rows.shape[0] // grid.m
    pieces = yield from swap_step(grid, [rows[k * r : (k + 1) * r] for k in range(grid.m)], "e", 1)
    own = jnp.concatenate(pieces, axis=0)
    return (yield from swap_step(grid, [own] * grid.size["z"], "z", 1))


def home_steps(grid, pieces):
    pieces = yield from swap_step(grid, pieces, "z", -1)
    own = sum([p.astype(F32) for p in pieces]).astype(BF16)
    r = own.shape[0] // grid.m
    pieces = yield from swap_step(grid, [own[k * r : (k + 1) * r] for k in range(grid.m)], "e", -1)
    return jnp.concatenate(pieces, axis=0)


def neighbour_steps(grid, arrays):
    received = yield [[grid.send(a, "y", 1) for a in arrays]]
    return received[0]


class Flow:
    def __init__(self, steps):
        self.steps, self.value, self.done = steps, None, False
        self.advance(None)

    def advance(self, received):
        try:
            self.waiting = self.steps.send(received)
        except StopIteration as end:
            self.value, self.done, self.waiting = end.value, True, None


def beside(flows, token, work=None):
    flows = [flow for flow in flows if flow is not None and not flow.done]
    made = work(token) if work else ()
    received, made, token = lax.optimization_barrier(([flow.waiting for flow in flows], made, token))
    for flow, arrays in zip(flows, received):
        flow.advance(arrays)
    return made, token


def dot(a, b, ca=1, cb=0):
    return lax.dot_general(a, b, (((ca,), (cb,)), ((), ())), preferred_element_type=F32)


def padded(v, step):
    return -(-v // step) * step


def standardized(v):
    width = v.shape[-1]
    mean = jnp.sum(v, axis=-1, keepdims=True) * (1.0 / width)
    center = v - mean
    root = lax.rsqrt(jnp.sum(center * center, axis=-1, keepdims=True) * (1.0 / width) + EPSILON)
    return center * root, mean, root


def lanes_of(head, width):
    return lax.broadcasted_iota(jnp.int32, (1, width), 1) // HEAD_DIM == head


def by_head(v, scale):
    width = v.shape[1]
    return jnp.concatenate([v * jnp.where(lanes_of(h, width), scale, 0.0).astype(BF16) for h in range(width // HEAD_DIM)], axis=0)


def own_columns(v):
    half = v.shape[0] // 2
    return jnp.where(lanes_of(0, v.shape[1]), v[:half], v[half:])


def routed(logits, tokens, slots):
    row = lax.broadcasted_iota(jnp.int32, logits.shape, 0)
    lane = lax.broadcasted_iota(jnp.int32, logits.shape, 1)
    valid = (row < tokens) & (lane < slots)
    kept = jnp.where(valid, logits, LOW)
    down = jnp.where(valid, jnp.exp(kept - jnp.max(kept, axis=0, keepdims=True)), 0.0)
    down_sum = jnp.sum(down, axis=0, keepdims=True)
    over_tokens = down * (1.0 / jnp.where(down_sum > 0, down_sum, 1.0))
    across = jnp.where(valid, jnp.exp(kept - jnp.max(kept, axis=1, keepdims=True)), 0.0)
    across_sum = jnp.sum(across, axis=1, keepdims=True)
    over_slots = across * (1.0 / jnp.where(across_sum > 0, across_sum, 1.0))
    return over_tokens, over_slots


def longer(v, count):
    return jnp.concatenate([v, jnp.zeros((count - v.shape[0], v.shape[1]), v.dtype)], axis=0)


def pad_kernel(tokens, cot_ref, out_ref):
    rows = out_ref.shape[1]
    for k in range(cot_ref.shape[1]):
        out_ref[k] = jnp.zeros((rows, out_ref.shape[2]), BF16)
        out_ref[k, :tokens] = cot_ref[0, k]


def standardize_kernel(tokens, x_ref, n1_ref, root_ref, pad_ref):
    @pl.when(pl.program_id(0) == 0)
    def _():
        pad_ref[...] = jnp.zeros_like(pad_ref)

    for k in range(x_ref.shape[1]):
        pad_ref[k, :tokens] = x_ref[0, k].astype(F32)
        n1, _, root = standardized(pad_ref[k])
        n1_ref[k] = n1.astype(BF16)
        root_ref[k] = jnp.broadcast_to(root, root_ref.shape[1:])


def forward_kernel(
    tokens, slots, place, live, x_ref, n1_ref, cot_ref, one_ref, two_ref, vec_ref,
    triple_ref, mixed_ref, hidden_ref, kept_ref, slot_ref, pad_ref,
):
    i = pl.program_id(0)
    rows, features = pad_ref.shape
    keys = padded(rows, 128)

    @pl.when(i == 0)
    def _():
        pad_ref[...] = jnp.zeros_like(pad_ref)

    @pl.when(live[i] == 0)
    def _():
        mixed_ref[...] = jnp.zeros_like(mixed_ref)
        for s in range(slots):
            slot_ref[pl.ds(place(live, s, i), 1)] = jnp.zeros((1, slot_ref.shape[1]), F32)

    @pl.when(live[i] != 0)
    def _():
        pad_ref[:tokens] = x_ref[0, 0].astype(F32)
        normed = (n1_ref[0].astype(F32) * vec_ref[0:1] + vec_ref[1:2]).astype(BF16)
        for part in range(3):
            cut = slice(part * features, (part + 1) * features)
            weights = one_ref[:, cut] if part < 2 else two_ref[:, :features]
            triple_ref[0, :, cut] = dot(normed, weights).astype(BF16)
        bias = jnp.where(lax.broadcasted_iota(jnp.int32, (1, keys), 1) < tokens, 0.0, LOW)
        for low in range(0, features, 128):
            q = triple_ref[0, :, low : low + 128]
            k = longer(triple_ref[0, :, features + low : features + low + 128], keys)
            v = longer(triple_ref[0, :, 2 * features + low : 2 * features + low + 128], keys)
            scores = dot(by_head(q, HEAD_DIM**-0.5), k, 1, 1) + bias
            powers = jnp.exp(scores - jnp.max(scores, axis=1, keepdims=True))
            total = dot(powers.astype(BF16), v) * (1.0 / jnp.sum(powers, axis=1, keepdims=True))
            mixed_ref[0, :, low : low + 128] = own_columns(total).astype(BF16)
        hidden = pad_ref[...] + dot(mixed_ref[0], two_ref[:, features : 2 * features])
        hidden_ref[0] = hidden
        n2, mean, root = standardized(hidden)
        normed_two = (n2 * vec_ref[2:3] + vec_ref[3:4]).astype(BF16)
        logits = dot(normed_two, two_ref[:, 2 * features :])
        dispatch, combine = routed(logits, tokens, slots)
        for part, value in enumerate((dispatch, combine, mean, root)):
            kept_ref[0, :, part * 128 : (part + 1) * 128] = jnp.broadcast_to(value, (rows, 128))
        slot_in = dot(dispatch.astype(BF16), normed_two, 0, 0)
        grad_slot = dot(combine.astype(BF16), cot_ref[0], 0, 0)
        for s in range(slots):
            slot_ref[pl.ds(place(live, s, i), 1), :features] = slot_in[s : s + 1]
            slot_ref[pl.ds(place(live, s, i), 1), features:] = grad_slot[s : s + 1]


def expert_kernel(pieces, images, *refs):
    rows_in, (up, up_other, down, down_other) = refs[:pieces], refs[pieces : pieces + 4]
    rows_out, (active_ref, slope_ref) = refs[pieces + 4 : 2 * pieces + 4], refs[2 * pieces + 4 :]
    per, features = up.shape[:2]
    both = jnp.concatenate([r[...] for r in rows_in], axis=0)
    rows, grads = both[:, :features], both[:, features:]
    index = lax.broadcasted_iota(jnp.int32, (rows.shape[0], 1), 0)
    total = total_back = 0.0
    for part, (up_ref, down_ref) in enumerate(((up, down), (up_other, down_other))):
        for j in range(per):
            mine = (index // images) % per == j
            pre = dot(rows, up_ref[j])
            phi = 0.5 * (1.0 + lax.erf(pre * (0.5**0.5)))
            density = jnp.exp(pre * pre * -0.5) * (0.5 / jnp.pi) ** 0.5
            active = jnp.where(mine, pre * phi, 0.0).astype(BF16)
            grad = dot(grads, down_ref[j], 1, 1)
            grad = jnp.where(mine, grad * (phi + pre * density), 0.0).astype(BF16)
            active_ref[part, j] = active
            slope_ref[part, j] = grad
            total = total + dot(active, down_ref[j])
            total_back = total_back + dot(grad, up_ref[j], 1, 1)
    size = rows_in[0].shape[0]
    for k, ref in enumerate(rows_out):
        ref[:, :features] = total[k * size : (k + 1) * size].astype(BF16)
        ref[:, features:] = total_back[k * size : (k + 1) * size].astype(BF16)


def expert_grad_kernel(pieces, *refs):
    rows_in, (active_ref, slope_ref) = refs[:pieces], refs[pieces : pieces + 2]
    outs = refs[pieces + 2 :]
    features = outs[0].shape[1]
    both = jnp.concatenate([r[...] for r in rows_in], axis=0)
    rows, grads = both[:, :features].T, both[:, features:]
    for part in range(2):
        up_ref, down_ref = outs[2 * part : 2 * part + 2]
        for j in range(up_ref.shape[0]):
            up_ref[j] = dot(rows, slope_ref[part, j]).astype(up_ref.dtype)
            down_ref[j] = dot(active_ref[part, j], grads, 0, 0).astype(down_ref.dtype)


def backward_kernel(
    tokens, slots, place, live, cot_ref, triple_ref, hidden_ref, kept_ref, home_ref, two_ref, phit_ref, vec_ref,
    out_ref, branch_ref, grad_ref, total_ref, small_ref, gm_ref,
):
    i = pl.program_id(0)
    rows, features = hidden_ref.shape[1:]
    keys = gm_ref.shape[0]

    @pl.when(i == 0)
    def _():
        gm_ref[...] = jnp.zeros_like(gm_ref)
        total_ref[...] = jnp.zeros_like(total_ref)
        small_ref[...] = jnp.zeros_like(small_ref)

    @pl.when(live[i] == 0)
    def _():
        out_ref[...] = jnp.zeros_like(out_ref)
        branch_ref[...] = jnp.zeros_like(branch_ref)
        grad_ref[...] = jnp.zeros_like(grad_ref)

    @pl.when(live[i] != 0)
    def _():
        hidden = hidden_ref[0]
        over_tokens, over_slots = kept_ref[0, :, :slots], kept_ref[0, :, 128 : 128 + slots]
        mean, root = (jnp.concatenate([kept_ref[0, :, low : low + 128]] * (features // 128), axis=1) for low in (256, 384))
        n2 = (hidden - mean) * root
        gain = vec_ref[2:3]
        normed_two = (n2 * gain + vec_ref[3:4]).astype(BF16)
        dispatch, combine = over_tokens.astype(BF16), over_slots.astype(BF16)
        home = jnp.concatenate([home_ref[pl.ds(place(live, s, i), 1)] for s in range(slots)], axis=0).astype(BF16)
        slot_out, grad_in = home[:, :features], home[:, features:]
        cot = cot_ref[0].astype(F32)
        result = hidden + dot(combine, slot_out)
        out_ref[0] = result[:tokens].astype(BF16)
        grad_combine = dot(cot_ref[0], slot_out, 1, 1)
        grad_dispatch = dot(normed_two, grad_in, 1, 1)
        grad_logits = over_tokens * (grad_dispatch - jnp.sum(grad_dispatch * over_tokens, axis=0, keepdims=True))
        grad_logits += over_slots * (grad_combine - jnp.sum(grad_combine * over_slots, axis=1, keepdims=True))
        grad_logits = grad_logits.astype(BF16)
        grad_two = dot(dispatch, grad_in) + dot(grad_logits, phit_ref[:slots])
        small_ref[:slots] += dot(grad_logits, normed_two, 0, 0)
        small_ref[slots : slots + 1] += jnp.sum(grad_two * n2, axis=0, keepdims=True)
        small_ref[slots + 1 : slots + 2] += jnp.sum(grad_two, axis=0, keepdims=True)
        u = grad_two * gain
        inner = u - jnp.sum(u, axis=-1, keepdims=True) * (1.0 / features)
        inner = inner - n2 * (jnp.sum(u * n2, axis=-1, keepdims=True) * (1.0 / features))
        branch = (cot + root * inner).astype(BF16)
        branch_ref[0] = branch
        gm_ref[:rows] = dot(branch, two_ref[:, features : 2 * features], 1, 1).astype(BF16)
        valid = lax.broadcasted_iota(jnp.int32, (rows, 1), 0) < tokens
        for low in range(0, features, 256):
            q = longer(triple_ref[0, :, low : low + 256], keys)
            k = triple_ref[0, :, features + low : features + low + 256]
            v = triple_ref[0, :, 2 * features + low : 2 * features + low + 256]
            gm = gm_ref[:, low : low + 256]
            scores_all = dot(by_head(k, HEAD_DIM**-0.5), q, 1, 1)
            grad_all = dot(by_head(v, 1.0), gm, 1, 1)
            for pair in range(2):
                attention, grad_scores = [], []
                for head in (2 * pair, 2 * pair + 1):
                    cut = slice(head * rows, (head + 1) * rows)
                    scores = jnp.where(valid, scores_all[cut], LOW)
                    powers = jnp.exp(scores - jnp.max(scores, axis=0, keepdims=True))
                    inverse = 1.0 / jnp.sum(powers, axis=0, keepdims=True)
                    mean = jnp.sum(grad_all[cut] * powers, axis=0, keepdims=True) * inverse
                    powers = powers * inverse
                    attention.append(powers.astype(BF16))
                    grad_scores.append((powers * (grad_all[cut] - mean)).astype(BF16))
                own = slice(pair * 128, (pair + 1) * 128)
                grads = (
                    own_columns(dot(jnp.concatenate([g.T for g in grad_scores], axis=0), k[:, own]))[:rows] * HEAD_DIM**-0.5,
                    own_columns(dot(jnp.concatenate(grad_scores, axis=0), q[:, own])) * HEAD_DIM**-0.5,
                    own_columns(dot(jnp.concatenate(attention, axis=0), gm[:, own])),
                )
                for part, grad in enumerate(grads):
                    cut = slice(part * features + low + pair * 128, part * features + low + (pair + 1) * 128)
                    grad_ref[0, :, cut] = grad.astype(BF16)
                    total_ref[0:1, cut] += jnp.sum(grad, axis=0, keepdims=True)


def input_kernel(tokens, triple_ref, n1_ref, root_ref, branch_ref, one_ref, two_ref, vec_ref, *refs):
    out_ref = refs[-1]
    count, rows, features = branch_ref.shape
    flat = lambda a: a.reshape(count * rows, a.shape[-1])
    triple, n1, root = flat(triple_ref[...]), flat(n1_ref[...]).astype(F32), flat(root_ref[...])[:, :1]
    v = dot(triple[:, : 2 * features], one_ref[...], 1, 1) + dot(triple[:, 2 * features :], two_ref[...], 1, 1)
    v = v * vec_ref[0:1]
    inner = v - jnp.sum(v, axis=-1, keepdims=True) * (1.0 / features)
    inner = inner - n1 * (jnp.sum(v * n1, axis=-1, keepdims=True) * (1.0 / features))
    grad = flat(branch_ref[...]).astype(F32) + root * inner
    for k in range(count):
        out_ref[k] = grad[k * rows : k * rows + tokens].astype(BF16)


def weight_grad_kernel(slots, devices, core, left_ref, left_out_hbm, right_ref, right_out_ref, one_ref, two_ref, total_ref, small_ref, columns_ref, *refs):
    *outs, norm_ref, left_out_ref, arrived = refs
    i, features, tile = pl.program_id(0), left_ref.shape[0], outs[0].shape[1]
    third = features // tile

    def store(value):
        if len(outs) == 1:
            outs[0][...] = value.astype(BF16)
            return
        value = value.reshape(devices // 2, 2, -1, tile)
        for k, ref in enumerate(outs):
            half = jnp.where(core[0] == k, value[:, 0], value[:, 1])
            ref[...] = half.reshape(-1, tile).astype(BF16)

    later = pltpu.make_async_copy(left_out_hbm, left_out_ref, arrived)

    @pl.when(i == 0)
    def _():
        later.start()
        norm_ref[...] = jnp.zeros_like(norm_ref)

    @pl.when(i == 3 * third)
    def _():
        later.wait()

    def tokens(ref):
        return ref[...].reshape(-1, tile)

    def wide_part(w_ref):
        product = dot(left_ref[...], tokens(right_ref))
        total = total_ref[0:1]
        store(product * columns_ref[:, 0:1] + columns_ref[:, 1:2] * total)
        for low in range(0, tile, 128):
            cut = slice(low, low + 128)
            weights = w_ref[:, cut].astype(F32)
            norm_ref[:, :128] += weights * product[:, cut]
            norm_ref[:, 128:] += weights * total[:, cut]

    @pl.when(i < 2 * third)
    def _():
        wide_part(one_ref)

    @pl.when((i >= 2 * third) & (i < 3 * third))
    def _():
        wide_part(two_ref)

    @pl.when((i >= 3 * third) & (i < 4 * third))
    def _():
        store(dot(left_out_ref[...], tokens(right_out_ref)))

    @pl.when(i == 4 * third)
    def _():
        lane = lax.broadcasted_iota(jnp.int32, (features, 128), 1)
        gain = jnp.sum(norm_ref[:, :128], axis=1, keepdims=True)
        bias = jnp.sum(norm_ref[:, 128:], axis=1, keepdims=True)
        narrow = jnp.where(lane == slots + 2, gain, jnp.where(lane == slots + 3, bias, small_ref[...]))
        store(jnp.concatenate([narrow] * (tile // 128), axis=1))


def own(*shape, low=0):
    return pl.BlockSpec((1,) + shape, lambda i, live: (i + low,) + (0,) * len(shape))


def fixed(*shape):
    return pl.BlockSpec(shape, lambda i, *live: (0,) * len(shape), pipeline_mode=pl.Buffered(1))


def shaped(*shape, dtype=BF16):
    return jax.ShapeDtypeStruct(shape, dtype)


def params(mib, axes=1):
    return pltpu.CompilerParams(vmem_limit_bytes=mib * 1024 * 1024, dimension_semantics=("arbitrary",) * axes)


def by_image(kernel, images, in_specs, out_specs, out_shape, scratch, flops, mib):
    return pl.pallas_call(
        kernel,
        grid_spec=pltpu.PrefetchScalarGridSpec(
            num_scalar_prefetch=1, grid=(images,), in_specs=in_specs, out_specs=out_specs, scratch_shapes=scratch
        ),
        out_shape=out_shape,
        compiler_params=params(mib),
        cost_estimate=pl.CostEstimate(flops=flops, bytes_accessed=flops // 1000, transcendentals=0),
    )


class Mixer:
    def __init__(self, grid, inputs, slots, live, expert):
        self.inputs, self.slots = inputs, slots
        self.live = jnp.concatenate([live, expert[None]])
        self.owners, self.per = grid.m, slots // grid.m
        self.batches, self.capacity, self.tokens, self.features = inputs.shape
        self.images = self.batches * self.capacity
        self.rows, self.keys = padded(self.tokens, 16), padded(self.tokens, 128)
        self.pad = pltpu.VMEM((self.rows, self.features), F32)
        self.flops = self.rows * self.features * self.features * 8

    def place(self, live, s, i):
        owner = lax.rem(s // self.per + self.owners - live[self.images], self.owners)
        return (owner * self.per + s % self.per) * self.images + i

    def image(self, low):
        return pl.BlockSpec((1, 1, self.tokens, self.features), lambda i, live: ((i + low) // self.capacity, (i + low) % self.capacity, 0, 0))

    def made(self, low=0):
        return pl.BlockSpec((1, self.tokens, self.features), lambda i, live: (i + low, 0, 0))

    def padded_cotangent(self, cotangent):
        n, c, r, f = self.images, self.capacity, self.rows, self.features
        return pl.pallas_call(
            partial(pad_kernel, self.tokens),
            grid=(self.batches,),
            in_specs=[pl.BlockSpec((1, c, self.tokens, f), lambda i: (i, 0, 0, 0))],
            out_specs=pl.BlockSpec((c, r, f), lambda i: (i, 0, 0)),
            out_shape=shaped(n, r, f),
            compiler_params=params(LIMIT),
        )(cotangent)

    def standardize(self):
        n, c, r, f = self.images, self.capacity, self.rows, self.features
        group = lambda *shape: pl.BlockSpec((c,) + shape, lambda i: (i,) + (0,) * len(shape))
        return pl.pallas_call(
            partial(standardize_kernel, self.tokens),
            grid=(self.batches,),
            in_specs=[pl.BlockSpec((1, c, self.tokens, f), lambda i: (i, 0, 0, 0))],
            out_specs=[group(r, f), group(r, 128)],
            out_shape=[shaped(n, r, f), shaped(n, r, 128, dtype=F32)],
            scratch_shapes=[pltpu.VMEM((c, r, f), F32)],
            compiler_params=params(LIMIT),
        )(self.inputs)

    def forward(self, n1, cot, one, two, vec):
        n, r, f = self.images, self.rows, self.features
        return by_image(
            partial(forward_kernel, self.tokens, self.slots, self.place), n,
            [self.image(0), own(r, f), own(r, f), fixed(*one.shape), fixed(*two.shape), fixed(*vec.shape)],
            [own(r, 3 * f), own(r, f), own(r, f), own(r, 512), fixed(self.slots * n, 2 * f)],
            [shaped(n, r, 3 * f), shaped(n, r, f), shaped(n, r, f, dtype=F32), shaped(n, r, 512, dtype=F32), shaped(self.slots * n, 2 * f, dtype=F32)],
            [self.pad], 3 * n * self.flops, LIMIT,
        )(self.live, self.inputs, n1, cot, one, two, vec)

    def backward(self, cot, triple, hidden, logits, home, two, phit, vec):
        n, r, f = self.images, self.rows, self.features
        small = padded(self.slots + 2, 8)
        return by_image(
            partial(backward_kernel, self.tokens, self.slots, self.place), n,
            [own(r, f), own(r, 3 * f), own(r, f), own(r, 512), fixed(self.slots * n, 2 * f), fixed(*two.shape), fixed(*phit.shape), fixed(*vec.shape)],
            [self.made(), own(r, f), own(r, 3 * f), fixed(8, 3 * f), fixed(small, f)],
            [shaped(n, self.tokens, f), shaped(n, r, f), shaped(n, r, 3 * f), shaped(8, 3 * f, dtype=F32), shaped(small, f, dtype=F32)],
            [pltpu.VMEM((self.keys, f), BF16)], 3 * n * self.flops, LIMIT,
        )(self.live, cot, triple, hidden, logits, home, two, phit, vec)

    def input_back(self, low, high, triple, n1, root, branch, one, two, vec, into, step):
        r, f = self.rows, self.features
        some = lambda *shape: pl.BlockSpec((step,) + shape, lambda i: (i + low // step,) + (0,) * len(shape))
        return pl.pallas_call(
            partial(input_kernel, self.tokens),
            grid=((high - low) // step,),
            in_specs=[some(r, 3 * f), some(r, f), some(r, 128), some(r, f), fixed(*one.shape), fixed(f, f), fixed(*vec.shape)]
            + [pl.BlockSpec(memory_space=pl.ANY)] * (into is not None),
            out_specs=some(self.tokens, f),
            out_shape=shaped(self.images, self.tokens, f),
            input_output_aliases={} if into is None else {7: 0},
            compiler_params=params(LIMIT),
        )(triple, n1, root, branch, one, two, vec, *([] if into is None else [into]))

    def turned(self, array):
        return array.reshape(-1, array.shape[-1]).T

    def weight_grads(self, core, devices, left, left_out, right, right_out, one, two, total, small, columns, tile=256):
        f, third = self.features, self.features // tile
        apart = f // devices % 8 == 0
        rows = [f // 2, f // 2] if apart else [f]

        def at(array, first, count):
            lead = array.shape[:-1]
            return pl.BlockSpec(lead + (tile,), lambda i, core: (0,) * len(lead) + (jnp.clip(i - first, 0, count - 1),))

        return pl.pallas_call(
            partial(weight_grad_kernel, self.slots, devices),
            grid_spec=pltpu.PrefetchScalarGridSpec(
                num_scalar_prefetch=1,
                grid=(4 * third + 1,),
                in_specs=[fixed(*left.shape), pl.BlockSpec(memory_space=pl.ANY), at(right, 0, 3 * third), at(right_out, 3 * third, third),
                          at(one, 0, 2 * third), at(two, 2 * third, third), at(total, 0, 3 * third), fixed(*small.shape), fixed(*columns.shape)],
                out_specs=[pl.BlockSpec((r, tile), lambda i, core: (0, i)) for r in rows],
                scratch_shapes=[pltpu.VMEM((f, 256), F32), pltpu.VMEM(left_out.shape, BF16), pltpu.SemaphoreType.DMA],
            ),
            out_shape=[shaped(r, 4 * f + 128) for r in rows],
            compiler_params=params(LIMIT),
        )(core[None], left, left_out, right, right_out, one, two, total, small, columns)


def expert_forward(pieces, weights, images):
    per, _, hidden = weights[0].shape
    size, count = pieces[0].shape[0], len(pieces)
    kept = shaped(2, per, size * count, hidden)
    made = pl.pallas_call(
        partial(expert_kernel, count, images),
        out_shape=[shaped(*p.shape) for p in pieces] + [kept, kept],
        compiler_params=params(SMALL, 0),
    )(*pieces, *weights)
    return made[:count], made[count:]


def expert_grads(pieces, kept, up, down):
    return pl.pallas_call(
        partial(expert_grad_kernel, len(pieces)),
        out_shape=[shaped(*up.shape, dtype=F32), shaped(*down.shape, dtype=F32), shaped(*up.shape), shaped(*down.shape)],
        compiler_params=params(SMALL, 0),
    )(*pieces, *kept)


def wide(a, width=128):
    return jnp.pad(a, ((0, 0), (0, width - a.shape[1])))


def body(grid, inputs, counts, ln1_gain, ln1_bias, w_qkv, w_out, ln2_gain, ln2_bias, phi, w_up, w_down, cotangent):
    me = grid.coords()
    batches, capacity, tokens, features = inputs.shape
    images = batches * capacity
    slots = phi.shape[1]
    per = slots // grid.m
    token = (jnp.arange(capacity)[None, :] < counts).astype(jnp.int32).reshape(-1)
    mixer = Mixer(grid, inputs, slots, token, me["e"])
    vectors = jnp.stack([ln1_gain, ln1_bias, ln2_gain, ln2_bias])
    vectors = dot(vectors, jnp.eye(4, dtype=BF16), 0, 0).astype(BF16)
    packed = jnp.concatenate([w_qkv, w_out, wide(jnp.concatenate([phi, vectors], axis=1))], axis=1)
    flow = Flow(gather_steps(grid, me, packed, 2 * features))
    cot, token = beside([flow], token, lambda token: mixer.padded_cotangent(cotangent))
    _, token = beside([flow], token)
    (n1, root), token = beside([flow], token, lambda token: mixer.standardize())
    other = Flow(neighbour_steps(grid, lax.optimization_barrier(([w_up, w_down], token))[0]))
    _, token = beside([flow], token)
    one, two = flow.value
    columns = two[:, 2 * features : 2 * features + padded(slots + 4, 16)].astype(F32)
    turned = columns.T
    vec = jnp.pad(turned[slots : slots + 4], ((0, 4), (0, 0)))

    made, token = beside([], token, lambda token: mixer.forward(n1, cot, one, two, vec))
    triple, mixed, hidden, logits, slot = made
    flow = Flow(out_steps(grid, slot.astype(BF16)))
    _, token = beside([flow, other], token)
    lefts, token = beside([flow], token, lambda token: (mixer.turned(n1), mixer.turned(mixed)))
    pieces = flow.value
    back, kept = expert_forward(pieces, [w_up, other.value[0], w_down, other.value[1]], images)
    flow = Flow(home_steps(grid, back))
    made, token = beside([flow], token, lambda token: expert_grads(pieces, kept, w_up, w_down))
    grad_up, grad_down, *others = made
    _, token = beside([flow], token)
    split = (per + 1) // 2
    other = Flow(neighbour_steps(grid, [others[0], others[1][:split]]))
    made, token = beside(
        [other], token, lambda token: mixer.backward(cot, triple, hidden, logits, flow.value.astype(F32), two, turned.astype(BF16), vec)
    )
    outs, branch, grad_triple, total, small = made
    rest = Flow(neighbour_steps(grid, lax.optimization_barrier((others[1][split:], token))[:1]))
    packed, token = beside([rest], token, lambda token: mixer.weight_grads(
        me["c"], grid.n * grid.m, *lefts, grad_triple, branch, one, two, total, wide(small.T), columns[:, slots : slots + 2]
    ))
    flow = Flow(reduce_steps(grid, me, packed, padded(packed[0].shape[1] // 2, 128)))
    grad_in, low, flows = None, 0, [flow]
    for count in SHARES:
        (grad_in, outs), token = beside(
            flows,
            token,
            lambda token: (mixer.input_back(
                low * images // 12, (low + count) * images // 12, grad_triple, n1, root, branch, one, two, vec, grad_in, max(images // 6, 1)
            ), outs),
        )
        low += count
    while not flow.done:
        _, token = beside([flow], token)
    sums = flow.value
    grad_up = grad_up + other.value[0].astype(F32)
    grad_down = grad_down + jnp.concatenate([other.value[1], rest.value[0]], axis=0).astype(F32)
    small = sums[:, 4 * features :]
    return (
        outs.reshape(inputs.shape),
        grad_in.reshape(inputs.shape),
        small[:, slots + 2],
        small[:, slots + 3],
        sums[:, : 3 * features],
        sums[:, 3 * features : 4 * features],
        small[:, slots],
        small[:, slots + 1],
        small[:, :slots],
        grad_up,
        grad_down,
    )


def solution(mesh):
    rows = P(BOTH, None)
    row = P(BOTH)
    image = P(None, BOTH, None, None)
    up, down = P("expert", None, "dp"), P("expert", "dp", None)
    grid = Grid(mesh.shape["dp"], mesh.shape["expert"])
    return jax.shard_map(
        partial(body, grid),
        mesh=mesh,
        in_specs=(image, P(None, BOTH), row, row, rows, rows, row, row, rows, up, down, image),
        out_specs=(image, image, row, row, rows, rows, row, row, rows, up, down),
        check_vma=False,
    )
```

```python
from functools import partial

import jax
import jax.numpy as jnp
from jax import lax
from jax.experimental import pallas as pl
from jax.experimental.pallas import tpu as pltpu
from jax.sharding import PartitionSpec as P

HEAD_DIM = 64
EPSILON = 1e-06
BOTH = ("dp", "expert")
F32, BF16 = jnp.float32, jnp.bfloat16
LOW = -1e30
LIMIT = 51
SHARES = (2, 8, 2)
SMALL = 51
GATHER_CUT = 1664


class Grid:
    def __init__(self, n, m):
        self.n, self.m = n, m
        self.size = {"z": n // 2, "y": 2, "x": m // 2, "c": 2, "e": m}

    def coords(self):
        d, e = lax.axis_index("dp"), lax.axis_index("expert")
        return {"z": d // 2, "y": d % 2, "x": e // 2, "c": e % 2, "e": e}

    def perm(self, axis, k):
        pairs = []
        for source in range(self.n * self.m):
            d, e = divmod(source, self.m)
            p = {"z": d // 2, "y": d % 2, "x": e // 2, "c": e % 2, "e": e}
            q = (p[axis] + k) % self.size[axis]
            if axis == "e":
                target = d * self.m + q
            else:
                p[axis] = q
                target = (p["z"] * 2 + p["y"]) * self.m + p["x"] * 2 + p["c"]
            pairs.append((source, target))
        return pairs

    def send(self, a, axis, k):
        return lax.ppermute(a, BOTH, self.perm(axis, k))

    def by_coordinate(self, me, axis, pieces, at=0):
        s = self.size[axis]
        if s == 2:
            return jnp.stack([jnp.where(me == p, pieces[0], pieces[1]) for p in range(2)], axis=at)
        if s <= 4:
            return jnp.stack([lax.select_n((me - p) % s, *pieces) for p in range(s)], axis=at)
        shape = pieces[0].shape
        out = jnp.zeros(shape[:at] + (s,) + shape[at:], pieces[0].dtype)
        for k in range(s):
            out = lax.dynamic_update_index_in_dim(out, pieces[k], (me - k) % s, at)
        return out

    def block(self, a, axis, me, k, at=0):
        return lax.dynamic_index_in_dim(a, (me[axis] + k) % self.size[axis], at, keepdims=False)


def joined(parts, axis):
    return jnp.concatenate(parts, axis=axis) if len(parts) > 1 else parts[0]


def send_on(grid, items):
    return [[grid.send(a, axis, k) for k in range(1, grid.size[axis])] for a, axis in items]


def gather_steps(grid, me, a, cut):
    got = yield send_on(grid, [(a, "z")])
    a = grid.by_coordinate(me["z"], "z", [a] + got[0])
    parts = [a[..., :cut], a[..., cut:]]
    for axes, at in (("yx", (1, 1)), ("xy", (2, 1)), ("cc", (3, 3))):
        got = yield send_on(grid, list(zip(parts, axes)))
        parts = [grid.by_coordinate(me[x], x, [p] + r, i) for p, r, x, i in zip(parts, got, axes, at)]
    return [p.reshape(-1, p.shape[-1]) for p in parts]


def reduce_steps(grid, me, a, cut):
    s = grid.size
    if len(a) == 1:
        a = a[0].reshape(s["z"], 2, s["x"], 2, -1, a[0].shape[1])
        own, other = (grid.block(a, "c", me, k, 3) for k in range(2))
    else:
        own, other = (p.reshape(s["z"], 2, s["x"], -1, p.shape[1]) for p in a)
    got = yield [[grid.send(other, "c", 1)]]
    a = (own.astype(F32) + got[0][0].astype(F32)).astype(BF16)
    parts = [a[..., :cut], a[..., cut:]]
    for axes, at in (("xy", (2, 1)), ("yx", (1, 1))):
        blocks = [[grid.block(p, x, me, k, i) for k in range(s[x])] for p, x, i in zip(parts, axes, at)]
        got = yield [[grid.send(b, x, k) for k, b in enumerate(bs) if k] for bs, x in zip(blocks, axes)]
        parts = [sum([b.astype(F32) for b in r], bs[0].astype(F32)).astype(BF16) for bs, r in zip(blocks, got)]
    a = jnp.concatenate(parts, axis=-1)
    blocks = [grid.block(a, "z", me, k) for k in range(s["z"])]
    got = yield [[grid.send(b, "z", k) for k, b in enumerate(blocks) if k]]
    return sum([b.astype(F32) for b in got[0]], blocks[0].astype(F32))


def swap_step(grid, blocks, axis, sign):
    received = yield [[grid.send(b, axis, sign * k) for k, b in enumerate(blocks) if k]]
    return list(blocks[:1]) + received[0]


def out_steps(grid, rows):
    r = rows.shape[0] // grid.m
    pieces = yield from swap_step(grid, [rows[k * r : (k + 1) * r] for k in range(grid.m)], "e", 1)
    own = jnp.concatenate(pieces, axis=0)
    return (yield from swap_step(grid, [own] * grid.size["z"], "z", 1))


def home_steps(grid, pieces):
    pieces = yield from swap_step(grid, pieces, "z", -1)
    own = sum([p.astype(F32) for p in pieces]).astype(BF16)
    r = own.shape[0] // grid.m
    pieces = yield from swap_step(grid, [own[k * r : (k + 1) * r] for k in range(grid.m)], "e", -1)
    return jnp.concatenate(pieces, axis=0)


def neighbour_steps(grid, arrays):
    received = yield [[grid.send(a, "y", 1) for a in arrays]]
    return received[0]


class Flow:
    def __init__(self, steps):
        self.steps, self.value, self.done = steps, None, False
        self.advance(None)

    def advance(self, received):
        try:
            self.waiting = self.steps.send(received)
        except StopIteration as end:
            self.value, self.done, self.waiting = end.value, True, None


def beside(flows, token, work=None):
    flows = [flow for flow in flows if flow is not None and not flow.done]
    made = work(token) if work else ()
    received, made, token = lax.optimization_barrier(([flow.waiting for flow in flows], made, token))
    for flow, arrays in zip(flows, received):
        flow.advance(arrays)
    return made, token


def dot(a, b, ca=1, cb=0):
    return lax.dot_general(a, b, (((ca,), (cb,)), ((), ())), preferred_element_type=F32)


def padded(v, step):
    return -(-v // step) * step


def standardized(v):
    width = v.shape[-1]
    mean = jnp.sum(v, axis=-1, keepdims=True) * (1.0 / width)
    center = v - mean
    root = lax.rsqrt(jnp.sum(center * center, axis=-1, keepdims=True) * (1.0 / width) + EPSILON)
    return center * root, mean, root


def lanes_of(head, width):
    return lax.broadcasted_iota(jnp.int32, (1, width), 1) // HEAD_DIM == head


def by_head(v, scale):
    width = v.shape[1]
    return jnp.concatenate([v * jnp.where(lanes_of(h, width), scale, 0.0).astype(BF16) for h in range(width // HEAD_DIM)], axis=0)


def own_columns(v):
    half = v.shape[0] // 2
    return jnp.where(lanes_of(0, v.shape[1]), v[:half], v[half:])


def routed(logits, tokens, slots):
    row = lax.broadcasted_iota(jnp.int32, logits.shape, 0)
    lane = lax.broadcasted_iota(jnp.int32, logits.shape, 1)
    valid = (row < tokens) & (lane < slots)
    kept = jnp.where(valid, logits, LOW)
    down = jnp.where(valid, jnp.exp(kept - jnp.max(kept, axis=0, keepdims=True)), 0.0)
    down_sum = jnp.sum(down, axis=0, keepdims=True)
    over_tokens = down * (1.0 / jnp.where(down_sum > 0, down_sum, 1.0))
    across = jnp.where(valid, jnp.exp(kept - jnp.max(kept, axis=1, keepdims=True)), 0.0)
    across_sum = jnp.sum(across, axis=1, keepdims=True)
    over_slots = across * (1.0 / jnp.where(across_sum > 0, across_sum, 1.0))
    return over_tokens, over_slots


def longer(v, count):
    return jnp.concatenate([v, jnp.zeros((count - v.shape[0], v.shape[1]), v.dtype)], axis=0)


def pad_kernel(tokens, cot_ref, out_ref):
    rows = out_ref.shape[1]
    for k in range(cot_ref.shape[1]):
        full = tokens // 16 * 16
        out_ref[k, full:] = jnp.zeros((rows - full, out_ref.shape[2]), BF16)
        out_ref[k, :tokens] = cot_ref[0, k]


def standardize_kernel(tokens, x_ref, n1_ref, root_ref, pad_ref):
    @pl.when(pl.program_id(0) == 0)
    def _():
        pad_ref[...] = jnp.zeros_like(pad_ref)

    for k in range(x_ref.shape[1]):
        pad_ref[k, :tokens] = x_ref[0, k].astype(F32)
        n1, _, root = standardized(pad_ref[k])
        n1_ref[k] = n1.astype(BF16)
        root_ref[k] = jnp.broadcast_to(root, root_ref.shape[1:])


def forward_kernel(
    tokens, slots, place, live, x_ref, n1_ref, cot_ref, one_ref, two_ref, vec_ref,
    triple_ref, mixed_ref, hidden_ref, kept_ref, slot_ref, pad_ref,
):
    i = pl.program_id(0)
    rows, features = pad_ref.shape
    keys = padded(rows, 128)

    @pl.when(i == 0)
    def _():
        pad_ref[...] = jnp.zeros_like(pad_ref)

    @pl.when(live[i] == 0)
    def _():
        mixed_ref[...] = jnp.zeros_like(mixed_ref)
        for s in range(slots):
            slot_ref[pl.ds(place(live, s, i), 1)] = jnp.zeros((1, slot_ref.shape[1]), F32)

    @pl.when(live[i] != 0)
    def _():
        pad_ref[:tokens] = x_ref[0, 0].astype(F32)
        normed = (n1_ref[0].astype(F32) * vec_ref[0:1] + vec_ref[1:2]).astype(BF16)
        for part in range(3):
            cut = slice(part * features, (part + 1) * features)
            weights = one_ref[:, cut] if part < 2 else two_ref[:, :features]
            triple_ref[0, :, cut] = dot(normed, weights).astype(BF16)
        bias = jnp.where(lax.broadcasted_iota(jnp.int32, (1, keys), 1) < tokens, 0.0, LOW)
        for low in range(0, features, 128):
            q = triple_ref[0, :, low : low + 128]
            k = longer(triple_ref[0, :, features + low : features + low + 128], keys)
            v = longer(triple_ref[0, :, 2 * features + low : 2 * features + low + 128], keys)
            scores = dot(by_head(q, HEAD_DIM**-0.5), k, 1, 1) + bias
            powers = jnp.exp(scores - jnp.max(scores, axis=1, keepdims=True))
            total = dot(powers.astype(BF16), v) * (1.0 / jnp.sum(powers, axis=1, keepdims=True))
            mixed_ref[0, :, low : low + 128] = own_columns(total).astype(BF16)
        hidden = pad_ref[...] + dot(mixed_ref[0], two_ref[:, features : 2 * features])
        hidden_ref[0] = hidden
        n2, mean, root = standardized(hidden)
        normed_two = (n2 * vec_ref[2:3] + vec_ref[3:4]).astype(BF16)
        logits = dot(normed_two, two_ref[:, 2 * features :])
        dispatch, combine = routed(logits, tokens, slots)
        for part, value in enumerate((dispatch, combine, mean, root)):
            kept_ref[0, :, part * 128 : (part + 1) * 128] = jnp.broadcast_to(value, (rows, 128))
        slot_in = dot(dispatch.astype(BF16), normed_two, 0, 0)
        grad_slot = dot(combine.astype(BF16), cot_ref[0], 0, 0)
        for s in range(slots):
            slot_ref[pl.ds(place(live, s, i), 1), :features] = slot_in[s : s + 1]
            slot_ref[pl.ds(place(live, s, i), 1), features:] = grad_slot[s : s + 1]


def expert_kernel(pieces, images, *refs):
    rows_in, (up, up_other, down, down_other) = refs[:pieces], refs[pieces : pieces + 4]
    rows_out, (active_ref, slope_ref) = refs[pieces + 4 : 2 * pieces + 4], refs[2 * pieces + 4 :]
    per, features = up.shape[:2]
    both = jnp.concatenate([r[...] for r in rows_in], axis=0)
    rows, grads = both[:, :features], both[:, features:]
    index = lax.broadcasted_iota(jnp.int32, (rows.shape[0], 1), 0)
    total = total_back = 0.0
    for part, (up_ref, down_ref) in enumerate(((up, down), (up_other, down_other))):
        for j in range(per):
            mine = (index // images) % per == j
            pre = dot(rows, up_ref[j])
            phi = 0.5 * (1.0 + lax.erf(pre * (0.5**0.5)))
            density = jnp.exp(pre * pre * -0.5) * (0.5 / jnp.pi) ** 0.5
            active = jnp.where(mine, pre * phi, 0.0).astype(BF16)
            grad = dot(grads, down_ref[j], 1, 1)
            grad = jnp.where(mine, grad * (phi + pre * density), 0.0).astype(BF16)
            active_ref[part, j] = active
            slope_ref[part, j] = grad
            total = total + dot(active, down_ref[j])
            total_back = total_back + dot(grad, up_ref[j], 1, 1)
    size = rows_in[0].shape[0]
    for k, ref in enumerate(rows_out):
        ref[:, :features] = total[k * size : (k + 1) * size].astype(BF16)
        ref[:, features:] = total_back[k * size : (k + 1) * size].astype(BF16)


def expert_grad_kernel(pieces, *refs):
    rows_in, (active_ref, slope_ref) = refs[:pieces], refs[pieces : pieces + 2]
    outs = refs[pieces + 2 :]
    features = outs[0].shape[1]
    both = jnp.concatenate([r[...] for r in rows_in], axis=0)
    rows, grads = both[:, :features].T, both[:, features:]
    for part in range(2):
        up_ref, down_ref = outs[2 * part : 2 * part + 2]
        for j in range(up_ref.shape[0]):
            up_ref[j] = dot(rows, slope_ref[part, j]).astype(up_ref.dtype)
            down_ref[j] = dot(active_ref[part, j], grads, 0, 0).astype(down_ref.dtype)


def backward_kernel(
    tokens, slots, place, live, cot_ref, triple_ref, hidden_ref, kept_ref, home_ref, two_ref, phit_ref, vec_ref,
    out_ref, branch_ref, grad_ref, total_ref, small_ref, gm_ref,
):
    i = pl.program_id(0)
    rows, features = hidden_ref.shape[1:]
    keys = gm_ref.shape[0]

    @pl.when(i == 0)
    def _():
        gm_ref[...] = jnp.zeros_like(gm_ref)
        total_ref[...] = jnp.zeros_like(total_ref)
        small_ref[...] = jnp.zeros_like(small_ref)

    @pl.when(live[i] == 0)
    def _():
        out_ref[...] = jnp.zeros_like(out_ref)
        branch_ref[...] = jnp.zeros_like(branch_ref)
        grad_ref[...] = jnp.zeros_like(grad_ref)

    @pl.when(live[i] != 0)
    def _():
        hidden = hidden_ref[0]
        over_tokens, over_slots = kept_ref[0, :, :slots], kept_ref[0, :, 128 : 128 + slots]
        mean, root = (jnp.concatenate([kept_ref[0, :, low : low + 128]] * (features // 128), axis=1) for low in (256, 384))
        n2 = (hidden - mean) * root
        gain = vec_ref[2:3]
        normed_two = (n2 * gain + vec_ref[3:4]).astype(BF16)
        dispatch, combine = over_tokens.astype(BF16), over_slots.astype(BF16)
        home = jnp.concatenate([home_ref[pl.ds(place(live, s, i), 1)] for s in range(slots)], axis=0).astype(BF16)
        slot_out, grad_in = home[:, :features], home[:, features:]
        cot = cot_ref[0].astype(F32)
        result = hidden + dot(combine, slot_out)
        out_ref[0] = result[:tokens].astype(BF16)
        grad_combine = dot(cot_ref[0], slot_out, 1, 1)
        grad_dispatch = dot(normed_two, grad_in, 1, 1)
        grad_logits = over_tokens * (grad_dispatch - jnp.sum(grad_dispatch * over_tokens, axis=0, keepdims=True))
        grad_logits += over_slots * (grad_combine - jnp.sum(grad_combine * over_slots, axis=1, keepdims=True))
        grad_logits = grad_logits.astype(BF16)
        grad_two = dot(dispatch, grad_in) + dot(grad_logits, phit_ref[:slots])
        small_ref[:slots] += dot(grad_logits, normed_two, 0, 0)
        small_ref[slots : slots + 1] += jnp.sum(grad_two * n2, axis=0, keepdims=True)
        small_ref[slots + 1 : slots + 2] += jnp.sum(grad_two, axis=0, keepdims=True)
        u = grad_two * gain
        inner = u - jnp.sum(u, axis=-1, keepdims=True) * (1.0 / features)
        inner = inner - n2 * (jnp.sum(u * n2, axis=-1, keepdims=True) * (1.0 / features))
        branch = (cot + root * inner).astype(BF16)
        branch_ref[0] = branch
        gm_ref[:rows] = dot(branch, two_ref[:, features : 2 * features], 1, 1).astype(BF16)
        valid = lax.broadcasted_iota(jnp.int32, (rows, 1), 0) < tokens
        for low in range(0, features, 256):
            q = longer(triple_ref[0, :, low : low + 256], keys)
            k = triple_ref[0, :, features + low : features + low + 256]
            v = triple_ref[0, :, 2 * features + low : 2 * features + low + 256]
            gm = gm_ref[:, low : low + 256]
            scores_all = dot(by_head(k, HEAD_DIM**-0.5), q, 1, 1)
            grad_all = dot(by_head(v, 1.0), gm, 1, 1)
            for pair in range(2):
                attention, grad_scores = [], []
                for head in (2 * pair, 2 * pair + 1):
                    cut = slice(head * rows, (head + 1) * rows)
                    scores = jnp.where(valid, scores_all[cut], LOW)
                    powers = jnp.exp(scores - jnp.max(scores, axis=0, keepdims=True))
                    inverse = 1.0 / jnp.sum(powers, axis=0, keepdims=True)
                    mean = jnp.sum(grad_all[cut] * powers, axis=0, keepdims=True) * inverse
                    powers = powers * inverse
                    attention.append(powers.astype(BF16))
                    grad_scores.append((powers * (grad_all[cut] - mean)).astype(BF16))
                own = slice(pair * 128, (pair + 1) * 128)
                grads = (
                    own_columns(dot(jnp.concatenate([g.T for g in grad_scores], axis=0), k[:, own]))[:rows] * HEAD_DIM**-0.5,
                    own_columns(dot(jnp.concatenate(grad_scores, axis=0), q[:, own])) * HEAD_DIM**-0.5,
                    own_columns(dot(jnp.concatenate(attention, axis=0), gm[:, own])),
                )
                for part, grad in enumerate(grads):
                    cut = slice(part * features + low + pair * 128, part * features + low + (pair + 1) * 128)
                    grad_ref[0, :, cut] = grad.astype(BF16)
                    total_ref[0:1, cut] += jnp.sum(grad, axis=0, keepdims=True)


def input_kernel(tokens, triple_ref, n1_ref, root_ref, branch_ref, one_ref, two_ref, vec_ref, *refs):
    out_ref = refs[-1]
    count, rows, features = branch_ref.shape
    flat = lambda a: a.reshape(count * rows, a.shape[-1])
    triple, n1, root = flat(triple_ref[...]), flat(n1_ref[...]).astype(F32), flat(root_ref[...])[:, :1]
    v = dot(triple[:, : 2 * features], one_ref[...], 1, 1) + dot(triple[:, 2 * features :], two_ref[...], 1, 1)
    v = v * vec_ref[0:1]
    inner = v - jnp.sum(v, axis=-1, keepdims=True) * (1.0 / features)
    inner = inner - n1 * (jnp.sum(v * n1, axis=-1, keepdims=True) * (1.0 / features))
    grad = flat(branch_ref[...]).astype(F32) + root * inner
    for k in range(count):
        out_ref[k] = grad[k * rows : k * rows + tokens].astype(BF16)


def weight_grad_kernel(slots, devices, core, left_ref, left_out_hbm, right_ref, right_out_ref, one_ref, two_ref, total_ref, small_ref, columns_ref, *refs):
    *outs, norm_ref, left_out_ref, arrived = refs
    i, features, tile = pl.program_id(0), left_ref.shape[0], outs[0].shape[1]
    third = features // tile

    def store(value):
        if len(outs) == 1:
            outs[0][...] = value.astype(BF16)
            return
        value = value.reshape(devices // 2, 2, -1, tile)
        for k, ref in enumerate(outs):
            half = jnp.where(core[0] == k, value[:, 0], value[:, 1])
            ref[...] = half.reshape(-1, tile).astype(BF16)

    later = pltpu.make_async_copy(left_out_hbm, left_out_ref, arrived)

    @pl.when(i == 0)
    def _():
        later.start()
        norm_ref[...] = jnp.zeros_like(norm_ref)

    @pl.when(i == 3 * third)
    def _():
        later.wait()

    def tokens(ref):
        return ref[...].reshape(-1, tile)

    def wide_part(w_ref):
        product = dot(left_ref[...], tokens(right_ref))
        total = total_ref[0:1]
        store(product * columns_ref[:, 0:1] + columns_ref[:, 1:2] * total)
        for low in range(0, tile, 128):
            cut = slice(low, low + 128)
            weights = w_ref[:, cut].astype(F32)
            norm_ref[:, :128] += weights * product[:, cut]
            norm_ref[:, 128:] += weights * total[:, cut]

    @pl.when(i < 2 * third)
    def _():
        wide_part(one_ref)

    @pl.when((i >= 2 * third) & (i < 3 * third))
    def _():
        wide_part(two_ref)

    @pl.when((i >= 3 * third) & (i < 4 * third))
    def _():
        store(dot(left_out_ref[...], tokens(right_out_ref)))

    @pl.when(i == 4 * third)
    def _():
        lane = lax.broadcasted_iota(jnp.int32, (features, 128), 1)
        gain = jnp.sum(norm_ref[:, :128], axis=1, keepdims=True)
        bias = jnp.sum(norm_ref[:, 128:], axis=1, keepdims=True)
        narrow = jnp.where(lane == slots + 2, gain, jnp.where(lane == slots + 3, bias, small_ref[...]))
        store(jnp.concatenate([narrow] * (tile // 128), axis=1))


def own(*shape, low=0):
    return pl.BlockSpec((1,) + shape, lambda i, live: (i + low,) + (0,) * len(shape))


def fixed(*shape):
    return pl.BlockSpec(shape, lambda i, *live: (0,) * len(shape), pipeline_mode=pl.Buffered(1))


def shaped(*shape, dtype=BF16):
    return jax.ShapeDtypeStruct(shape, dtype)


def params(mib, axes=1):
    return pltpu.CompilerParams(vmem_limit_bytes=mib * 1024 * 1024, dimension_semantics=("arbitrary",) * axes)


def by_image(kernel, images, in_specs, out_specs, out_shape, scratch, flops, mib):
    return pl.pallas_call(
        kernel,
        grid_spec=pltpu.PrefetchScalarGridSpec(
            num_scalar_prefetch=1, grid=(images,), in_specs=in_specs, out_specs=out_specs, scratch_shapes=scratch
        ),
        out_shape=out_shape,
        compiler_params=params(mib),
        cost_estimate=pl.CostEstimate(flops=flops, bytes_accessed=flops // 1000, transcendentals=0),
    )


class Mixer:
    def __init__(self, grid, inputs, slots, live, expert):
        self.inputs, self.slots = inputs, slots
        self.live = jnp.concatenate([live, expert[None]])
        self.owners, self.per = grid.m, slots // grid.m
        self.batches, self.capacity, self.tokens, self.features = inputs.shape
        self.images = self.batches * self.capacity
        self.rows, self.keys = padded(self.tokens, 16), padded(self.tokens, 128)
        self.pad = pltpu.VMEM((self.rows, self.features), F32)
        self.flops = self.rows * self.features * self.features * 8

    def place(self, live, s, i):
        owner = lax.rem(s // self.per + self.owners - live[self.images], self.owners)
        return (owner * self.per + s % self.per) * self.images + i

    def image(self, low):
        return pl.BlockSpec((1, 1, self.tokens, self.features), lambda i, live: ((i + low) // self.capacity, (i + low) % self.capacity, 0, 0))

    def made(self, low=0):
        return pl.BlockSpec((1, self.tokens, self.features), lambda i, live: (i + low, 0, 0))

    def padded_cotangent(self, cotangent):
        n, c, r, f = self.images, self.capacity, self.rows, self.features
        return pl.pallas_call(
            partial(pad_kernel, self.tokens),
            grid=(self.batches,),
            in_specs=[pl.BlockSpec((1, c, self.tokens, f), lambda i: (i, 0, 0, 0))],
            out_specs=pl.BlockSpec((c, r, f), lambda i: (i, 0, 0)),
            out_shape=shaped(n, r, f),
            compiler_params=params(LIMIT),
        )(cotangent)

    def standardize(self):
        n, c, r, f = self.images, self.capacity, self.rows, self.features
        group = lambda *shape: pl.BlockSpec((c,) + shape, lambda i: (i,) + (0,) * len(shape))
        return pl.pallas_call(
            partial(standardize_kernel, self.tokens),
            grid=(self.batches,),
            in_specs=[pl.BlockSpec((1, c, self.tokens, f), lambda i: (i, 0, 0, 0))],
            out_specs=[group(r, f), group(r, 128)],
            out_shape=[shaped(n, r, f), shaped(n, r, 128, dtype=F32)],
            scratch_shapes=[pltpu.VMEM((c, r, f), F32)],
            compiler_params=params(LIMIT),
        )(self.inputs)

    def forward(self, n1, cot, one, two, vec):
        n, r, f = self.images, self.rows, self.features
        return by_image(
            partial(forward_kernel, self.tokens, self.slots, self.place), n,
            [self.image(0), own(r, f), own(r, f), fixed(*one.shape), fixed(*two.shape), fixed(*vec.shape)],
            [own(r, 3 * f), own(r, f), own(r, f), own(r, 512), fixed(self.slots * n, 2 * f)],
            [shaped(n, r, 3 * f), shaped(n, r, f), shaped(n, r, f, dtype=F32), shaped(n, r, 512, dtype=F32), shaped(self.slots * n, 2 * f, dtype=F32)],
            [self.pad], 3 * n * self.flops, LIMIT,
        )(self.live, self.inputs, n1, cot, one, two, vec)

    def backward(self, cot, triple, hidden, logits, home, two, phit, vec):
        n, r, f = self.images, self.rows, self.features
        small = padded(self.slots + 2, 8)
        return by_image(
            partial(backward_kernel, self.tokens, self.slots, self.place), n,
            [own(r, f), own(r, 3 * f), own(r, f), own(r, 512), fixed(self.slots * n, 2 * f), fixed(*two.shape), fixed(*phit.shape), fixed(*vec.shape)],
            [self.made(), own(r, f), own(r, 3 * f), fixed(8, 3 * f), fixed(small, f)],
            [shaped(n, self.tokens, f), shaped(n, r, f), shaped(n, r, 3 * f), shaped(8, 3 * f, dtype=F32), shaped(small, f, dtype=F32)],
            [pltpu.VMEM((self.keys, f), BF16)], 3 * n * self.flops, LIMIT,
        )(self.live, cot, triple, hidden, logits, home, two, phit, vec)

    def input_back(self, low, high, triple, n1, root, branch, one, two, vec, into, step):
        r, f = self.rows, self.features
        some = lambda *shape: pl.BlockSpec((step,) + shape, lambda i: (i + low // step,) + (0,) * len(shape))
        return pl.pallas_call(
            partial(input_kernel, self.tokens),
            grid=((high - low) // step,),
            in_specs=[some(r, 3 * f), some(r, f), some(r, 128), some(r, f), fixed(*one.shape), fixed(f, f), fixed(*vec.shape)]
            + [pl.BlockSpec(memory_space=pl.ANY)] * (into is not None),
            out_specs=some(self.tokens, f),
            out_shape=shaped(self.images, self.tokens, f),
            input_output_aliases={} if into is None else {7: 0},
            compiler_params=params(LIMIT),
        )(triple, n1, root, branch, one, two, vec, *([] if into is None else [into]))

    def turned(self, array):
        return array.reshape(-1, array.shape[-1]).T

    def weight_grads(self, core, devices, left, left_out, right, right_out, one, two, total, small, columns, tile=256):
        f, third = self.features, self.features // tile
        apart = f // devices % 8 == 0
        rows = [f // 2, f // 2] if apart else [f]

        def at(array, first, count):
            lead = array.shape[:-1]
            return pl.BlockSpec(lead + (tile,), lambda i, core: (0,) * len(lead) + (jnp.clip(i - first, 0, count - 1),))

        return pl.pallas_call(
            partial(weight_grad_kernel, self.slots, devices),
            grid_spec=pltpu.PrefetchScalarGridSpec(
                num_scalar_prefetch=1,
                grid=(4 * third + 1,),
                in_specs=[fixed(*left.shape), pl.BlockSpec(memory_space=pl.ANY), at(right, 0, 3 * third), at(right_out, 3 * third, third),
                          at(one, 0, 2 * third), at(two, 2 * third, third), at(total, 0, 3 * third), fixed(*small.shape), fixed(*columns.shape)],
                out_specs=[pl.BlockSpec((r, tile), lambda i, core: (0, i)) for r in rows],
                scratch_shapes=[pltpu.VMEM((f, 256), F32), pltpu.VMEM(left_out.shape, BF16), pltpu.SemaphoreType.DMA],
            ),
            out_shape=[shaped(r, 4 * f + 128) for r in rows],
            compiler_params=params(LIMIT),
        )(core[None], left, left_out, right, right_out, one, two, total, small, columns)


def expert_forward(pieces, weights, images):
    per, _, hidden = weights[0].shape
    size, count = pieces[0].shape[0], len(pieces)
    kept = shaped(2, per, size * count, hidden)
    made = pl.pallas_call(
        partial(expert_kernel, count, images),
        out_shape=[shaped(*p.shape) for p in pieces] + [kept, kept],
        compiler_params=params(SMALL, 0),
    )(*pieces, *weights)
    return made[:count], made[count:]


def expert_grads(pieces, kept, up, down):
    return pl.pallas_call(
        partial(expert_grad_kernel, len(pieces)),
        out_shape=[shaped(*up.shape, dtype=F32), shaped(*down.shape, dtype=F32), shaped(*up.shape), shaped(*down.shape)],
        compiler_params=params(SMALL, 0),
    )(*pieces, *kept)


def wide(a, width=128):
    return jnp.pad(a, ((0, 0), (0, width - a.shape[1])))


def body(grid, inputs, counts, ln1_gain, ln1_bias, w_qkv, w_out, ln2_gain, ln2_bias, phi, w_up, w_down, cotangent):
    me = grid.coords()
    batches, capacity, tokens, features = inputs.shape
    images = batches * capacity
    slots = phi.shape[1]
    per = slots // grid.m
    token = (jnp.arange(capacity)[None, :] < counts).astype(jnp.int32).reshape(-1)
    mixer = Mixer(grid, inputs, slots, token, me["e"])
    vectors = jnp.stack([ln1_gain, ln1_bias, ln2_gain, ln2_bias])
    vectors = dot(vectors, jnp.eye(4, dtype=BF16), 0, 0).astype(BF16)
    packed = jnp.concatenate([w_qkv, w_out, wide(jnp.concatenate([phi, vectors], axis=1))], axis=1)
    flow = Flow(gather_steps(grid, me, packed, 2 * features))
    cot, token = beside([flow], token, lambda token: mixer.padded_cotangent(cotangent))
    _, token = beside([flow], token)
    (n1, root), token = beside([flow], token, lambda token: mixer.standardize())
    other = Flow(neighbour_steps(grid, lax.optimization_barrier(([w_up, w_down], token))[0]))
    _, token = beside([flow], token)
    one, two = flow.value
    columns = two[:, 2 * features : 2 * features + padded(slots + 4, 16)].astype(F32)
    turned = columns.T
    vec = jnp.pad(turned[slots : slots + 4], ((0, 4), (0, 0)))

    made, token = beside([], token, lambda token: mixer.forward(n1, cot, one, two, vec))
    triple, mixed, hidden, logits, slot = made
    flow = Flow(out_steps(grid, slot.astype(BF16)))
    _, token = beside([flow, other], token)
    lefts, token = beside([flow], token, lambda token: (mixer.turned(n1), mixer.turned(mixed)))
    pieces = flow.value
    back, kept = expert_forward(pieces, [w_up, other.value[0], w_down, other.value[1]], images)
    flow = Flow(home_steps(grid, back))
    made, token = beside([flow], token, lambda token: expert_grads(pieces, kept, w_up, w_down))
    grad_up, grad_down, *others = made
    _, token = beside([flow], token)
    split = (per + 1) // 2
    other = Flow(neighbour_steps(grid, [others[0], others[1][:split]]))
    made, token = beside(
        [other], token, lambda token: mixer.backward(cot, triple, hidden, logits, flow.value.astype(F32), two, turned.astype(BF16), vec)
    )
    outs, branch, grad_triple, total, small = made
    rest = Flow(neighbour_steps(grid, lax.optimization_barrier((others[1][split:], token))[:1]))
    packed, token = beside([rest], token, lambda token: mixer.weight_grads(
        me["c"], grid.n * grid.m, *lefts, grad_triple, branch, one, two, total, wide(small.T), columns[:, slots : slots + 2]
    ))
    flow = Flow(reduce_steps(grid, me, packed, padded(packed[0].shape[1] // 2, 128)))
    grad_in, low, flows = None, 0, [flow]
    for count in SHARES:
        (grad_in, outs), token = beside(
            flows,
            token,
            lambda token: (mixer.input_back(
                low * images // 12, (low + count) * images // 12, grad_triple, n1, root, branch, one, two, vec, grad_in, max(images // 6, 1)
            ), outs),
        )
        low += count
    while not flow.done:
        _, token = beside([flow], token)
    sums = flow.value
    grad_up = grad_up + other.value[0].astype(F32)
    grad_down = grad_down + jnp.concatenate([other.value[1], rest.value[0]], axis=0).astype(F32)
    small = sums[:, 4 * features :]
    return (
        outs.reshape(inputs.shape),
        grad_in.reshape(inputs.shape),
        small[:, slots + 2],
        small[:, slots + 3],
        sums[:, : 3 * features],
        sums[:, 3 * features : 4 * features],
        small[:, slots],
        small[:, slots + 1],
        small[:, :slots],
        grad_up,
        grad_down,
    )


def solution(mesh):
    rows = P(BOTH, None)
    row = P(BOTH)
    image = P(None, BOTH, None, None)
    up, down = P("expert", None, "dp"), P("expert", "dp", None)
    grid = Grid(mesh.shape["dp"], mesh.shape["expert"])
    return jax.shard_map(
        partial(body, grid),
        mesh=mesh,
        in_specs=(image, P(None, BOTH), row, row, rows, rows, row, row, rows, up, down, image),
        out_specs=(image, image, row, row, rows, rows, row, row, rows, up, down),
        check_vma=False,
    )
```
